256 devices in a mesh: band: 32 (over z, x_hi, core), head: 8 (over y, x_lo).
Axes of the slice: x: 4 (x_hi: 2, x_lo: 2; x = x_hi * 2 + x_lo), y: 4, z: 8, core: 2. Of those that a mesh axis runs over, the one named last changes fastest.
Arguments:
- grid_in: bfloat16 [110, 524288], P(None, ('band', 'head')), may hold values from -6 to 6
- enc_node: int32 [524288], P(('band', 'head')), may hold values from 0 to 40959, as said below
- dec_node: int32 [524288], P(('band', 'head')), may hold values from 0 to 40959, as said below
- win_offsets: int32 [2, 40960], P(None, 'band'), may hold values from 1 to 640, as said below
- w_in: bfloat16 [110, 1024], replicated, may hold values from -0.5 to 0.5
- b_in: float32 [1024], replicated, may hold values from -4 to 4
- w_qkv: bfloat16 [1024, 3072], replicated, may hold values from -8 to 8
- w_out: bfloat16 [1024, 1024], replicated, may hold values from -0.75 to 0.75
- norm_gain: float32 [1024], replicated, may hold values from 0.1 to 1.9
- w_dec: bfloat16 [1024, 110], replicated, may hold values from -0.1875 to 0.1875
- cotangent: bfloat16 [110, 524288], P(None, ('band', 'head')), may hold values from -6 to 6
Outputs:
- prediction: bfloat16 [110, 524288], P(None, ('band', 'head'))
- grad_dec: float32 [1024, 110], replicated
The draws below stay inside these ranges and needn't reach their ends.
Inputs may be any that keep to these rules, and one draw needn't show every extreme that they name: `enc_node`: grid points and nodes are numbered by latitude; the node of the encoder edge of a grid point held by index j of band+head is held by index j - 1, j or j + 1 of band+head. `dec_node`: the node of the decoder edge of a grid point held by index j of band+head is held by index j - 1, j or j + 1 of band+head. `win_offsets`: row 0 is the reach towards lower node numbers, row 1 towards higher ones.
All inputs are finite; a program needn't handle non-finite values.
Results may differ from the reference program's by a relative error of at most 0.012.
Values may be sent and summed in bfloat16 or wider, within the bound.
No kernel may reach another device: no remote copies, remote signals or barrier semaphores. Data moves between devices by JAX's collectives and lax.ppermute only.
A program may use at most 128 MiB of HBM per device.

```python
import jax
import jax.numpy as jnp
from jax import lax

D = 1024
HEADS = 16
C = 110
HDIM = 64
NODE_DEV = 160
GRID_DEV = 2048
NODES = 40960
GRID = 524288
WIN = 640
N_BAND = 32
N_HEAD = 8


def latitude_edges(key):
    grid_rows = jnp.arange(GRID, dtype=jnp.int32)
    base_node = grid_rows // GRID_DEV * NODE_DEV + grid_rows % GRID_DEV * NODE_DEV // GRID_DEV
    jitter = jax.random.randint(key, (GRID,), -NODE_DEV, NODE_DEV + 1, dtype=jnp.int32)
    target = jnp.clip(base_node + jitter, 0, NODES - 1)
    target = target.at[0].set(0)
    return target.at[GRID - 1].set(NODES - 1)


def draw_enc_node(key, part):
    key = jax.random.fold_in(key, 3)
    return latitude_edges(key)


def draw_dec_node(key, part):
    key = jax.random.fold_in(key, 5)
    return latitude_edges(key)


def draw_win_offsets(key, part):
    key = jax.random.fold_in(key, 11)
    reach = jax.random.randint(key, (2, NODES), 1, WIN + 1, dtype=jnp.int32)
    reach = reach.at[:, 0].set(WIN)
    return reach.at[:, 1].set(1)


def draw_w_qkv(key, part):
    key = jax.random.fold_in(key, 7)
    first = jax.random.fold_in(key, 0)
    third = jax.random.fold_in(key, 2)
    fourth = jax.random.fold_in(key, 3)
    scale = D ** (-0.5)
    queries = jax.random.normal(first, (D, D), jnp.float32) * scale
    key_part = jax.random.normal(third, (D, D), jnp.float32) * scale
    values = jax.random.normal(fourth, (D, D), jnp.float32) * scale
    return jnp.clip(jnp.concatenate([queries, key_part, values], axis=1), -8.0, 8.0).astype(jnp.bfloat16)


def steps_of(key, shape, cuts, low, high):
    loudness = 1.0
    for axis_at, shards_of in cuts:
        draws = jax.random.uniform(jax.random.fold_in(jax.random.fold_in(key, 6), axis_at), (shards_of,), jnp.float32, low / len(cuts), high / len(cuts))
        loudness = loudness * jnp.repeat(jnp.exp(draws), shape[axis_at] // shards_of).reshape((-1,) + (1,) * (len(shape) - 1 - axis_at))
    return loudness


def gaussian(rng, extent, width, most, shards=(), held_as=jnp.bfloat16):
    values = width * jax.random.normal(rng, extent, jnp.float32)
    if shards:
        values = values * steps_of(rng, extent, shards, -0.22, 0.18)
    return jnp.clip(values, -most, most).astype(held_as)


def setup_inputs(seed: int = 0) -> dict:
    splits = jax.random.split(jax.random.key(seed), 12)
    return {
        "grid_in": gaussian(splits[0], (C, GRID), 1.0, 6.0, ((1, 256),)),
        "enc_node": draw_enc_node(jax.random.fold_in(splits[11], 71), 0),
        "dec_node": draw_dec_node(jax.random.fold_in(splits[11], 71), 0),
        "win_offsets": draw_win_offsets(jax.random.fold_in(splits[11], 71), 0),
        "w_in": gaussian(splits[4], (C, D), C ** -0.5, 0.5),
        "b_in": gaussian(splits[5], (D,), 1.0, 4.0, (), jnp.float32),
        "w_qkv": draw_w_qkv(jax.random.fold_in(splits[11], 71), 0),
        "w_out": gaussian(splits[7], (D, D), (D // 16) ** -0.5, 0.75),
        "norm_gain": jnp.clip(1.0 + 0.18 * jax.random.normal(splits[8], (D,), jnp.float32), 0.1, 1.9),
        "w_dec": gaussian(splits[9], (D, C), D ** -0.5, 0.1875),
        "cotangent": gaussian(splits[10], (C, GRID), 1.0, 6.0, ((1, 256),)),
    }


def reference(grid_in, enc_node, dec_node, win_offsets, w_in, b_in, w_qkv, w_out, norm_gain, w_dec, cotangent):
    node_count = NODE_DEV * N_BAND * N_HEAD
    band_rows = NODE_DEV * N_HEAD
    group_rows = GRID_DEV * N_HEAD
    blocks = jnp.arange(N_BAND, dtype=jnp.int32)

    def encode(running, block_index):
        columns = lax.dynamic_slice_in_dim(grid_in, block_index * group_rows, group_rows, 1)
        targets = lax.dynamic_slice_in_dim(enc_node, block_index * group_rows, group_rows, 0)
        preact = lax.dot_general(columns, w_in, (((0,), (0,)), ((), ())), preferred_element_type=jnp.float32) + b_in
        return (running.at[targets].add(jax.nn.silu(preact)), None)
    encoded, _ = lax.scan(encode, jnp.zeros((node_count, D), jnp.float32), blocks)
    centred = encoded - lax.optimization_barrier(jnp.mean(encoded, axis=1, keepdims=True))
    spread_sq = lax.optimization_barrier(jnp.mean(centred * centred, axis=1, keepdims=True))
    normed = (centred * lax.rsqrt(spread_sq + 1e-05) * norm_gain).astype(jnp.bfloat16)
    packed = jnp.dot(normed, w_qkv, preferred_element_type=jnp.float32).astype(jnp.bfloat16)
    keys_padded = jnp.pad(packed[:, D:], ((WIN, WIN), (0, 0)))
    key_count = band_rows + 2 * WIN

    def attend(block_index):
        first_node = block_index * band_rows
        queries = lax.dynamic_slice_in_dim(packed[:, :D], first_node, band_rows, 0).astype(jnp.float32).reshape(band_rows, HEADS, HDIM)
        window = lax.dynamic_slice_in_dim(keys_padded, first_node, key_count, 0).astype(jnp.float32)
        key_block = window[:, :D].reshape(key_count, HEADS, HDIM)
        values = window[:, D:].reshape(key_count, HEADS, HDIM)
        offsets = lax.dynamic_slice_in_dim(win_offsets, first_node, band_rows, 1)
        offset_grid = jnp.arange(key_count, dtype=jnp.int32)[None, :] - WIN - jnp.arange(band_rows, dtype=jnp.int32)[:, None]
        global_key = first_node - WIN + jnp.arange(key_count, dtype=jnp.int32)
        allowed = (offset_grid >= -offsets[0][:, None]) & (offset_grid <= offsets[1][:, None])
        allowed = allowed & (global_key >= 0)[None, :] & (global_key < node_count)[None, :]
        scores = jnp.einsum('qhd,khd->hqk', queries, key_block) * HDIM ** (-0.5)
        scores = jnp.where(allowed[None], scores, -jnp.inf)
        largest = lax.optimization_barrier(jnp.max(scores, axis=2, keepdims=True))
        weights = jnp.exp(scores - largest)
        weights = (weights / lax.optimization_barrier(jnp.sum(weights, axis=2, keepdims=True))).astype(jnp.bfloat16)
        result = jnp.einsum('hqk,khd->qhd', weights.astype(jnp.float32), values)
        return result.reshape(band_rows, D).astype(jnp.bfloat16)
    attended = lax.map(attend, blocks).reshape(node_count, D)
    state = (encoded + jnp.dot(attended, w_out, preferred_element_type=jnp.float32)).astype(jnp.bfloat16)

    def decode(running, block_index):
        columns = lax.dynamic_slice_in_dim(grid_in, block_index * group_rows, group_rows, 1)
        upstream = lax.dynamic_slice_in_dim(cotangent, block_index * group_rows, group_rows, 1)
        targets = lax.dynamic_slice_in_dim(dec_node, block_index * group_rows, group_rows, 0)
        node_rows = state[targets]
        decoded = lax.dot_general(w_dec, node_rows, (((0,), (1,)), ((), ())), preferred_element_type=jnp.float32)
        prediction = (columns.astype(jnp.float32) + decoded).astype(jnp.bfloat16)
        grad_term = lax.dot_general(node_rows, upstream, (((0,), (1,)), ((), ())), preferred_element_type=jnp.float32)
        return (running + grad_term, prediction)
    grad_dec, pieces = lax.scan(decode, jnp.zeros((D, C), jnp.float32), blocks)
    prediction = jnp.transpose(pieces, (1, 0, 2)).reshape(C, GRID)
    return (prediction, grad_dec)
```

```python
import functools

import jax
import jax.numpy as jnp
from jax import lax
from jax.experimental import pallas as pl
from jax.experimental.pallas import tpu as pltpu
from jax.sharding import PartitionSpec as P

HDIM = 64
NODE_DEV = 160
BOTH = ("band", "head")
LANES = 128
BF = jnp.bfloat16
F32 = jnp.float32
LOG2E = 1.4426950408889634
NEG = -1e30


def params(mib=40):
    return pltpu.CompilerParams(vmem_limit_bytes=mib * 1024 * 1024)


def dot(a, b, ca, cb):
    return lax.dot_general(a, b, (((ca,), (cb,)), ((), ())), preferred_element_type=F32)


def my_index():
    return lax.axis_index("band") * lax.axis_size("head") + lax.axis_index("head")


def encode_kernel(grid_ref, enc_ref, w_ref, b_ref, cot_ref, dec_ref, own_ref, low_ref, high_ref,
                  rows_ref, w_pad, cot_pad, pick_ref):
    channels, points = grid_ref.shape
    model = w_ref.shape[1]
    nodes = NODE_DEV
    base = (my_index() - 1) * nodes
    padded = jnp.concatenate(
        [grid_ref[...].astype(F32), jnp.zeros((LANES - channels, points), F32)], axis=0
    )
    rows_ref[...] = padded.T.astype(BF)
    w_pad[...] = jnp.zeros_like(w_pad)
    w_pad[:channels, :] = (w_ref[...].astype(F32) * 0.5).astype(BF)
    node_id = lax.broadcasted_iota(jnp.int32, (3 * nodes, points), 0)
    pick_ref[...] = jnp.where(node_id == enc_ref[...] - base, 1.0, 0.0).astype(BF)
    width = 256
    for at in range(0, model, width):
        half = dot(rows_ref[...], w_pad[:, at : at + width], 1, 0) + b_ref[:, at : at + width] * 0.5
        message = (half + half * jnp.tanh(half)).astype(BF)
        spread = dot(pick_ref[...], message, 1, 0)
        low_ref[:, at : at + width] = spread[:nodes].astype(BF)
        own_ref[:, at : at + width] = spread[nodes : 2 * nodes]
        high_ref[:, at : at + width] = spread[2 * nodes :].astype(BF)
    cot_pad[...] = jnp.zeros_like(cot_pad)
    cot_pad[:channels, :] = cot_ref[...]
    pick_ref[...] = jnp.where(node_id == dec_ref[...] - base, 1.0, 0.0).astype(BF)
    spread = dot(pick_ref[...], cot_pad[...], 1, 1)
    low_ref[:, model:] = spread[:nodes].astype(BF)
    own_ref[:, model:] = spread[nodes : 2 * nodes]
    high_ref[:, model:] = spread[2 * nodes :].astype(BF)


def encode(grid_in, enc_row, w_in, b_row, cotangent, dec_row):
    channels, points = grid_in.shape
    model = w_in.shape[1]
    wide = model + LANES
    return pl.pallas_call(
        encode_kernel,
        out_shape=(
            jax.ShapeDtypeStruct((NODE_DEV, wide), F32),
            jax.ShapeDtypeStruct((NODE_DEV, wide), BF),
            jax.ShapeDtypeStruct((NODE_DEV, wide), BF),
        ),
        scratch_shapes=[
            pltpu.VMEM((points, LANES), BF),
            pltpu.VMEM((LANES, model), BF),
            pltpu.VMEM((LANES, points), BF),
            pltpu.VMEM((3 * NODE_DEV, points), BF),
        ],
        compiler_params=params(),
        name="encode",
    )(grid_in, enc_row, w_in, b_row, cotangent, dec_row)


def project_kernel(own_ref, from_low, from_high, gain_ref, wq_ref, wk_ref, wv_ref,
                   packed_ref, enc_ref, s_ref, normed_ref):
    model = gain_ref.shape[1]

    @pl.when(pl.program_id(0) == 0)
    def _():
        total = own_ref[...] + from_low[...].astype(F32) + from_high[...].astype(F32)
        enc = total[:, :model]
        s_ref[...] = total[:, model:].astype(BF)
        enc_ref[...] = enc.astype(BF)
        centred = enc - jnp.mean(enc, axis=1, keepdims=True)
        spread_sq = jnp.mean(centred * centred, axis=1, keepdims=True)
        normed_ref[...] = (centred * lax.rsqrt(spread_sq + 1e-05) * gain_ref[...]).astype(BF)

    normed = normed_ref[...]
    scale = HDIM ** (-0.5) * LOG2E
    packed_ref[0, :, :LANES] = (dot(normed, wq_ref[...], 1, 0) * scale).astype(BF)
    packed_ref[0, :, LANES : 2 * LANES] = dot(normed, wk_ref[...], 1, 0).astype(BF)
    packed_ref[0, :, 2 * LANES :] = dot(normed, wv_ref[...], 1, 0).astype(BF)


def project(own, from_low, from_high, gain_row, w_qkv):
    model = w_qkv.shape[0]
    groups = model // LANES
    whole = lambda shape: pl.BlockSpec(shape, lambda h: (0, 0))
    return pl.pallas_call(
        project_kernel,
        grid=(groups,),
        in_specs=[
            whole(own.shape),
            whole(own.shape),
            whole(own.shape),
            whole(gain_row.shape),
            pl.BlockSpec((model, LANES), lambda h: (0, h)),
            pl.BlockSpec((model, LANES), lambda h: (0, h + groups)),
            pl.BlockSpec((model, LANES), lambda h: (0, h + 2 * groups)),
        ],
        out_specs=(
            pl.BlockSpec((1, NODE_DEV, 3 * LANES), lambda h: (h, 0, 0)),
            whole((NODE_DEV, model)),
            whole((NODE_DEV, LANES)),
        ),
        out_shape=(
            jax.ShapeDtypeStruct((groups, NODE_DEV, 3 * LANES), BF),
            jax.ShapeDtypeStruct((NODE_DEV, model), BF),
            jax.ShapeDtypeStruct((NODE_DEV, LANES), BF),
        ),
        scratch_shapes=[pltpu.VMEM((NODE_DEV, model), BF)],
        compiler_params=params(),
        name="project",
    )(own, from_low, from_high, gain_row, w_qkv, w_qkv, w_qkv)


def side_kernel(head_ref, enc_ref, s_ref, w_dec_ref, w_out_ref, send_ref, node_ref, mix_ref, dec_pad):
    channels = w_dec_ref.shape[1]
    groups = send_ref.shape[0]
    dec_pad[...] = jnp.zeros_like(dec_pad)
    dec_pad[:, :channels] = w_dec_ref[...]
    enc = enc_ref[...]
    summed = s_ref[...]
    node_ref[...] = dot(enc, dec_pad[...], 1, 0)
    mix_ref[...] = dot(w_out_ref[...], dec_pad[...], 1, 0).astype(BF)
    grad = dot(summed, enc, 0, 0).T.astype(BF)
    for group in range(groups):
        send_ref[group, :NODE_DEV, :] = summed
        send_ref[group, NODE_DEV:, :] = grad[group * LANES : (group + 1) * LANES]


def side(enc, summed, w_dec, w_out):
    model = enc.shape[1]
    groups = model // LANES
    head = lax.axis_index("head").astype(jnp.int32)[None]
    whole = lambda shape: pl.BlockSpec(shape, lambda i, h: (0,) * len(shape))
    send_shape = (groups, NODE_DEV + LANES, LANES)
    return pl.pallas_call(
        side_kernel,
        grid_spec=pltpu.PrefetchScalarGridSpec(
            num_scalar_prefetch=1,
            grid=(1,),
            in_specs=[
                whole(enc.shape),
                whole(summed.shape),
                whole(w_dec.shape),
                pl.BlockSpec((LANES, model), lambda i, h: (h[0], 0)),
            ],
            out_specs=(whole(send_shape), whole((NODE_DEV, LANES)), whole((LANES, LANES))),
            scratch_shapes=[pltpu.VMEM((model, LANES), BF)],
        ),
        out_shape=(
            jax.ShapeDtypeStruct(send_shape, BF),
            jax.ShapeDtypeStruct((NODE_DEV, LANES), F32),
            jax.ShapeDtypeStruct((LANES, LANES), BF),
        ),
        compiler_params=params(),
        name="side",
    )(head, enc, summed, w_dec, w_out)


QB = 256
KC = 128


def attend_kernel(reach, qkv_ref, low_ref, high_ref, win_ref, extra_ref, mix_ref,
                  node_ref, grad_ref, k_ref, vt_ref, score_ref, prob_ref, out_ref):
    groups = extra_ref.shape[0]
    band_rows = qkv_ref.shape[0]
    first_node = lax.axis_index("band") * band_rows
    node_total = lax.axis_size("band") * band_rows
    keys = QB + 2 * reach
    chunks = keys // KC
    k_ref[:reach, :] = low_ref[:, :LANES]
    k_ref[reach : reach + band_rows, :] = qkv_ref[:, LANES : 2 * LANES]
    k_ref[reach + band_rows :, :] = high_ref[:, :LANES]
    ones = jnp.ones((16, band_rows + 2 * reach), BF)
    vt = jnp.concatenate(
        [low_ref[:, LANES:].astype(F32), qkv_ref[:, 2 * LANES :].astype(F32), high_ref[:, LANES:].astype(F32)],
        axis=0,
    ).T.astype(BF)
    for head in range(2):
        vt_ref[head, :HDIM, :] = vt[head * HDIM : (head + 1) * HDIM]
        vt_ref[head, HDIM:, :] = ones
    lane = lax.broadcasted_iota(jnp.int32, (QB, LANES), 1)
    zero = jnp.zeros((QB, LANES), BF)
    for block in range(band_rows // QB):
        start = block * QB
        queries = qkv_ref[start : start + QB, :LANES]
        both = jnp.concatenate(
            [jnp.where(lane < HDIM, queries, zero), jnp.where(lane >= HDIM, queries, zero)], axis=0
        )
        offsets = win_ref[:, start : start + QB]
        column = lax.broadcasted_iota(jnp.int32, (1, QB), 1) + reach
        bottom = jnp.maximum(column - offsets[0:1], reach - start - first_node)
        top = jnp.minimum(column + offsets[1:2], reach - start - first_node + node_total - 1)
        bottom = jnp.concatenate([bottom, bottom], axis=1)
        top = jnp.concatenate([top, top], axis=1)
        largest = jnp.full((8, 2 * QB), NEG, F32)
        for chunk in range(chunks):
            at = chunk * KC
            scores = dot(k_ref[start + at : start + at + KC, :], both, 1, 1)
            key = lax.broadcasted_iota(jnp.int32, (KC, 2 * QB), 0) + at
            if at + KC - 1 <= reach:
                scores = jnp.where(key >= bottom, scores, NEG)
            elif at >= reach + QB - 1:
                scores = jnp.where(key <= top, scores, NEG)
            else:
                scores = jnp.where((key >= bottom) & (key <= top), scores, NEG)
            score_ref[at : at + KC, :] = scores
            largest = jnp.maximum(largest, jnp.max(scores.reshape(KC // 8, 8, 2 * QB), axis=0))
        largest = jnp.max(largest, axis=0, keepdims=True)
        for chunk in range(chunks):
            at = chunk * KC
            prob_ref[at : at + KC, :] = jnp.exp2(score_ref[at : at + KC, :] - largest).astype(BF)
        for head in range(2):
            mixed = dot(vt_ref[head, :, start : start + keys], prob_ref[:, head * QB : (head + 1) * QB], 1, 0)
            out_ref[head * HDIM : (head + 1) * HDIM, start : start + QB] = (
                mixed[:HDIM] / mixed[HDIM : HDIM + 1]
            ).astype(BF)
    attended = out_ref[...]
    grad = jnp.zeros((LANES, LANES), F32)
    total = jnp.zeros((LANES, LANES), F32)
    for group in range(groups):
        summed = extra_ref[group, :NODE_DEV, :]
        grad += dot(attended[:, group * NODE_DEV : (group + 1) * NODE_DEV], summed, 1, 0)
        total += extra_ref[group, NODE_DEV:, :].astype(F32)
    grad_ref[:LANES, :] = grad.astype(BF)
    grad_ref[LANES:, :] = total.astype(BF)
    node = dot(mix_ref[...], attended, 0, 0).T.astype(BF)
    for group in range(groups):
        node_ref[group] = node[group * NODE_DEV : (group + 1) * NODE_DEV]


def attend(qkv, low, high, win, extra, mix):
    band_rows = qkv.shape[0]
    reach = low.shape[0]
    keys = QB + 2 * reach
    total = band_rows + 2 * reach
    return pl.pallas_call(
        functools.partial(attend_kernel, reach),
        out_shape=(
            jax.ShapeDtypeStruct((extra.shape[0], NODE_DEV, LANES), BF),
            jax.ShapeDtypeStruct((2 * LANES, LANES), BF),
        ),
        scratch_shapes=[
            pltpu.VMEM((total, LANES), BF),
            pltpu.VMEM((2, HDIM + 16, total), BF),
            pltpu.VMEM((keys, 2 * QB), F32),
            pltpu.VMEM((keys, 2 * QB), BF),
            pltpu.VMEM((LANES, band_rows), BF),
        ],
        compiler_params=params(),
        name="attend",
    )(qkv, low, high, win, extra, mix)


def nodes_kernel(parts_ref, node_ref, out_ref):
    total = node_ref[...]
    for group in range(parts_ref.shape[0]):
        total += parts_ref[group].astype(F32)
    out_ref[...] = total.astype(BF)


def sum_nodes(parts, node):
    return pl.pallas_call(
        nodes_kernel,
        out_shape=jax.ShapeDtypeStruct(node.shape, BF),
        compiler_params=params(),
        name="sum_nodes",
    )(parts, node)


def decode_kernel(low_ref, own_ref, high_ref, dec_ref, grid_ref, pred_ref):
    channels, points = grid_ref.shape
    nodes = NODE_DEV
    rows = 4 * LANES
    base = (my_index() - 1) * nodes
    table = jnp.concatenate(
        [
            low_ref[...].astype(F32),
            own_ref[...].astype(F32),
            high_ref[...].astype(F32),
            jnp.zeros((rows - 3 * nodes, LANES), F32),
        ],
        axis=0,
    ).T.astype(BF)
    width = 512
    for at in range(0, points, width):
        node_id = lax.broadcasted_iota(jnp.int32, (rows, width), 0)
        pick = jnp.where(node_id == dec_ref[:, at : at + width] - base, 1.0, 0.0).astype(BF)
        decoded = dot(table, pick, 1, 0)
        pred_ref[:, at : at + width] = (
            grid_ref[:, at : at + width].astype(F32) + decoded[:channels]
        ).astype(BF)


def decode(low, own, high, dec_row, grid_in):
    return pl.pallas_call(
        decode_kernel,
        out_shape=jax.ShapeDtypeStruct(grid_in.shape, BF),
        compiler_params=params(),
        name="decode",
    )(low, own, high, dec_row, grid_in)


def gradient_kernel(parts_ref, w_out_ref, grad_ref):
    model, channels = grad_ref.shape
    groups = parts_ref.shape[0]
    mixed = jnp.zeros((LANES, model), F32)
    for group in range(groups):
        part = parts_ref[group, :LANES, :].astype(F32).T.astype(BF)
        mixed += dot(part, w_out_ref[group * LANES : (group + 1) * LANES, :], 1, 0)
    mixed = mixed.T
    for group in range(groups):
        at = group * LANES
        whole = mixed[at : at + LANES] + parts_ref[group, LANES:, :].astype(F32)
        grad_ref[at : at + LANES, :] = whole[:, :channels]


def gradient(parts, w_out, channels):
    return pl.pallas_call(
        gradient_kernel,
        out_shape=jax.ShapeDtypeStruct((w_out.shape[0], channels), F32),
        compiler_params=params(),
        name="gradient",
    )(parts, w_out)


def steps(axis, shift):
    count = lax.axis_size(axis)
    return [(i, i + shift) for i in range(count) if 0 <= i + shift < count]


def exchange(to_low, to_high, axis):
    from_high = lax.ppermute(to_low, axis, steps(axis, -1))
    from_low = lax.ppermute(to_high, axis, steps(axis, 1))
    return from_low, from_high


def shards(
    grid_in, enc_node, dec_node, win_offsets, w_in, b_in, w_qkv, w_out, norm_gain, w_dec, cotangent
):
    channels = grid_in.shape[0]
    enc_row = enc_node[None]
    dec_row = dec_node[None]
    own, low, high = encode(grid_in, enc_row, w_in, b_in[None], cotangent, dec_row)
    from_low, from_high = exchange(low, high, BOTH)
    packed, enc, summed = project(own, from_low, from_high, norm_gain[None], w_qkv)
    head_rows = lax.all_to_all(packed, "head", split_axis=0, concat_axis=0, tiled=True)
    send, node, mix = side(enc, summed, w_dec, w_out)
    qkv = head_rows.reshape(-1, head_rows.shape[2])
    reach = qkv.shape[0] // 2
    kv_low, kv_high = exchange(qkv[:reach, LANES:], qkv[reach:, LANES:], "band")
    extra = lax.all_to_all(send, "head", split_axis=0, concat_axis=0, tiled=True)
    node_parts, grad_part = attend(qkv, kv_low, kv_high, win_offsets, extra, mix)
    node_parts = lax.all_to_all(node_parts, "head", split_axis=0, concat_axis=0, tiled=True)
    table = sum_nodes(node_parts, node)
    table_low, table_high = exchange(table, table, BOTH)
    prediction = decode(table_low, table, table_high, dec_row, grid_in)
    shift = 1
    count = lax.axis_size("band")
    while shift < count:
        other = lax.ppermute(grad_part, "band", [(i, i ^ shift) for i in range(count)])
        grad_part = (grad_part.astype(F32) + other.astype(F32)).astype(BF)
        shift *= 2
    groups = lax.axis_size("head")
    spread = jnp.broadcast_to(grad_part[None], (groups,) + grad_part.shape)
    parts = lax.all_to_all(spread, "head", split_axis=0, concat_axis=0, tiled=True)
    grad_dec = gradient(parts, w_out, channels)
    return (prediction, grad_dec)


def solution(mesh):
    placed = (
        P(None, BOTH),
        P(BOTH),
        P(BOTH),
        P(None, "band"),
        P(),
        P(),
        P(),
        P(),
        P(),
        P(),
        P(None, BOTH),
    )
    return jax.shard_map(
        shards,
        mesh=mesh,
        in_specs=placed,
        out_specs=(P(None, BOTH), P()),
        check_vma=False,
    )
```

```python
import functools

import jax
import jax.numpy as jnp
from jax import lax
from jax.experimental import pallas as pl
from jax.experimental.pallas import tpu as pltpu
from jax.sharding import PartitionSpec as P

HDIM = 64
NODE_DEV = 160
BOTH = ("band", "head")
LANES = 128
QB = 256
KC = 128
BF = jnp.bfloat16
F32 = jnp.float32
LOG2E = 1.4426950408889634
NEG = -1e30
HBM = pl.BlockSpec(memory_space=pltpu.HBM)
VMEM = pl.BlockSpec(memory_space=pltpu.VMEM)


def params(mib=24):
    return pltpu.CompilerParams(vmem_limit_bytes=mib * 1024 * 1024)


def dot(a, b, ca, cb):
    return lax.dot_general(a, b, (((ca,), (cb,)), ((), ())), preferred_element_type=F32)


def shape(dims, dtype):
    return jax.ShapeDtypeStruct(dims, dtype)


def pinned(*arrays):
    return tuple(pltpu.with_memory_space_constraint(a, pltpu.HBM) for a in arrays)


def started(copies):
    for copy in copies:
        copy.start()
    return copies


def chunk_bases():
    index = lax.axis_index("band") * lax.axis_size("head") + lax.axis_index("head")
    side = 1 - 2 * lax.rem(index, 2)
    return (index - side) * NODE_DEV, index * NODE_DEV, (index + side) * NODE_DEV


def encode_kernel(grid_hbm, enc_hbm, w_hbm, b_hbm, cot_hbm, dec_hbm, far_ref, mid_ref, own_ref,
                  grid_ref, enc_ref, w_ref, b_ref, cot_ref, dec_ref, rows_ref, w_pad, cot_pad, pick_ref, sem):
    channels, points = grid_ref.shape
    model = w_ref.shape[1]
    nodes = NODE_DEV
    copies = started(
        [
            pltpu.make_async_copy(source, target, sem.at[at])
            for at, (source, target) in enumerate(
                [(grid_hbm, grid_ref), (enc_hbm, enc_ref), (w_hbm, w_ref), (b_hbm, b_ref), (cot_hbm, cot_ref), (dec_hbm, dec_ref)]
            )
        ]
    )
    bases = chunk_bases()
    node_id = lax.broadcasted_iota(jnp.int32, (nodes, points), 0)

    def pick(target):
        for at, base in enumerate(bases):
            pick_ref[at * nodes : (at + 1) * nodes, :] = jnp.where(node_id == target - base, 1.0, 0.0).astype(BF)

    copies[1].wait()
    pick(enc_ref[...])
    copies[0].wait()
    padded = jnp.concatenate(
        [grid_ref[...].astype(F32), jnp.zeros((LANES - channels, points), F32)], axis=0
    )
    rows_ref[...] = padded.T.astype(BF)
    copies[2].wait()
    copies[3].wait()
    w_pad[...] = jnp.zeros_like(w_pad)
    w_pad[:channels, :] = (w_ref[...].astype(F32) * 0.5).astype(BF)
    width = 256
    for at in range(0, model, width):
        half = dot(rows_ref[...], w_pad[:, at : at + width], 1, 0) + b_ref[:, at : at + width] * 0.5
        message = (half + half * jnp.tanh(half)).astype(BF)
        spread = dot(pick_ref[...], message, 1, 0)
        far_ref[:, at : at + width] = spread[:nodes].astype(BF)
        mid_ref[:, at : at + width] = spread[nodes : 2 * nodes].astype(BF)
        own_ref[:, at : at + width] = spread[2 * nodes :]
    copies[4].wait()
    copies[5].wait()
    cot_pad[...] = jnp.zeros_like(cot_pad)
    cot_pad[:channels, :] = cot_ref[...]
    pick(dec_ref[...])
    spread = dot(pick_ref[...], cot_pad[...], 1, 1)
    far_ref[:, model:] = spread[:nodes].astype(BF)
    mid_ref[:, model:] = spread[nodes : 2 * nodes].astype(BF)
    own_ref[:, model:] = spread[2 * nodes :]


def encode(grid_in, enc_row, w_in, b_row, cotangent, dec_row):
    channels, points = grid_in.shape
    model = w_in.shape[1]
    wide = model + LANES
    operands = (grid_in, enc_row, w_in, b_row, cotangent, dec_row)
    return pl.pallas_call(
        encode_kernel,
        in_specs=[HBM] * 6,
        out_specs=(VMEM,) * 3,
        out_shape=(shape((NODE_DEV, wide), BF), shape((NODE_DEV, wide), BF), shape((NODE_DEV, wide), F32)),
        scratch_shapes=[pltpu.VMEM(a.shape, a.dtype) for a in operands]
        + [
            pltpu.VMEM((points, LANES), BF),
            pltpu.VMEM((LANES, model), BF),
            pltpu.VMEM((LANES, points), BF),
            pltpu.VMEM((3 * NODE_DEV, points), BF),
            pltpu.SemaphoreType.DMA((6,)),
        ],
        compiler_params=params(),
        name="encode",
    )(*pinned(*operands))


def load_kernel(w_hbm, out_hbm, dec_hbm, after_ref, w_ref, dec_ref, mix_ref, out_rows, dec_rows, sem):
    channels = dec_rows.shape[0]
    at = pl.multiple_of(lax.axis_index("head") * LANES, LANES)
    copies = started(
        [
            pltpu.make_async_copy(out_hbm.at[pl.ds(at, LANES), :], out_rows, sem.at[0]),
            pltpu.make_async_copy(dec_hbm, dec_rows, sem.at[1]),
            pltpu.make_async_copy(w_hbm, w_ref, sem.at[2]),
        ]
    )
    copies[0].wait()
    copies[1].wait()
    dec_ref[...] = jnp.zeros_like(dec_ref)
    dec_ref[:channels, :] = dec_rows[...]
    mix_ref[...] = dot(out_rows[...], dec_ref[...], 1, 1).astype(BF)
    copies[2].wait()


def load(w_qkv, w_out, dec_cols, after):
    model = w_qkv.shape[0]
    return pl.pallas_call(
        load_kernel,
        in_specs=[HBM] * 3 + [pl.BlockSpec(memory_space=pl.ANY)],
        out_specs=(VMEM,) * 3,
        out_shape=(shape(w_qkv.shape, BF), shape((LANES, model), BF), shape((LANES, LANES), BF)),
        scratch_shapes=[
            pltpu.VMEM((LANES, model), BF),
            pltpu.VMEM(dec_cols.shape, BF),
            pltpu.SemaphoreType.DMA((3,)),
        ],
        compiler_params=params(),
        cost_estimate=pl.CostEstimate(flops=2 * model * LANES * LANES, bytes_accessed=2 * w_qkv.size, transcendentals=0),
        name="load",
    )(*pinned(w_qkv, w_out, dec_cols), after)


def project_kernel(own_ref, mid_ref, far_ref, gain_ref, w_ref, packed_hbm, enc_ref, s_ref, packed, sem):
    model = gain_ref.shape[1]
    total = own_ref[...] + mid_ref[...].astype(F32) + far_ref[...].astype(F32)
    enc = total[:, :model]
    s_ref[...] = total[:, model:].astype(BF)
    enc_ref[...] = enc
    centred = enc - jnp.mean(enc, axis=1, keepdims=True)
    spread_sq = jnp.mean(centred * centred, axis=1, keepdims=True)
    normed = (centred * lax.rsqrt(spread_sq + 1e-05) * gain_ref[...]).astype(BF)
    scale = HDIM ** (-0.5) * LOG2E
    copies = []
    for pair in range(model // (2 * LANES)):
        for part in range(3):
            at = part * model + pair * 2 * LANES
            cols = dot(normed, w_ref[:, at : at + 2 * LANES], 1, 0)
            if part == 0:
                cols = cols * scale
            cols = cols.astype(BF)
            for half in range(2):
                packed[2 * pair + half, :, part * LANES : (part + 1) * LANES] = cols[:, half * LANES : (half + 1) * LANES]
        rows = pl.ds(2 * pair, 2)
        copies += started([pltpu.make_async_copy(packed.at[rows], packed_hbm.at[rows], sem.at[pair])])
    for copy in copies:
        copy.wait()


def project(own, mid, far, gain_row, w_qkv):
    model = w_qkv.shape[0]
    groups = model // LANES
    return pl.pallas_call(
        project_kernel,
        in_specs=[VMEM] * 5,
        out_specs=(HBM, VMEM, VMEM),
        out_shape=(
            shape((groups, NODE_DEV, 3 * LANES), BF),
            shape((NODE_DEV, model), F32),
            shape((NODE_DEV, LANES), BF),
        ),
        scratch_shapes=[
            pltpu.VMEM((groups, NODE_DEV, 3 * LANES), BF),
            pltpu.SemaphoreType.DMA((groups // 2,)),
        ],
        compiler_params=params(),
        name="project",
    )(own, mid, far, gain_row, w_qkv)


def side_kernel(enc_ref, s_ref, dec_ref, send_hbm, node_ref, send, sem):
    groups = send.shape[0]
    enc = enc_ref[...]
    summed = s_ref[...]
    high = enc.astype(BF)
    low = (enc - high.astype(F32)).astype(BF)
    node_ref[...] = dot(high, dec_ref[...], 1, 1)
    grad = (dot(summed, high, 0, 0) + dot(summed, low, 0, 0)).astype(BF)
    for group in range(groups):
        send[group, :NODE_DEV, :] = summed
        send[group, NODE_DEV:, :] = grad[:, group * LANES : (group + 1) * LANES]
    copy = pltpu.make_async_copy(send, send_hbm, sem)
    copy.start()
    copy.wait()


def side(enc, summed, dec_pad):
    groups = enc.shape[1] // LANES
    send_shape = (groups, NODE_DEV + LANES, LANES)
    return pl.pallas_call(
        side_kernel,
        in_specs=[VMEM] * 3,
        out_specs=(HBM, VMEM),
        out_shape=(shape(send_shape, BF), shape((NODE_DEV, LANES), F32)),
        scratch_shapes=[pltpu.VMEM(send_shape, BF), pltpu.SemaphoreType.DMA],
        compiler_params=params(),
        name="side",
    )(enc, summed, dec_pad)


def limits(win, reach, start, first_node, node_total):
    column = lax.broadcasted_iota(jnp.int32, (1, QB), 1) + reach
    bottom = jnp.maximum(column - win[0:1], reach - start - first_node)
    top = jnp.minimum(column + win[1:2], reach - start - first_node + node_total - 1)
    return jnp.concatenate([bottom, bottom], axis=1), jnp.concatenate([top, top], axis=1)


def masked(scores, at, reach, bottom, top):
    key = lax.broadcasted_iota(jnp.int32, scores.shape, 0) + at
    if at + KC - 1 <= reach:
        keep = key >= bottom
    elif at >= reach + QB - 1:
        keep = key <= top
    else:
        keep = (key >= bottom) & (key <= top)
    return jnp.where(keep, scores, NEG)


def fold(scores):
    return jnp.max(scores.reshape(KC // 8, 8, 2 * QB), axis=0)


def near_kernel(reach, qkv_ref, win_ref, acc_ref, top_ref, q_ref, k_ref, v_ref, vt_ref, score_ref, prob_ref):
    groups = qkv_ref.shape[0]
    band_rows = groups * NODE_DEV
    first_node = lax.axis_index("band") * band_rows
    node_total = lax.axis_size("band") * band_rows
    lane = lax.broadcasted_iota(jnp.int32, (NODE_DEV, LANES), 1)
    zero = jnp.zeros((NODE_DEV, LANES), BF)
    for group in range(groups):
        rows = pl.ds((group ^ 1) * NODE_DEV, NODE_DEV)
        queries = qkv_ref[group, :, :LANES]
        q_ref[0, rows, :] = jnp.where(lane < HDIM, queries, zero)
        q_ref[1, rows, :] = jnp.where(lane >= HDIM, queries, zero)
        k_ref[rows, :] = qkv_ref[group, :, LANES : 2 * LANES]
        v_ref[rows, :] = qkv_ref[group, :, 2 * LANES :].astype(F32)
    vt = v_ref[...].T.astype(BF)
    for head in range(2):
        vt_ref[head, :HDIM, :] = vt[head * HDIM : (head + 1) * HDIM]
        vt_ref[head, HDIM:, :] = jnp.ones((16, band_rows), BF)
    for block in range(band_rows // QB):
        start = block * QB
        both = jnp.concatenate([q_ref[0, start : start + QB, :], q_ref[1, start : start + QB, :]], axis=0)
        bottom, top = limits(win_ref[:, start : start + QB], reach, start, first_node, node_total)
        first = max(0, reach - start)
        last = min(QB + 2 * reach, band_rows + reach - start)
        largest = jnp.full((8, 2 * QB), NEG, F32)
        for at in range(first, last, KC):
            key = start + at - reach
            scores = masked(dot(k_ref[key : key + KC, :], both, 1, 1), at, reach, bottom, top)
            score_ref[at - first : at - first + KC, :] = scores
            largest = jnp.maximum(largest, fold(scores))
        largest = jnp.max(largest, axis=0, keepdims=True)
        top_ref[block] = largest
        for at in range(0, last - first, KC):
            prob_ref[at : at + KC, :] = jnp.exp2(score_ref[at : at + KC, :] - largest).astype(BF)
        key = start + first - reach
        for head in range(2):
            acc_ref[block, head] = dot(
                vt_ref[head, :, key : key + last - first],
                prob_ref[: last - first, head * QB : (head + 1) * QB],
                1,
                0,
            )


def near(qkv, win, reach):
    groups = qkv.shape[0]
    band_rows = groups * NODE_DEV
    blocks = band_rows // QB
    keys = min(QB + 2 * reach, band_rows)
    return pl.pallas_call(
        functools.partial(near_kernel, reach),
        in_specs=[VMEM] * 2,
        out_specs=(VMEM,) * 3,
        out_shape=(
            shape((blocks, 2, HDIM + 16, QB), F32),
            shape((blocks, 1, 2 * QB), F32),
            shape((2, band_rows, LANES), BF),
        ),
        scratch_shapes=[
            pltpu.VMEM((band_rows, LANES), BF),
            pltpu.VMEM((band_rows, LANES), F32),
            pltpu.VMEM((2, HDIM + 16, band_rows), BF),
            pltpu.VMEM((keys, 2 * QB), F32),
            pltpu.VMEM((keys, 2 * QB), BF),
        ],
        compiler_params=params(),
        cost_estimate=pl.CostEstimate(flops=6_000_000_000, bytes_accessed=4_000_000, transcendentals=3_000_000),
        name="near",
    )(qkv, win)


def far_kernel(reach, q_ref, acc_ref, top_ref, low_ref, high_ref, win_ref, extra_ref, mix_ref,
               node_hbm, grad_ref, k_ref, v_ref, vt_ref, score_ref, prob_ref, out_ref, node_ref, sem):
    groups = extra_ref.shape[0]
    band_rows = groups * NODE_DEV
    first_node = lax.axis_index("band") * band_rows
    node_total = lax.axis_size("band") * band_rows
    for side_at, half in enumerate((low_ref, high_ref)):
        for group in range(groups // 2):
            rows = pl.ds(side_at * reach + (group ^ 1) * NODE_DEV, NODE_DEV)
            k_ref[rows, :] = half[group, :, :LANES]
            v_ref[rows, :] = half[group, :, LANES:].astype(F32)
    vt = v_ref[...].T.astype(BF)
    for head in range(2):
        vt_ref[head, :HDIM, :] = vt[head * HDIM : (head + 1) * HDIM]
        vt_ref[head, HDIM:, :] = jnp.ones((16, 2 * reach), BF)
    for block in range(band_rows // QB):
        start = block * QB
        both = jnp.concatenate([q_ref[0, start : start + QB, :], q_ref[1, start : start + QB, :]], axis=0)
        bottom, top = limits(win_ref[:, start : start + QB], reach, start, first_node, node_total)
        low_to = max(0, reach - start)
        high_from = min(QB + 2 * reach, band_rows + reach - start)
        pieces = [(at, start + at) for at in range(0, low_to, KC)]
        pieces += [(at, start + at - band_rows) for at in range(high_from, QB + 2 * reach, KC)]
        before = top_ref[block]
        largest = jnp.full((8, 2 * QB), NEG, F32)
        for row, (at, key) in enumerate(pieces):
            scores = masked(dot(k_ref[key : key + KC, :], both, 1, 1), at, reach, bottom, top)
            score_ref[row * KC : (row + 1) * KC, :] = scores
            largest = jnp.maximum(largest, fold(scores))
        largest = jnp.maximum(jnp.max(largest, axis=0, keepdims=True), before)
        decay = jnp.exp2(before - largest)
        for row in range(len(pieces)):
            prob_ref[row * KC : (row + 1) * KC, :] = jnp.exp2(score_ref[row * KC : (row + 1) * KC, :] - largest).astype(BF)
        low_rows, high_rows = low_to, QB + 2 * reach - high_from
        for head in range(2):
            cols = slice(head * QB, (head + 1) * QB)
            mixed = acc_ref[block, head] * decay[:, cols]
            if low_rows:
                mixed += dot(vt_ref[head, :, start:reach], prob_ref[:low_rows, cols], 1, 0)
            if high_rows:
                at = reach
                mixed += dot(vt_ref[head, :, at : at + high_rows], prob_ref[low_rows : low_rows + high_rows, cols], 1, 0)
            out_ref[head * HDIM : (head + 1) * HDIM, start : start + QB] = (
                mixed[:HDIM] / mixed[HDIM : HDIM + 1]
            ).astype(BF)
    attended = out_ref[...]
    node = dot(mix_ref[...], attended, 0, 0).T.astype(BF)
    for group in range(groups):
        node_ref[group] = node[(group ^ 1) * NODE_DEV : ((group ^ 1) + 1) * NODE_DEV]
    copy = pltpu.make_async_copy(node_ref, node_hbm, sem)
    copy.start()
    grad = jnp.zeros((LANES, LANES), F32)
    total = jnp.zeros((LANES, LANES), F32)
    for group in range(groups):
        at = (group ^ 1) * NODE_DEV
        grad += dot(extra_ref[group, :NODE_DEV, :], attended[:, at : at + NODE_DEV], 0, 1)
        total += extra_ref[group, NODE_DEV:, :].astype(F32)
    grad_ref[:LANES, :] = grad
    grad_ref[LANES:, :] = total
    copy.wait()


def far(queries, acc, top, low, high, win, extra, mix):
    groups = extra.shape[0]
    reach = low.shape[0] * NODE_DEV
    band_rows = groups * NODE_DEV
    return pl.pallas_call(
        functools.partial(far_kernel, reach),
        in_specs=[VMEM] * 8,
        out_specs=(HBM, VMEM),
        out_shape=(shape((groups, NODE_DEV, LANES), BF), shape((2 * LANES, LANES), F32)),
        scratch_shapes=[
            pltpu.VMEM((2 * reach, LANES), BF),
            pltpu.VMEM((2 * reach, LANES), F32),
            pltpu.VMEM((2, HDIM + 16, 2 * reach), BF),
            pltpu.VMEM((reach, 2 * QB), F32),
            pltpu.VMEM((reach, 2 * QB), BF),
            pltpu.VMEM((LANES, band_rows), BF),
            pltpu.VMEM((groups, NODE_DEV, LANES), BF),
            pltpu.SemaphoreType.DMA,
        ],
        compiler_params=params(),
        name="far",
    )(queries, acc, top, low, high, win, extra, mix)


def nodes_kernel(parts_ref, node_ref, out_ref):
    total = node_ref[...]
    for group in range(parts_ref.shape[0]):
        total += parts_ref[group].astype(F32)
    out_ref[...] = total.astype(BF)


def sum_nodes(parts, node):
    return pl.pallas_call(
        nodes_kernel,
        in_specs=[VMEM] * 2,
        out_specs=VMEM,
        out_shape=shape(node.shape, BF),
        compiler_params=params(),
        name="sum_nodes",
    )(parts, node)


def decode_kernel(far_ref, mid_ref, own_ref, dec_ref, grid_ref, pred_ref):
    channels, points = grid_ref.shape
    nodes = NODE_DEV
    rows = 4 * LANES
    table = jnp.concatenate(
        [
            far_ref[...].astype(F32),
            mid_ref[...].astype(F32),
            own_ref[...].astype(F32),
            jnp.zeros((rows - 3 * nodes, LANES), F32),
        ],
        axis=0,
    ).T.astype(BF)
    width = 512
    bases = chunk_bases()
    node_id = lax.broadcasted_iota(jnp.int32, (nodes, width), 0)
    for at in range(0, points, width):
        target = dec_ref[:, at : at + width]
        pick = [jnp.where(node_id == target - base, 1.0, 0.0) for base in bases]
        pick = jnp.concatenate(pick + [jnp.zeros((rows - 3 * nodes, width), F32)], axis=0).astype(BF)
        decoded = dot(table, pick, 1, 0)
        pred_ref[:, at : at + width] = (
            grid_ref[:, at : at + width].astype(F32) + decoded[:channels]
        ).astype(BF)


def decode(far_rows, mid_rows, own_rows, dec_row, grid_in):
    return pl.pallas_call(
        decode_kernel,
        in_specs=[VMEM] * 5,
        out_specs=VMEM,
        out_shape=shape(grid_in.shape, BF),
        compiler_params=params(),
        name="decode",
    )(far_rows, mid_rows, own_rows, dec_row, grid_in)


def gradient_kernel(parts_ref, w_out_ref, grad_ref):
    channels, model = grad_ref.shape
    mixed = jnp.zeros((LANES, model), F32)
    for group in range(parts_ref.shape[0]):
        mixed += dot(parts_ref[group, :LANES, :], w_out_ref[group * LANES : (group + 1) * LANES, :], 1, 0)
    for group in range(parts_ref.shape[0]):
        cols = slice(group * LANES, (group + 1) * LANES)
        whole = mixed[:, cols] + parts_ref[group, LANES:, :].astype(F32)
        grad_ref[:, cols] = whole[:channels]


def gradient(parts, w_out, channels):
    return pl.pallas_call(
        gradient_kernel,
        in_specs=[VMEM] * 2,
        out_specs=VMEM,
        out_shape=shape((channels, w_out.shape[0]), F32),
        compiler_params=params(),
        name="gradient",
    )(parts, w_out)


def total_devices():
    return lax.axis_size("band") * lax.axis_size("head")


def to_partner(block):
    return lax.ppermute(block, BOTH, [(i, i ^ 1) for i in range(total_devices())])


def two_over(block, sign):
    count = total_devices()
    pairs = [(i, i + sign * (2 - 4 * (i % 2))) for i in range(count)]
    return lax.ppermute(block, BOTH, [(i, j) for i, j in pairs if 0 <= j < count])


def along_band(block, shift):
    count = lax.axis_size("band")
    return lax.ppermute(block, "band", [(i, i + shift) for i in range(count) if 0 <= i + shift < count])


def swap(block):
    return lax.all_to_all(block, "head", split_axis=0, concat_axis=0, tiled=True)


def shards(
    grid_in, enc_node, dec_node, win_offsets, w_in, b_in, w_qkv, w_out, norm_gain, w_dec, cotangent
):
    channels = grid_in.shape[0]
    groups = lax.axis_size("head")
    dec_row = dec_node[None]
    far_part, mid_part, own = encode(grid_in, enc_node[None], w_in, b_in[None], cotangent, dec_row)
    weights, dec_pad, mix = load(w_qkv, w_out, w_dec.T, far_part)
    mid_in = to_partner(mid_part)
    far_in = two_over(far_part, -1)
    packed, enc, summed = project(own, mid_in, far_in, norm_gain[None], weights)
    qkv = swap(packed)
    send, node = side(enc, summed, dec_pad)
    half = groups // 2
    reach = half * NODE_DEV
    from_low = along_band(qkv[half:, :, LANES:], 1)
    from_high = along_band(qkv[:half, :, LANES:], -1)
    extra = swap(send)
    acc, top, queries = near(qkv, win_offsets, reach)
    node_parts, grad_part = far(queries, acc, top, from_low, from_high, win_offsets, extra, mix)
    table = sum_nodes(swap(node_parts), node)
    prediction = decode(two_over(table, 1), to_partner(table), table, dec_row, grid_in)
    shift = 1
    count = lax.axis_size("band")
    while shift < count:
        other = lax.ppermute(grad_part, "band", [(i, i ^ shift) for i in range(count)])
        grad_part = (grad_part.astype(F32) + other.astype(F32)).astype(BF)
        shift *= 2
    parts = swap(jnp.broadcast_to(grad_part[None], (groups,) + grad_part.shape))
    grad_dec = gradient(parts, w_out, channels).T
    return (prediction, grad_dec)


def solution(mesh):
    placed = (
        P(None, BOTH),
        P(BOTH),
        P(BOTH),
        P(None, "band"),
        P(),
        P(),
        P(),
        P(),
        P(),
        P(),
        P(None, BOTH),
    )
    return jax.shard_map(
        shards,
        mesh=mesh,
        in_specs=placed,
        out_specs=(P(None, BOTH), P()),
        check_vma=False,
    )
```

```python
import functools

import jax
import jax.numpy as jnp
from jax import lax
from jax.experimental import pallas as pl
from jax.experimental.pallas import tpu as pltpu
from jax.sharding import PartitionSpec as P

HDIM = 64
NODE_DEV = 160
BOTH = ("band", "head")
LANES = 128
QB = 256
KC = 128
ROWS = 112
BF = jnp.bfloat16
F32 = jnp.float32
LOG2E = 1.4426950408889634
NEG = -1e30
HBM = pl.BlockSpec(memory_space=pltpu.HBM)
VMEM = pl.BlockSpec(memory_space=pltpu.VMEM)


def params(mib=24):
    return pltpu.CompilerParams(vmem_limit_bytes=mib * 1024 * 1024)


def dot(a, b, ca, cb):
    return lax.dot_general(a, b, (((ca,), (cb,)), ((), ())), preferred_element_type=F32)


def shape(dims, dtype):
    return jax.ShapeDtypeStruct(dims, dtype)


def in_hbm(a):
    return pltpu.HBM(a.shape, a.dtype)


def pinned(*arrays):
    return tuple(pltpu.with_memory_space_constraint(a, pltpu.HBM) for a in arrays)


def started(copies):
    for copy in copies:
        copy.start()
    return copies


def chunk_bases():
    index = lax.axis_index("band") * lax.axis_size("head") + lax.axis_index("head")
    side = 1 - 2 * lax.rem(index, 2)
    return (index - side) * NODE_DEV, index * NODE_DEV, (index + side) * NODE_DEV


def encode_kernel(grid_hbm, enc_hbm, w_hbm, b_hbm, cot_hbm, dec_hbm, far_ref, mid_ref, own_ref,
                  grid_ref, enc_ref, w_ref, b_ref, cot_ref, dec_ref, rows_ref, w_pad, cot_pad, pick_ref, sem):
    channels, points = grid_ref.shape
    model = w_ref.shape[1]
    nodes = NODE_DEV
    copies = started(
        [
            pltpu.make_async_copy(source, target, sem.at[at])
            for at, (source, target) in enumerate(
                [(grid_hbm, grid_ref), (enc_hbm, enc_ref), (w_hbm, w_ref), (b_hbm, b_ref), (cot_hbm, cot_ref), (dec_hbm, dec_ref)]
            )
        ]
    )
    bases = chunk_bases()
    node_id = lax.broadcasted_iota(jnp.int32, (nodes, points), 0)

    def pick(target):
        for at, base in enumerate(bases):
            pick_ref[at * nodes : (at + 1) * nodes, :] = jnp.where(node_id == target - base, 1.0, 0.0).astype(BF)

    copies[1].wait()
    pick(enc_ref[...])
    copies[0].wait()
    padded = jnp.concatenate(
        [grid_ref[...].astype(F32), jnp.zeros((LANES - channels, points), F32)], axis=0
    )
    rows_ref[...] = padded.T.astype(BF)
    copies[2].wait()
    copies[3].wait()
    w_pad[...] = jnp.zeros_like(w_pad)
    w_pad[:channels, :] = (w_ref[...].astype(F32) * 0.5).astype(BF)
    width = 256
    for at in range(0, model, width):
        half = dot(rows_ref[...], w_pad[:, at : at + width], 1, 0) + b_ref[:, at : at + width] * 0.5
        message = (half + half * jnp.tanh(half)).astype(BF)
        spread = dot(pick_ref[...], message, 1, 0)
        far_ref[:, at : at + width] = spread[:nodes].astype(BF)
        mid_ref[:, at : at + width] = spread[nodes : 2 * nodes].astype(BF)
        own_ref[:, at : at + width] = spread[2 * nodes :]
    copies[4].wait()
    copies[5].wait()
    cot_pad[...] = jnp.zeros_like(cot_pad)
    cot_pad[:channels, :] = cot_ref[...]
    pick(dec_ref[...])
    spread = dot(pick_ref[...], cot_pad[...], 1, 1)
    far_ref[:, model:] = spread[:nodes].astype(BF)
    mid_ref[:, model:] = spread[nodes : 2 * nodes].astype(BF)
    own_ref[:, model:] = spread[2 * nodes :]


def encode(grid_in, enc_row, w_in, b_row, cotangent, dec_row):
    channels, points = grid_in.shape
    model = w_in.shape[1]
    wide = model + LANES
    operands = (grid_in, enc_row, w_in, b_row, cotangent, dec_row)
    return pl.pallas_call(
        encode_kernel,
        in_specs=[HBM] * 6,
        out_specs=(VMEM,) * 3,
        out_shape=(shape((NODE_DEV, wide), BF), shape((NODE_DEV, wide), BF), shape((NODE_DEV, wide), F32)),
        scratch_shapes=[pltpu.VMEM(a.shape, a.dtype) for a in operands]
        + [
            pltpu.VMEM((points, LANES), BF),
            pltpu.VMEM((LANES, model), BF),
            pltpu.VMEM((LANES, points), BF),
            pltpu.VMEM((3 * NODE_DEV, points), BF),
            pltpu.SemaphoreType.DMA((6,)),
        ],
        compiler_params=params(),
        name="encode",
    )(*pinned(*operands))


def load_kernel(w_hbm, out_hbm, dec_hbm, after_ref, w_ref, dec_ref, mix_hbm, mix_ref, out_rows, dec_rows, sem):
    channels = dec_rows.shape[0]
    at = pl.multiple_of(lax.axis_index("head") * LANES, LANES)
    copies = started(
        [
            pltpu.make_async_copy(out_hbm.at[pl.ds(at, LANES), :], out_rows, sem.at[0]),
            pltpu.make_async_copy(dec_hbm, dec_rows, sem.at[1]),
            pltpu.make_async_copy(w_hbm, w_ref, sem.at[2]),
        ]
    )
    copies[0].wait()
    copies[1].wait()
    dec_ref[...] = jnp.zeros_like(dec_ref)
    dec_ref[:channels, :] = dec_rows[...]
    mix_ref[...] = dot(out_rows[...], dec_ref[...], 1, 1).astype(BF)
    copy = pltpu.make_async_copy(mix_ref, mix_hbm, sem.at[3])
    copy.start()
    copy.wait()
    copies[2].wait()


def load(w_qkv, w_out, dec_cols, after):
    model = w_qkv.shape[0]
    return pl.pallas_call(
        load_kernel,
        in_specs=[HBM] * 3 + [pl.BlockSpec(memory_space=pl.ANY)],
        out_specs=(VMEM, VMEM, HBM),
        out_shape=(shape(w_qkv.shape, BF), shape((LANES, model), BF), in_hbm(shape((LANES, LANES), BF))),
        scratch_shapes=[
            pltpu.VMEM((LANES, LANES), BF),
            pltpu.VMEM((LANES, model), BF),
            pltpu.VMEM(dec_cols.shape, BF),
            pltpu.SemaphoreType.DMA((4,)),
        ],
        compiler_params=params(),
        cost_estimate=pl.CostEstimate(flops=2 * model * LANES * LANES, bytes_accessed=2 * w_qkv.size, transcendentals=0),
        name="load",
    )(*pinned(w_qkv, w_out, dec_cols), after)


def project_kernel(own_ref, mid_ref, far_ref, gain_ref, w_ref, packed_hbm, enc_ref, s_ref, packed, sem):
    model = gain_ref.shape[1]
    total = own_ref[...] + mid_ref[...].astype(F32) + far_ref[...].astype(F32)
    enc = total[:, :model]
    s_ref[...] = total[:, model:].astype(BF)
    enc_ref[...] = enc
    centred = enc - jnp.mean(enc, axis=1, keepdims=True)
    spread_sq = jnp.mean(centred * centred, axis=1, keepdims=True)
    normed = (centred * lax.rsqrt(spread_sq + 1e-05) * gain_ref[...]).astype(BF)
    scale = HDIM ** (-0.5) * LOG2E
    copies = []
    for pair in range(model // (2 * LANES)):
        for part in range(3):
            at = part * model + pair * 2 * LANES
            cols = dot(normed, w_ref[:, at : at + 2 * LANES], 1, 0)
            if part == 0:
                cols = cols * scale
            cols = cols.astype(BF)
            for half in range(2):
                packed[2 * pair + half, :, part * LANES : (part + 1) * LANES] = cols[:, half * LANES : (half + 1) * LANES]
        rows = pl.ds(2 * pair, 2)
        copies += started([pltpu.make_async_copy(packed.at[rows], packed_hbm.at[rows], sem.at[pair])])
    for copy in copies:
        copy.wait()


def project(own, mid, far, gain_row, w_qkv):
    model = w_qkv.shape[0]
    groups = model // LANES
    return pl.pallas_call(
        project_kernel,
        in_specs=[VMEM] * 5,
        out_specs=(HBM, VMEM, VMEM),
        out_shape=(
            in_hbm(shape((groups, NODE_DEV, 3 * LANES), BF)),
            shape((NODE_DEV, model), F32),
            shape((NODE_DEV, LANES), BF),
        ),
        scratch_shapes=[
            pltpu.VMEM((groups, NODE_DEV, 3 * LANES), BF),
            pltpu.SemaphoreType.DMA((groups // 2,)),
        ],
        compiler_params=params(),
        name="project",
    )(own, mid, far, gain_row, w_qkv)


def side_kernel(enc_ref, s_ref, dec_ref, send_hbm, node_ref, send, sem):
    groups = send.shape[0]
    enc = enc_ref[...]
    summed = s_ref[...]
    high = enc.astype(BF)
    low = (enc - high.astype(F32)).astype(BF)
    node_ref[...] = dot(high, dec_ref[...], 1, 1)
    grad = (dot(summed, high, 0, 0) + dot(summed, low, 0, 0)).astype(BF)
    for group in range(groups):
        send[group, :NODE_DEV, :] = summed
        send[group, NODE_DEV:, :] = grad[:ROWS, group * LANES : (group + 1) * LANES]
    copy = pltpu.make_async_copy(send, send_hbm, sem)
    copy.start()
    copy.wait()


def side(enc, summed, dec_pad):
    groups = enc.shape[1] // LANES
    send_shape = (groups, NODE_DEV + ROWS, LANES)
    return pl.pallas_call(
        side_kernel,
        in_specs=[VMEM] * 3,
        out_specs=(HBM, VMEM),
        out_shape=(in_hbm(shape(send_shape, BF)), shape((NODE_DEV, LANES), F32)),
        scratch_shapes=[pltpu.VMEM(send_shape, BF), pltpu.SemaphoreType.DMA],
        compiler_params=params(),
        name="side",
    )(enc, summed, dec_pad)


def limits(win, reach, start, first_node, node_total):
    column = lax.broadcasted_iota(jnp.int32, (1, QB), 1) + reach
    bottom = jnp.maximum(column - win[0:1], reach - start - first_node)
    top = jnp.minimum(column + win[1:2], reach - start - first_node + node_total - 1)
    return jnp.concatenate([bottom, bottom], axis=1), jnp.concatenate([top, top], axis=1)


def masked(scores, at, reach, bottom, top):
    key = lax.broadcasted_iota(jnp.int32, scores.shape, 0) + at
    if at + KC - 1 <= reach:
        keep = key >= bottom
    elif at >= reach + QB - 1:
        keep = key <= top
    else:
        keep = (key >= bottom) & (key <= top)
    return jnp.where(keep, scores, NEG)


def fold(scores):
    return jnp.max(scores.reshape(KC // 8, 8, 2 * QB), axis=0)


def near_kernel(reach, qkv_ref, win_hbm, acc_hbm, top_hbm, q_hbm,
                win_ref, acc_ref, top_ref, q_ref, k_ref, v_ref, vt_ref, score_ref, prob_ref, sem):
    groups = qkv_ref.shape[0]
    win_copy = pltpu.make_async_copy(win_hbm, win_ref, sem.at[0])
    win_copy.start()
    band_rows = groups * NODE_DEV
    first_node = lax.axis_index("band") * band_rows
    node_total = lax.axis_size("band") * band_rows
    lane = lax.broadcasted_iota(jnp.int32, (NODE_DEV, LANES), 1)
    zero = jnp.zeros((NODE_DEV, LANES), BF)
    for group in range(groups):
        rows = pl.ds((group ^ 1) * NODE_DEV, NODE_DEV)
        queries = qkv_ref[group, :, :LANES]
        q_ref[0, rows, :] = jnp.where(lane < HDIM, queries, zero)
        q_ref[1, rows, :] = jnp.where(lane >= HDIM, queries, zero)
        k_ref[rows, :] = qkv_ref[group, :, LANES : 2 * LANES]
        v_ref[rows, :] = qkv_ref[group, :, 2 * LANES :].astype(F32)
    vt = v_ref[...].T.astype(BF)
    for head in range(2):
        vt_ref[head, :HDIM, :] = vt[head * HDIM : (head + 1) * HDIM]
        vt_ref[head, HDIM:, :] = jnp.ones((16, band_rows), BF)
    copies = started([pltpu.make_async_copy(q_ref, q_hbm, sem.at[1])])
    win_copy.wait()
    for block in range(band_rows // QB):
        start = block * QB
        both = jnp.concatenate([q_ref[0, start : start + QB, :], q_ref[1, start : start + QB, :]], axis=0)
        bottom, top = limits(win_ref[:, start : start + QB], reach, start, first_node, node_total)
        first = max(0, reach - start)
        last = min(QB + 2 * reach, band_rows + reach - start)
        largest = jnp.full((8, 2 * QB), NEG, F32)
        for at in range(first, last, KC):
            key = start + at - reach
            scores = masked(dot(k_ref[key : key + KC, :], both, 1, 1), at, reach, bottom, top)
            score_ref[at - first : at - first + KC, :] = scores
            largest = jnp.maximum(largest, fold(scores))
        largest = jnp.max(largest, axis=0, keepdims=True)
        top_ref[block] = largest
        for at in range(0, last - first, KC):
            prob_ref[at : at + KC, :] = jnp.exp2(score_ref[at : at + KC, :] - largest).astype(BF)
        key = start + first - reach
        for head in range(2):
            acc_ref[block, head] = dot(
                vt_ref[head, :, key : key + last - first],
                prob_ref[: last - first, head * QB : (head + 1) * QB],
                1,
                0,
            )
        copies += started([pltpu.make_async_copy(acc_ref.at[block], acc_hbm.at[block], sem.at[3 + block])])
    copies += started([pltpu.make_async_copy(top_ref, top_hbm, sem.at[2])])
    for copy in copies:
        copy.wait()


def near(qkv, win, reach):
    groups = qkv.shape[0]
    band_rows = groups * NODE_DEV
    blocks = band_rows // QB
    keys = min(QB + 2 * reach, band_rows)
    outs = (
        shape((blocks, 2, HDIM + 16, QB), F32),
        shape((blocks, 1, 2 * QB), F32),
        shape((2, band_rows, LANES), BF),
    )
    return pl.pallas_call(
        functools.partial(near_kernel, reach),
        in_specs=[VMEM, HBM],
        out_specs=(HBM,) * 3,
        out_shape=tuple(in_hbm(a) for a in outs),
        scratch_shapes=[
            pltpu.VMEM(win.shape, win.dtype),
            *[pltpu.VMEM(a.shape, a.dtype) for a in outs],
            pltpu.VMEM((band_rows, LANES), BF),
            pltpu.VMEM((band_rows, LANES), F32),
            pltpu.VMEM((2, HDIM + 16, band_rows), BF),
            pltpu.VMEM((keys, 2 * QB), F32),
            pltpu.VMEM((keys, 2 * QB), BF),
            pltpu.SemaphoreType.DMA((3 + blocks,)),
        ],
        compiler_params=params(),
        cost_estimate=pl.CostEstimate(flops=6_000_000_000, bytes_accessed=4_000_000, transcendentals=3_000_000),
        name="near",
    )(qkv, *pinned(win))


def far_kernel(reach, q_hbm, acc_hbm, top_hbm, win_hbm, mix_hbm, low_hbm, high_hbm, node_hbm, out_ref,
               q_ref, acc_ref, top_ref, win_ref, mix_ref, low_ref, high_ref,
               k_ref, v_ref, vt_ref, score_ref, prob_ref, node_ref, sem):
    band_rows = q_ref.shape[1]
    groups = band_rows // NODE_DEV
    first_node = lax.axis_index("band") * band_rows
    node_total = lax.axis_size("band") * band_rows
    copies = started(
        [
            pltpu.make_async_copy(source, target, sem.at[at])
            for at, (source, target) in enumerate(
                [(low_hbm, low_ref), (high_hbm, high_ref), (q_hbm, q_ref), (acc_hbm, acc_ref), (top_hbm, top_ref), (win_hbm, win_ref), (mix_hbm, mix_ref)]
            )
        ]
    )
    copies[0].wait()
    copies[1].wait()
    for side_at, half in enumerate((low_ref, high_ref)):
        for group in range(groups // 2):
            rows = pl.ds(side_at * reach + (group ^ 1) * NODE_DEV, NODE_DEV)
            k_ref[rows, :] = half[group, :, :LANES]
            v_ref[rows, :] = half[group, :, LANES:].astype(F32)
    vt = v_ref[...].T.astype(BF)
    for head in range(2):
        vt_ref[head, :HDIM, :] = vt[head * HDIM : (head + 1) * HDIM]
        vt_ref[head, HDIM:, :] = jnp.ones((16, 2 * reach), BF)
    for copy in copies[2:]:
        copy.wait()
    for block in range(band_rows // QB):
        start = block * QB
        both = jnp.concatenate([q_ref[0, start : start + QB, :], q_ref[1, start : start + QB, :]], axis=0)
        bottom, top = limits(win_ref[:, start : start + QB], reach, start, first_node, node_total)
        low_to = max(0, reach - start)
        high_from = min(QB + 2 * reach, band_rows + reach - start)
        pieces = [(at, start + at) for at in range(0, low_to, KC)]
        pieces += [(at, start + at - band_rows) for at in range(high_from, QB + 2 * reach, KC)]
        before = top_ref[block]
        largest = jnp.full((8, 2 * QB), NEG, F32)
        for row, (at, key) in enumerate(pieces):
            scores = masked(dot(k_ref[key : key + KC, :], both, 1, 1), at, reach, bottom, top)
            score_ref[row * KC : (row + 1) * KC, :] = scores
            largest = jnp.maximum(largest, fold(scores))
        largest = jnp.maximum(jnp.max(largest, axis=0, keepdims=True), before)
        decay = jnp.exp2(before - largest)
        for row in range(len(pieces)):
            prob_ref[row * KC : (row + 1) * KC, :] = jnp.exp2(score_ref[row * KC : (row + 1) * KC, :] - largest).astype(BF)
        low_rows, high_rows = low_to, QB + 2 * reach - high_from
        for head in range(2):
            cols = slice(head * QB, (head + 1) * QB)
            mixed = acc_ref[block, head] * decay[:, cols]
            if low_rows:
                mixed += dot(vt_ref[head, :, start:reach], prob_ref[:low_rows, cols], 1, 0)
            if high_rows:
                at = reach
                mixed += dot(vt_ref[head, :, at : at + high_rows], prob_ref[low_rows : low_rows + high_rows, cols], 1, 0)
            out_ref[head * HDIM : (head + 1) * HDIM, start : start + QB] = (
                mixed[:HDIM] / mixed[HDIM : HDIM + 1]
            ).astype(BF)
    node_ref[...] = dot(mix_ref[...], out_ref[...], 0, 0).T.astype(BF)
    rows = pl.ds(0, NODE_DEV)
    sends = started(
        [
            pltpu.make_async_copy(
                node_ref.at[pl.ds((group ^ 1) * NODE_DEV, NODE_DEV), :],
                node_hbm.at[group, rows, :],
                sem.at[len(copies) + group],
            )
            for group in range(groups)
        ]
    )
    for copy in sends:
        copy.wait()


def far(queries, acc, top, low, high, win, mix):
    band_rows = queries.shape[1]
    groups = band_rows // NODE_DEV
    reach = low.shape[0] * NODE_DEV
    held = (queries, acc, top, win, mix, low, high)
    return pl.pallas_call(
        functools.partial(far_kernel, reach),
        in_specs=[HBM] * 7,
        out_specs=(HBM, VMEM),
        out_shape=(
            in_hbm(shape((groups, NODE_DEV + 2 * ROWS, LANES), BF)),
            shape((LANES, band_rows), BF),
        ),
        scratch_shapes=[pltpu.VMEM(a.shape, a.dtype) for a in held]
        + [
            pltpu.VMEM((2 * reach, LANES), BF),
            pltpu.VMEM((2 * reach, LANES), F32),
            pltpu.VMEM((2, HDIM + 16, 2 * reach), BF),
            pltpu.VMEM((reach, 2 * QB), F32),
            pltpu.VMEM((reach, 2 * QB), BF),
            pltpu.VMEM((band_rows, LANES), BF),
            pltpu.SemaphoreType.DMA((len(held) + groups,)),
        ],
        compiler_params=params(),
        cost_estimate=pl.CostEstimate(flops=6_000_000_000, bytes_accessed=2_000_000, transcendentals=1_000_000),
        name="far",
    )(*pinned(*held))


def grads_kernel(out_ref, extra_ref, grad_ref):
    groups = extra_ref.shape[0]
    grad = jnp.zeros((LANES, LANES), F32)
    total = jnp.zeros((ROWS, LANES), F32)
    for group in range(groups):
        at = (group ^ 1) * NODE_DEV
        grad += dot(extra_ref[group, :NODE_DEV, :], out_ref[:, at : at + NODE_DEV], 0, 1)
        total += extra_ref[group, NODE_DEV:, :].astype(F32)
    grad_ref[:ROWS, :] = grad[:ROWS]
    grad_ref[ROWS:, :] = total


def grads(out, extra):
    return pl.pallas_call(
        grads_kernel,
        in_specs=[VMEM] * 2,
        out_specs=VMEM,
        out_shape=shape((2 * ROWS, LANES), F32),
        compiler_params=params(),
        name="grads",
    )(out, extra)


def table_kernel(parts_ref, node_ref, table_ref):
    total = node_ref[...]
    for group in range(parts_ref.shape[0]):
        total += parts_ref[group, :NODE_DEV, :].astype(F32)
    table_ref[...] = total.astype(BF)


def make_table(parts, node):
    return pl.pallas_call(
        table_kernel,
        in_specs=[VMEM] * 2,
        out_specs=VMEM,
        out_shape=shape(node.shape, BF),
        compiler_params=params(),
        name="make_table",
    )(parts, node)


def decode_kernel(far_ref, mid_ref, own_ref, dec_ref, grid_ref, pred_ref):
    channels, points = grid_ref.shape
    nodes = NODE_DEV
    rows = 4 * LANES
    table = jnp.concatenate(
        [
            far_ref[...].astype(F32),
            mid_ref[...].astype(F32),
            own_ref[...].astype(F32),
            jnp.zeros((rows - 3 * nodes, LANES), F32),
        ],
        axis=0,
    ).T.astype(BF)
    width = 512
    bases = chunk_bases()
    node_id = lax.broadcasted_iota(jnp.int32, (nodes, width), 0)
    for at in range(0, points, width):
        target = dec_ref[:, at : at + width]
        pick = [jnp.where(node_id == target - base, 1.0, 0.0) for base in bases]
        pick = jnp.concatenate(pick + [jnp.zeros((rows - 3 * nodes, width), F32)], axis=0).astype(BF)
        decoded = dot(table, pick, 1, 0)
        pred_ref[:, at : at + width] = (
            grid_ref[:, at : at + width].astype(F32) + decoded[:channels]
        ).astype(BF)


def decode(far_rows, mid_rows, own_rows, dec_row, grid_in):
    return pl.pallas_call(
        decode_kernel,
        in_specs=[VMEM] * 5,
        out_specs=VMEM,
        out_shape=shape(grid_in.shape, BF),
        compiler_params=params(),
        name="decode",
    )(far_rows, mid_rows, own_rows, dec_row, grid_in)


def spread_kernel(grad_ref, more_ref, parts_hbm, filled_hbm, sum_ref, sem):
    sum_ref[...] = (grad_ref[...].astype(F32) + more_ref[...].astype(F32)).astype(BF)
    rows = pl.ds(NODE_DEV, sum_ref.shape[0])
    copies = [
        pltpu.make_async_copy(sum_ref, filled_hbm.at[at, rows, :], sem.at[at]) for at in range(filled_hbm.shape[0])
    ]
    for copy in started(copies):
        copy.wait()


def spread(grad, more, parts):
    return pl.pallas_call(
        spread_kernel,
        in_specs=[VMEM, VMEM, HBM],
        out_specs=HBM,
        out_shape=in_hbm(parts),
        input_output_aliases={2: 0},
        scratch_shapes=[pltpu.VMEM(grad.shape, BF), pltpu.SemaphoreType.DMA((parts.shape[0],))],
        compiler_params=params(),
        name="spread",
    )(grad, more, *pinned(parts))


def gradient_kernel(parts_ref, w_out_ref, grad_ref):
    channels, model = grad_ref.shape
    mixed = jnp.zeros((ROWS, model), F32)
    for group in range(parts_ref.shape[0]):
        mixed += dot(parts_ref[group, NODE_DEV : NODE_DEV + ROWS, :], w_out_ref[group * LANES : (group + 1) * LANES, :], 1, 0)
    for group in range(parts_ref.shape[0]):
        cols = slice(group * LANES, (group + 1) * LANES)
        whole = mixed[:, cols] + parts_ref[group, NODE_DEV + ROWS :, :].astype(F32)
        grad_ref[:, cols] = whole[:channels]


def gradient(parts, w_out, channels):
    return pl.pallas_call(
        gradient_kernel,
        in_specs=[VMEM] * 2,
        out_specs=VMEM,
        out_shape=shape((channels, w_out.shape[0]), F32),
        compiler_params=params(),
        name="gradient",
    )(parts, w_out)


def total_devices():
    return lax.axis_size("band") * lax.axis_size("head")


def to_partner(block):
    return lax.ppermute(block, BOTH, [(i, i ^ 1) for i in range(total_devices())])


def two_over(block, sign):
    count = total_devices()
    pairs = [(i, i + sign * (2 - 4 * (i % 2))) for i in range(count)]
    return lax.ppermute(block, BOTH, [(i, j) for i, j in pairs if 0 <= j < count])


def along_band(block, shift):
    count = lax.axis_size("band")
    return lax.ppermute(block, "band", [(i, i + shift) for i in range(count) if 0 <= i + shift < count])


def flipped(block, axis, bit):
    return lax.ppermute(block, axis, [(i, i ^ (1 << bit)) for i in range(lax.axis_size(axis))])


def swap(block):
    return lax.all_to_all(block, "head", split_axis=0, concat_axis=0, tiled=True)


def shards(
    grid_in, enc_node, dec_node, win_offsets, w_in, b_in, w_qkv, w_out, norm_gain, w_dec, cotangent
):
    channels = grid_in.shape[0]
    groups = lax.axis_size("head")
    dec_row = dec_node[None]
    far_part, mid_part, own = encode(grid_in, enc_node[None], w_in, b_in[None], cotangent, dec_row)
    weights, dec_pad, mix = load(w_qkv, w_out, w_dec.T, far_part)
    mid_in = to_partner(mid_part)
    far_in = two_over(far_part, -1)
    packed, enc, summed = project(own, mid_in, far_in, norm_gain[None], weights)
    qkv = swap(packed)
    send, node = side(enc, summed, dec_pad)
    qkv, send, node = lax.optimization_barrier((qkv, send, node))
    half = groups // 2
    reach = half * NODE_DEV
    from_low = along_band(qkv[half:, :, LANES:], 1)
    from_high = along_band(qkv[:half, :, LANES:], -1)
    extra = swap(send)
    acc, top, queries = near(qkv, win_offsets, reach)
    parts, attended = far(queries, acc, top, from_low, from_high, win_offsets, mix)
    grad = grads(attended, extra)
    grad = (grad + flipped(grad, "band", 0)).astype(BF)
    for bit in (1, 2, 3):
        grad = (grad.astype(F32) + flipped(grad, "band", bit).astype(F32)).astype(BF)
    parts = swap(spread(grad, flipped(grad, "band", 4), parts))
    table = make_table(parts, node)
    prediction = decode(two_over(table, 1), to_partner(table), table, dec_row, grid_in)
    grad_dec = gradient(parts, w_out, channels).T
    return (prediction, grad_dec)


def solution(mesh):
    placed = (
        P(None, BOTH),
        P(BOTH),
        P(BOTH),
        P(None, "band"),
        P(),
        P(),
        P(),
        P(),
        P(),
        P(),
        P(None, BOTH),
    )
    return jax.shard_map(
        shards,
        mesh=mesh,
        in_specs=placed,
        out_specs=(P(None, BOTH), P()),
        check_vma=False,
    )
```

```python
import functools

import jax
import jax.numpy as jnp
from jax import lax
from jax.experimental import pallas as pl
from jax.experimental.pallas import tpu as pltpu
from jax.sharding import PartitionSpec as P

HDIM = 64
NODE_DEV = 160
BOTH = ("band", "head")
LANES = 128
QB = 256
KC = 128
ROWS = 112
EXTRA = 16
BF = jnp.bfloat16
F32 = jnp.float32
LOG2E = 1.4426950408889634
NEG = -1e30
HBM = pl.BlockSpec(memory_space=pltpu.HBM)
VMEM = pl.BlockSpec(memory_space=pltpu.VMEM)


def params(mib=24):
    return pltpu.CompilerParams(vmem_limit_bytes=mib * 1024 * 1024)


def dot(a, b, ca, cb):
    return lax.dot_general(a, b, (((ca,), (cb,)), ((), ())), preferred_element_type=F32)


def shape(dims, dtype):
    return jax.ShapeDtypeStruct(dims, dtype)


def in_hbm(a):
    return pltpu.HBM(a.shape, a.dtype)


def pinned(*arrays):
    return tuple(pltpu.with_memory_space_constraint(a, pltpu.HBM) for a in arrays)


def started(copies):
    for copy in copies:
        copy.start()
    return copies


def chunk_bases():
    index = lax.axis_index("band") * lax.axis_size("head") + lax.axis_index("head")
    side = 1 - 2 * lax.rem(index, 2)
    return (index - side) * NODE_DEV, index * NODE_DEV, (index + side) * NODE_DEV


def encode_kernel(grid_hbm, enc_hbm, w_hbm, b_hbm, cot_hbm, dec_hbm, far_ref, mid_ref, own_ref,
                  grid_ref, enc_ref, w_ref, b_ref, cot_ref, dec_ref, rows_ref, w_pad, cot_pad, pick_ref, sem):
    channels, points = grid_ref.shape
    model = w_ref.shape[1]
    nodes = NODE_DEV
    copies = started(
        [
            pltpu.make_async_copy(source, target, sem.at[at])
            for at, (source, target) in enumerate(
                [(grid_hbm, grid_ref), (enc_hbm, enc_ref), (w_hbm, w_ref), (b_hbm, b_ref), (cot_hbm, cot_ref), (dec_hbm, dec_ref)]
            )
        ]
    )
    bases = chunk_bases()
    node_id = lax.broadcasted_iota(jnp.int32, (nodes, points), 0)

    def pick(target):
        for at, base in enumerate(bases):
            pick_ref[at * nodes : (at + 1) * nodes, :] = jnp.where(node_id == target - base, 1.0, 0.0).astype(BF)

    copies[1].wait()
    pick(enc_ref[...])
    copies[0].wait()
    padded = jnp.concatenate(
        [grid_ref[...].astype(F32), jnp.zeros((LANES - channels, points), F32)], axis=0
    )
    rows_ref[...] = padded.T.astype(BF)
    copies[2].wait()
    copies[3].wait()
    w_pad[...] = jnp.zeros_like(w_pad)
    w_pad[:channels, :] = (w_ref[...].astype(F32) * 0.5).astype(BF)
    width = 256
    for at in range(0, model, width):
        half = dot(rows_ref[...], w_pad[:, at : at + width], 1, 0) + b_ref[:, at : at + width] * 0.5
        message = (half + half * jnp.tanh(half)).astype(BF)
        spread = dot(pick_ref[...], message, 1, 0)
        far_ref[:, at : at + width] = spread[:nodes].astype(BF)
        mid_ref[:nodes, at : at + width] = spread[nodes : 2 * nodes].astype(BF)
        own_ref[:, at : at + width] = spread[2 * nodes :]
    copies[4].wait()
    copies[5].wait()
    cot_pad[...] = jnp.zeros_like(cot_pad)
    cot_pad[:channels, :] = cot_ref[...]
    pick(dec_ref[...])
    spread = dot(pick_ref[...], cot_pad[...], 1, 1)
    far_ref[:, model:] = spread[:nodes].astype(BF)
    mid_ref[nodes:, :] = jnp.zeros((EXTRA, mid_ref.shape[1]), BF)
    mid_ref[:nodes, model:] = spread[nodes : 2 * nodes].astype(BF)
    own_ref[:, model:] = spread[2 * nodes :]


def encode(grid_in, enc_row, w_in, b_row, cotangent, dec_row):
    channels, points = grid_in.shape
    model = w_in.shape[1]
    wide = model + LANES
    operands = (grid_in, enc_row, w_in, b_row, cotangent, dec_row)
    return pl.pallas_call(
        encode_kernel,
        in_specs=[HBM] * 6,
        out_specs=(VMEM,) * 3,
        out_shape=(shape((NODE_DEV, wide), BF), shape((NODE_DEV + EXTRA, wide), BF), shape((NODE_DEV, wide), F32)),
        scratch_shapes=[pltpu.VMEM(a.shape, a.dtype) for a in operands]
        + [
            pltpu.VMEM((points, LANES), BF),
            pltpu.VMEM((LANES, model), BF),
            pltpu.VMEM((LANES, points), BF),
            pltpu.VMEM((3 * NODE_DEV, points), BF),
            pltpu.SemaphoreType.DMA((6,)),
        ],
        compiler_params=params(),
        name="encode",
    )(*pinned(*operands))


def load_kernel(w_hbm, out_hbm, dec_hbm, after_ref, w_ref, dec_ref, mix_hbm, mix_ref, out_rows, dec_rows, sem):
    channels = dec_rows.shape[0]
    at = pl.multiple_of(lax.axis_index("head") * LANES, LANES)
    copies = started(
        [
            pltpu.make_async_copy(out_hbm.at[pl.ds(at, LANES), :], out_rows, sem.at[0]),
            pltpu.make_async_copy(dec_hbm, dec_rows, sem.at[1]),
            pltpu.make_async_copy(w_hbm, w_ref, sem.at[2]),
        ]
    )
    copies[0].wait()
    copies[1].wait()
    dec_ref[...] = jnp.zeros_like(dec_ref)
    dec_ref[:channels, :] = dec_rows[...]
    mix_ref[...] = dot(out_rows[...], dec_ref[...], 1, 1).astype(BF)
    copy = pltpu.make_async_copy(mix_ref, mix_hbm, sem.at[3])
    copy.start()
    copy.wait()
    copies[2].wait()


def load(w_qkv, w_out, dec_cols, after):
    model = w_qkv.shape[0]
    return pl.pallas_call(
        load_kernel,
        in_specs=[HBM] * 3 + [pl.BlockSpec(memory_space=pl.ANY)],
        out_specs=(VMEM, VMEM, HBM),
        out_shape=(shape(w_qkv.shape, BF), shape((LANES, model), BF), in_hbm(shape((LANES, LANES), BF))),
        scratch_shapes=[
            pltpu.VMEM((LANES, LANES), BF),
            pltpu.VMEM((LANES, model), BF),
            pltpu.VMEM(dec_cols.shape, BF),
            pltpu.SemaphoreType.DMA((4,)),
        ],
        compiler_params=params(),
        cost_estimate=pl.CostEstimate(flops=2 * model * LANES * LANES, bytes_accessed=2 * w_qkv.size, transcendentals=0),
        name="load",
    )(*pinned(w_qkv, w_out, dec_cols), after)


def project_kernel(own_ref, mid_ref, far_ref, gain_ref, w_ref, packed_hbm, enc_ref, s_ref, packed, sem):
    model = gain_ref.shape[1]
    total = own_ref[...] + mid_ref[:NODE_DEV].astype(F32) + far_ref[...].astype(F32)
    enc = total[:, :model]
    s_ref[...] = total[:, model:].astype(BF)
    enc_ref[...] = enc
    centred = enc - jnp.mean(enc, axis=1, keepdims=True)
    spread_sq = jnp.mean(centred * centred, axis=1, keepdims=True)
    normed = (centred * lax.rsqrt(spread_sq + 1e-05) * gain_ref[...]).astype(BF)
    scale = HDIM ** (-0.5) * LOG2E
    copies = []
    for pair in range(model // (2 * LANES)):
        for part in range(3):
            at = part * model + pair * 2 * LANES
            cols = dot(normed, w_ref[:, at : at + 2 * LANES], 1, 0)
            if part == 0:
                cols = cols * scale
            cols = cols.astype(BF)
            for half in range(2):
                packed[2 * pair + half, :, part * LANES : (part + 1) * LANES] = cols[:, half * LANES : (half + 1) * LANES]
        rows = pl.ds(2 * pair, 2)
        copies += started([pltpu.make_async_copy(packed.at[rows], packed_hbm.at[rows], sem.at[pair])])
    for copy in copies:
        copy.wait()


def project(own, mid, far, gain_row, w_qkv):
    model = w_qkv.shape[0]
    groups = model // LANES
    return pl.pallas_call(
        project_kernel,
        in_specs=[VMEM] * 5,
        out_specs=(HBM, VMEM, VMEM),
        out_shape=(
            in_hbm(shape((groups, NODE_DEV, 3 * LANES), BF)),
            shape((NODE_DEV, model), F32),
            shape((NODE_DEV, LANES), BF),
        ),
        scratch_shapes=[
            pltpu.VMEM((groups, NODE_DEV, 3 * LANES), BF),
            pltpu.SemaphoreType.DMA((groups // 2,)),
        ],
        compiler_params=params(),
        name="project",
    )(own, mid, far, gain_row, w_qkv)


def side_kernel(enc_ref, s_ref, dec_ref, send_hbm, node_ref, send, sem):
    groups = send.shape[0]
    enc = enc_ref[...]
    summed = s_ref[...]
    high = enc.astype(BF)
    low = (enc - high.astype(F32)).astype(BF)
    node_ref[...] = dot(high, dec_ref[...], 1, 1)
    grad = (dot(summed, high, 0, 0) + dot(summed, low, 0, 0)).astype(BF)
    for group in range(groups):
        send[group, :NODE_DEV, :] = summed
        send[group, NODE_DEV:, :] = grad[:ROWS, group * LANES : (group + 1) * LANES]
    copy = pltpu.make_async_copy(send, send_hbm, sem)
    copy.start()
    copy.wait()


def side(enc, summed, dec_pad):
    groups = enc.shape[1] // LANES
    send_shape = (groups, NODE_DEV + ROWS, LANES)
    return pl.pallas_call(
        side_kernel,
        in_specs=[VMEM] * 3,
        out_specs=(HBM, VMEM),
        out_shape=(in_hbm(shape(send_shape, BF)), shape((NODE_DEV, LANES), F32)),
        scratch_shapes=[pltpu.VMEM(send_shape, BF), pltpu.SemaphoreType.DMA],
        compiler_params=params(),
        name="side",
    )(enc, summed, dec_pad)


def limits(win, reach, start, first_node, node_total):
    column = lax.broadcasted_iota(jnp.int32, (1, QB), 1) + reach
    bottom = jnp.maximum(column - win[0:1], reach - start - first_node)
    top = jnp.minimum(column + win[1:2], reach - start - first_node + node_total - 1)
    return jnp.concatenate([bottom, bottom], axis=1), jnp.concatenate([top, top], axis=1)


def masked(scores, at, reach, bottom, top):
    key = lax.broadcasted_iota(jnp.int32, scores.shape, 0) + at
    if at + KC - 1 <= reach:
        keep = key >= bottom
    elif at >= reach + QB - 1:
        keep = key <= top
    else:
        keep = (key >= bottom) & (key <= top)
    return jnp.where(keep, scores, NEG)


def fold(scores):
    return jnp.max(scores.reshape(KC // 8, 8, 2 * QB), axis=0)


def near_kernel(reach, qkv_ref, win_hbm, acc_hbm, top_hbm, q_hbm,
                win_ref, acc_ref, top_ref, q_ref, k_ref, v_ref, vt_ref, score_ref, prob_ref, sem):
    groups = qkv_ref.shape[0]
    win_copy = pltpu.make_async_copy(win_hbm, win_ref, sem.at[0])
    win_copy.start()
    band_rows = groups * NODE_DEV
    first_node = lax.axis_index("band") * band_rows
    node_total = lax.axis_size("band") * band_rows
    lane = lax.broadcasted_iota(jnp.int32, (NODE_DEV, LANES), 1)
    zero = jnp.zeros((NODE_DEV, LANES), BF)
    for group in range(groups):
        rows = pl.ds((group ^ 1) * NODE_DEV, NODE_DEV)
        queries = qkv_ref[group, :, :LANES]
        q_ref[0, rows, :] = jnp.where(lane < HDIM, queries, zero)
        q_ref[1, rows, :] = jnp.where(lane >= HDIM, queries, zero)
        k_ref[rows, :] = qkv_ref[group, :, LANES : 2 * LANES]
        v_ref[rows, :] = qkv_ref[group, :, 2 * LANES :].astype(F32)
    vt = v_ref[...].T.astype(BF)
    for head in range(2):
        vt_ref[head, :HDIM, :] = vt[head * HDIM : (head + 1) * HDIM]
        vt_ref[head, HDIM:, :] = jnp.ones((16, band_rows), BF)
    copies = started([pltpu.make_async_copy(q_ref, q_hbm, sem.at[1])])
    win_copy.wait()
    for block in range(band_rows // QB):
        start = block * QB
        both = jnp.concatenate([q_ref[0, start : start + QB, :], q_ref[1, start : start + QB, :]], axis=0)
        bottom, top = limits(win_ref[:, start : start + QB], reach, start, first_node, node_total)
        first = max(0, reach - start)
        last = min(QB + 2 * reach, band_rows + reach - start)
        largest = jnp.full((8, 2 * QB), NEG, F32)
        for at in range(first, last, KC):
            key = start + at - reach
            scores = masked(dot(k_ref[key : key + KC, :], both, 1, 1), at, reach, bottom, top)
            score_ref[at - first : at - first + KC, :] = scores
            largest = jnp.maximum(largest, fold(scores))
        largest = jnp.max(largest, axis=0, keepdims=True)
        top_ref[block] = largest
        for at in range(0, last - first, KC):
            prob_ref[at : at + KC, :] = jnp.exp2(score_ref[at : at + KC, :] - largest).astype(BF)
        key = start + first - reach
        for head in range(2):
            acc_ref[block, head] = dot(
                vt_ref[head, :, key : key + last - first],
                prob_ref[: last - first, head * QB : (head + 1) * QB],
                1,
                0,
            )
        copies += started([pltpu.make_async_copy(acc_ref.at[block], acc_hbm.at[block], sem.at[3 + block])])
    copies += started([pltpu.make_async_copy(top_ref, top_hbm, sem.at[2])])
    for copy in copies:
        copy.wait()


def near(qkv, win, reach):
    groups = qkv.shape[0]
    band_rows = groups * NODE_DEV
    blocks = band_rows // QB
    keys = min(QB + 2 * reach, band_rows)
    outs = (
        shape((blocks, 2, HDIM + 16, QB), F32),
        shape((blocks, 1, 2 * QB), F32),
        shape((2, band_rows, LANES), BF),
    )
    return pl.pallas_call(
        functools.partial(near_kernel, reach),
        in_specs=[VMEM, HBM],
        out_specs=(HBM,) * 3,
        out_shape=tuple(in_hbm(a) for a in outs),
        scratch_shapes=[
            pltpu.VMEM(win.shape, win.dtype),
            *[pltpu.VMEM(a.shape, a.dtype) for a in outs],
            pltpu.VMEM((band_rows, LANES), BF),
            pltpu.VMEM((band_rows, LANES), F32),
            pltpu.VMEM((2, HDIM + 16, band_rows), BF),
            pltpu.VMEM((keys, 2 * QB), F32),
            pltpu.VMEM((keys, 2 * QB), BF),
            pltpu.SemaphoreType.DMA((3 + blocks,)),
        ],
        compiler_params=params(),
        cost_estimate=pl.CostEstimate(flops=6_000_000_000, bytes_accessed=4_000_000, transcendentals=3_000_000),
        name="near",
    )(qkv, *pinned(win))


def far_kernel(reach, q_hbm, acc_hbm, top_hbm, win_hbm, mix_hbm, chip_hbm, off_hbm, node_hbm, out_ref,
               q_ref, acc_ref, top_ref, win_ref, mix_ref, chip_ref, off_ref,
               k_ref, v_ref, vt_ref, score_ref, prob_ref, node_ref, sem):
    band_rows = q_ref.shape[1]
    groups = band_rows // NODE_DEV
    first_node = lax.axis_index("band") * band_rows
    node_total = lax.axis_size("band") * band_rows
    copies = started(
        [
            pltpu.make_async_copy(source, target, sem.at[at])
            for at, (source, target) in enumerate(
                [(chip_hbm, chip_ref), (off_hbm, off_ref), (q_hbm, q_ref), (acc_hbm, acc_ref), (top_hbm, top_ref), (win_hbm, win_ref), (mix_hbm, mix_ref)]
            )
        ]
    )
    core = lax.rem(lax.axis_index("band"), 2)
    copies[0].wait()
    copies[1].wait()
    for base, half in (((1 - core) * reach, chip_ref), (core * reach, off_ref)):
        for group in range(groups // 2):
            rows = pl.ds(pl.multiple_of(base + (group ^ 1) * NODE_DEV, NODE_DEV), NODE_DEV)
            k_ref[rows, :] = half[group, :, :LANES]
            v_ref[rows, :] = half[group, :, LANES:].astype(F32)
    vt = v_ref[...].T.astype(BF)
    for head in range(2):
        vt_ref[head, :HDIM, :] = vt[head * HDIM : (head + 1) * HDIM]
        vt_ref[head, HDIM:, :] = jnp.ones((16, 2 * reach), BF)
    for copy in copies[2:]:
        copy.wait()
    for block in range(band_rows // QB):
        start = block * QB
        both = jnp.concatenate([q_ref[0, start : start + QB, :], q_ref[1, start : start + QB, :]], axis=0)
        bottom, top = limits(win_ref[:, start : start + QB], reach, start, first_node, node_total)
        low_to = max(0, reach - start)
        high_from = min(QB + 2 * reach, band_rows + reach - start)
        pieces = [(at, start + at) for at in range(0, low_to, KC)]
        pieces += [(at, start + at - band_rows) for at in range(high_from, QB + 2 * reach, KC)]
        before = top_ref[block]
        largest = jnp.full((8, 2 * QB), NEG, F32)
        for row, (at, key) in enumerate(pieces):
            scores = masked(dot(k_ref[key : key + KC, :], both, 1, 1), at, reach, bottom, top)
            score_ref[row * KC : (row + 1) * KC, :] = scores
            largest = jnp.maximum(largest, fold(scores))
        largest = jnp.maximum(jnp.max(largest, axis=0, keepdims=True), before)
        decay = jnp.exp2(before - largest)
        for row in range(len(pieces)):
            prob_ref[row * KC : (row + 1) * KC, :] = jnp.exp2(score_ref[row * KC : (row + 1) * KC, :] - largest).astype(BF)
        low_rows, high_rows = low_to, QB + 2 * reach - high_from
        for head in range(2):
            cols = slice(head * QB, (head + 1) * QB)
            mixed = acc_ref[block, head] * decay[:, cols]
            if low_rows:
                mixed += dot(vt_ref[head, :, start:reach], prob_ref[:low_rows, cols], 1, 0)
            if high_rows:
                at = reach
                mixed += dot(vt_ref[head, :, at : at + high_rows], prob_ref[low_rows : low_rows + high_rows, cols], 1, 0)
            out_ref[head * HDIM : (head + 1) * HDIM, start : start + QB] = (
                mixed[:HDIM] / mixed[HDIM : HDIM + 1]
            ).astype(BF)
    node_ref[...] = dot(mix_ref[...], out_ref[...], 0, 0).T.astype(BF)
    rows = pl.ds(0, NODE_DEV)
    sends = started(
        [
            pltpu.make_async_copy(
                node_ref.at[pl.ds((group ^ 1) * NODE_DEV, NODE_DEV), :],
                node_hbm.at[group, rows, :],
                sem.at[len(copies) + group],
            )
            for group in range(groups)
        ]
    )
    for copy in sends:
        copy.wait()


def far(queries, acc, top, on_chip, off_chip, win, mix):
    band_rows = queries.shape[1]
    groups = band_rows // NODE_DEV
    reach = on_chip.shape[0] * NODE_DEV
    held = (queries, acc, top, win, mix, on_chip, off_chip)
    return pl.pallas_call(
        functools.partial(far_kernel, reach),
        in_specs=[HBM] * 7,
        out_specs=(HBM, VMEM),
        out_shape=(
            in_hbm(shape((groups, NODE_DEV + ROWS, LANES), BF)),
            shape((LANES, band_rows), BF),
        ),
        scratch_shapes=[pltpu.VMEM(a.shape, a.dtype) for a in held]
        + [
            pltpu.VMEM((2 * reach, LANES), BF),
            pltpu.VMEM((2 * reach, LANES), F32),
            pltpu.VMEM((2, HDIM + 16, 2 * reach), BF),
            pltpu.VMEM((reach, 2 * QB), F32),
            pltpu.VMEM((reach, 2 * QB), BF),
            pltpu.VMEM((band_rows, LANES), BF),
            pltpu.SemaphoreType.DMA((len(held) + groups,)),
        ],
        compiler_params=params(),
        cost_estimate=pl.CostEstimate(flops=6_000_000_000, bytes_accessed=2_000_000, transcendentals=1_000_000),
        name="far",
    )(*pinned(*held))


def grads_kernel(out_ref, extra_ref, keep_ref, give_ref):
    groups = extra_ref.shape[0]
    grad = jnp.zeros((LANES, LANES), F32)
    total = jnp.zeros((ROWS, LANES), F32)
    for group in range(groups):
        at = (group ^ 1) * NODE_DEV
        grad += dot(extra_ref[group, :NODE_DEV, :], out_ref[:, at : at + NODE_DEV], 0, 1)
        total += extra_ref[group, NODE_DEV:, :].astype(F32)
    first = lax.rem(lax.axis_index("band"), 2) == 0
    keep_ref[...] = jnp.where(first, grad[:ROWS], total)
    give_ref[...] = jnp.where(first, total, grad[:ROWS])


def grads(out, extra):
    half = shape((ROWS, LANES), F32)
    return pl.pallas_call(
        grads_kernel,
        in_specs=[VMEM] * 2,
        out_specs=(VMEM,) * 2,
        out_shape=(half, half),
        compiler_params=params(),
        name="grads",
    )(out, extra)


def table_kernel(parts_ref, node_ref, table_ref):
    total = node_ref[...]
    for group in range(parts_ref.shape[0]):
        total += parts_ref[group, :NODE_DEV, :].astype(F32)
    table_ref[...] = total.astype(BF)


def make_table(parts, node):
    return pl.pallas_call(
        table_kernel,
        in_specs=[VMEM] * 2,
        out_specs=VMEM,
        out_shape=shape(node.shape, BF),
        compiler_params=params(),
        name="make_table",
    )(parts, node)


def decode_kernel(mid_ref, far_ref, own_ref, dec_ref, grid_ref, pred_ref):
    channels, points = grid_ref.shape
    nodes = NODE_DEV
    rows = 4 * LANES
    table = jnp.concatenate(
        [
            far_ref[...].astype(F32),
            mid_ref[...].astype(F32),
            own_ref[...].astype(F32),
            jnp.zeros((rows - 3 * nodes, LANES), F32),
        ],
        axis=0,
    ).T.astype(BF)
    width = 512
    bases = chunk_bases()
    node_id = lax.broadcasted_iota(jnp.int32, (nodes, width), 0)
    for at in range(0, points, width):
        target = dec_ref[:, at : at + width]
        pick = [jnp.where(node_id == target - base, 1.0, 0.0) for base in bases]
        pick = jnp.concatenate(pick + [jnp.zeros((rows - 3 * nodes, width), F32)], axis=0).astype(BF)
        decoded = dot(table, pick, 1, 0)
        pred_ref[:, at : at + width] = (
            grid_ref[:, at : at + width].astype(F32) + decoded[:channels]
        ).astype(BF)


def decode(far_rows, mid_rows, own_rows, dec_row, grid_in):
    return pl.pallas_call(
        decode_kernel,
        in_specs=[VMEM] * 5,
        out_specs=VMEM,
        out_shape=shape(grid_in.shape, BF),
        compiler_params=params(),
        name="decode",
    )(mid_rows, far_rows, own_rows, dec_row, grid_in)


def spread_kernel(grad_ref, more_ref, parts_hbm, filled_hbm, sum_ref, sem):
    sum_ref[...] = (grad_ref[...].astype(F32) + more_ref[...].astype(F32)).astype(BF)
    rows = pl.ds(NODE_DEV, sum_ref.shape[0])
    copies = [
        pltpu.make_async_copy(sum_ref, filled_hbm.at[at, rows, :], sem.at[at]) for at in range(filled_hbm.shape[0])
    ]
    for copy in started(copies):
        copy.wait()


def spread(grad, more, parts):
    return pl.pallas_call(
        spread_kernel,
        in_specs=[VMEM, VMEM, HBM],
        out_specs=HBM,
        out_shape=in_hbm(parts),
        input_output_aliases={2: 0},
        scratch_shapes=[pltpu.VMEM(grad.shape, BF), pltpu.SemaphoreType.DMA((parts.shape[0],))],
        compiler_params=params(),
        name="spread",
    )(grad, more, *pinned(parts))


def half_kernel(parts_ref, w_out_ref, half_ref):
    first = lax.rem(lax.axis_index("band"), 2) == 0
    groups = parts_ref.shape[0]

    @pl.when(first)
    def _():
        mixed = jnp.zeros(half_ref.shape, F32)
        for group in range(groups):
            rows = w_out_ref[group * LANES : (group + 1) * LANES, :]
            mixed += dot(parts_ref[group, NODE_DEV:, :], rows, 1, 0)
        half_ref[...] = mixed

    @pl.when(jnp.logical_not(first))
    def _():
        for group in range(groups):
            half_ref[:, group * LANES : (group + 1) * LANES] = parts_ref[group, NODE_DEV:, :].astype(F32)


def gradient_half(parts, w_out):
    return pl.pallas_call(
        half_kernel,
        in_specs=[VMEM] * 2,
        out_specs=VMEM,
        out_shape=shape((ROWS, w_out.shape[1]), F32),
        compiler_params=params(),
        name="gradient_half",
    )(parts, w_out)


def add_kernel(mine_ref, other_ref, out_ref):
    channels = out_ref.shape[0]
    out_ref[...] = mine_ref[:channels] + other_ref[:channels]


def add(mine, other, channels):
    return pl.pallas_call(
        add_kernel,
        in_specs=[VMEM] * 2,
        out_specs=VMEM,
        out_shape=shape((channels, mine.shape[1]), F32),
        compiler_params=params(),
        name="add",
    )(mine, other)


def total_devices():
    return lax.axis_size("band") * lax.axis_size("head")


def to_partner(block):
    return lax.ppermute(block, BOTH, [(i, i ^ 1) for i in range(total_devices())])


def two_over(block, sign):
    count = total_devices()
    pairs = [(i, i + sign * (2 - 4 * (i % 2))) for i in range(count)]
    return lax.ppermute(block, BOTH, [(i, j) for i, j in pairs if 0 <= j < count])


def next_chip(block):
    count = lax.axis_size("band")
    pairs = [(i, i - 1 + 2 * (i % 2)) for i in range(count)]
    return lax.ppermute(block, "band", [(i, j) for i, j in pairs if 0 <= j < count])


def flipped(block, axis, bit):
    return lax.ppermute(block, axis, [(i, i ^ (1 << bit)) for i in range(lax.axis_size(axis))])


def across(block):
    planes = lax.axis_size("band") // 4
    other = [(z + 6) % planes if z % 4 < 2 else (z + 2) % planes for z in range(planes)]
    return lax.ppermute(block, "band", [(i, other[i // 4] * 4 + i % 4) for i in range(planes * 4)])


def swap(block):
    return lax.all_to_all(block, "head", split_axis=0, concat_axis=0, tiled=True)


def shards(
    grid_in, enc_node, dec_node, win_offsets, w_in, b_in, w_qkv, w_out, norm_gain, w_dec, cotangent
):
    channels = grid_in.shape[0]
    groups = lax.axis_size("head")
    dec_row = dec_node[None]
    far_part, mid_part, own = encode(grid_in, enc_node[None], w_in, b_in[None], cotangent, dec_row)
    weights, dec_pad, mix = load(w_qkv, w_out, w_dec.T, far_part)
    mid_in = to_partner(mid_part)
    far_in = two_over(far_part, -1)
    packed, enc, summed = project(own, mid_in, far_in, norm_gain[None], weights)
    qkv = swap(packed)
    send, node = side(enc, summed, dec_pad)
    qkv, send, node = lax.optimization_barrier((qkv, send, node))
    half = groups // 2
    reach = half * NODE_DEV
    core = lax.rem(lax.axis_index("band"), 2)
    kv = qkv[:, :, LANES:]
    on_chip = flipped(lax.dynamic_slice_in_dim(kv, (1 - core) * half, half, 0), "band", 0)
    off_chip = next_chip(lax.dynamic_slice_in_dim(kv, core * half, half, 0))
    extra = swap(send)
    acc, top, queries = near(qkv, win_offsets, reach)
    parts, attended = far(queries, acc, top, on_chip, off_chip, win_offsets, mix)
    grad, give = grads(attended, extra)
    grad = (grad + flipped(give, "band", 0)).astype(BF)
    for bit in (1, 2, 3):
        grad = (grad.astype(F32) + flipped(grad, "band", bit).astype(F32)).astype(BF)
    parts = swap(spread(grad, across(grad), parts))
    table = make_table(parts, node)
    half_grad = gradient_half(parts, w_out)
    prediction = decode(two_over(table, 1), to_partner(table), table, dec_row, grid_in)
    grad_dec = add(half_grad, flipped(half_grad, "band", 0), channels)
    return (prediction, grad_dec.T)


def solution(mesh):
    placed = (
        P(None, BOTH),
        P(BOTH),
        P(BOTH),
        P(None, "band"),
        P(),
        P(),
        P(),
        P(),
        P(),
        P(),
        P(None, BOTH),
    )
    return jax.shard_map(
        shards,
        mesh=mesh,
        in_specs=placed,
        out_specs=(P(None, BOTH), P()),
        check_vma=False,
    )
```

```python
import functools

import jax
import jax.numpy as jnp
from jax import lax
from jax.experimental import pallas as pl
from jax.experimental.pallas import tpu as pltpu
from jax.sharding import PartitionSpec as P

HDIM = 64
NODE_DEV = 160
BOTH = ("band", "head")
LANES = 128
QB = 256
KC = 128
ROWS = 112
EXTRA = 16
BF = jnp.bfloat16
F32 = jnp.float32
LOG2E = 1.4426950408889634
NEG = -1e30
HBM = pl.BlockSpec(memory_space=pltpu.HBM)
VMEM = pl.BlockSpec(memory_space=pltpu.VMEM)


def params(mib=24):
    return pltpu.CompilerParams(vmem_limit_bytes=mib * 1024 * 1024)


def dot(a, b, ca, cb):
    return lax.dot_general(a, b, (((ca,), (cb,)), ((), ())), preferred_element_type=F32)


def shape(dims, dtype):
    return jax.ShapeDtypeStruct(dims, dtype)


def in_hbm(a):
    return pltpu.HBM(a.shape, a.dtype)


def pinned(*arrays):
    return tuple(pltpu.with_memory_space_constraint(a, pltpu.HBM) for a in arrays)


def started(copies):
    for copy in copies:
        copy.start()
    return copies


def chunk_bases():
    index = lax.axis_index("band") * lax.axis_size("head") + lax.axis_index("head")
    side = 1 - 2 * lax.rem(index, 2)
    return (index - side) * NODE_DEV, index * NODE_DEV, (index + side) * NODE_DEV


def fill_pick(pick_ref, target):
    nodes, points = NODE_DEV, pick_ref.shape[1]
    node_id = lax.broadcasted_iota(jnp.int32, (nodes, points), 0)
    for at, base in enumerate(chunk_bases()):
        pick_ref[at * nodes : (at + 1) * nodes, :] = jnp.where(node_id == target - base, 1.0, 0.0).astype(BF)


def encode_kernel(grid_hbm, enc_hbm, w_hbm, b_hbm, far_ref, mid_ref, own_ref,
                  grid_ref, enc_ref, w_ref, b_ref, w_half, pick_ref, sem):
    model = w_ref.shape[1]
    nodes = NODE_DEV
    copies = started(
        [
            pltpu.make_async_copy(source, target, sem.at[at])
            for at, (source, target) in enumerate(
                [(grid_hbm, grid_ref), (enc_hbm, enc_ref), (w_hbm, w_ref), (b_hbm, b_ref)]
            )
        ]
    )
    copies[1].wait()
    fill_pick(pick_ref, enc_ref[...])
    copies[2].wait()
    w_half[...] = (w_ref[...].astype(F32) * 0.5).astype(BF)
    copies[0].wait()
    copies[3].wait()
    width = 512
    mid_ref[nodes:, :] = jnp.zeros((EXTRA, model), BF)
    for at in range(0, model, width):
        half = dot(grid_ref[...], w_half[:, at : at + width], 0, 0) + b_ref[:, at : at + width] * 0.5
        message = (half + half * jnp.tanh(half)).astype(BF)
        spread = dot(pick_ref[...], message, 1, 0)
        far_ref[:, at : at + width] = spread[:nodes].astype(BF)
        mid_ref[:nodes, at : at + width] = spread[nodes : 2 * nodes].astype(BF)
        own_ref[:, at : at + width] = spread[2 * nodes :]


def encode(grid_in, enc_row, w_in, b_row):
    points = grid_in.shape[1]
    model = w_in.shape[1]
    operands = (grid_in, enc_row, w_in, b_row)
    return pl.pallas_call(
        encode_kernel,
        in_specs=[HBM] * 4,
        out_specs=(VMEM,) * 3,
        out_shape=(shape((NODE_DEV, model), BF), shape((NODE_DEV + EXTRA, model), BF), shape((NODE_DEV, model), F32)),
        scratch_shapes=[pltpu.VMEM(a.shape, a.dtype) for a in operands]
        + [
            pltpu.VMEM(w_in.shape, BF),
            pltpu.VMEM((3 * NODE_DEV, points), BF),
            pltpu.SemaphoreType.DMA((4,)),
        ],
        compiler_params=params(),
        name="encode",
    )(*pinned(*operands))


def prepare_kernel(w_hbm, out_hbm, dec_hbm, cot_hbm, target_hbm, after_ref,
                   w_ref, pad_ref, mix_hbm, far_ref, mid_ref, own_ref,
                   mix_ref, out_rows, dec_rows, cot_ref, target_ref, cot_pad, pick_ref, sem):
    channels = dec_rows.shape[0]
    nodes = NODE_DEV
    at = pl.multiple_of(lax.axis_index("head") * LANES, LANES)
    copies = started(
        [
            pltpu.make_async_copy(source, target, sem.at[number])
            for number, (source, target) in enumerate(
                [
                    (target_hbm, target_ref),
                    (cot_hbm, cot_ref),
                    (dec_hbm, dec_rows),
                    (out_hbm.at[pl.ds(at, LANES), :], out_rows),
                    (w_hbm, w_ref),
                ]
            )
        ]
    )
    copies[0].wait()
    fill_pick(pick_ref, target_ref[...])
    copies[1].wait()
    cot_pad[...] = jnp.zeros_like(cot_pad)
    cot_pad[:channels, :] = cot_ref[...]
    spread = dot(pick_ref[...], cot_pad[...], 1, 1)
    far_ref[...] = spread[:nodes].astype(BF)
    mid_ref[...] = spread[nodes : 2 * nodes].astype(BF)
    own_ref[...] = spread[2 * nodes :]
    copies[2].wait()
    pad_ref[...] = jnp.zeros_like(pad_ref)
    pad_ref[:channels, :] = dec_rows[...]
    copies[3].wait()
    mix_ref[...] = dot(out_rows[...], pad_ref[...], 1, 1).astype(BF)
    copy = pltpu.make_async_copy(mix_ref, mix_hbm, sem.at[len(copies)])
    copy.start()
    copy.wait()
    copies[4].wait()


def prepare(w_qkv, w_out, dec_cols, cotangent, dec_row, after):
    model = w_qkv.shape[0]
    points = cotangent.shape[1]
    part = (NODE_DEV, LANES)
    return pl.pallas_call(
        prepare_kernel,
        in_specs=[HBM] * 5 + [pl.BlockSpec(memory_space=pl.ANY)],
        out_specs=(VMEM, VMEM, HBM, VMEM, VMEM, VMEM),
        out_shape=(
            shape(w_qkv.shape, BF),
            shape((LANES, model), BF),
            in_hbm(shape((LANES, LANES), BF)),
            shape(part, BF),
            shape(part, BF),
            shape(part, F32),
        ),
        scratch_shapes=[
            pltpu.VMEM((LANES, LANES), BF),
            pltpu.VMEM((LANES, model), BF),
            pltpu.VMEM(dec_cols.shape, BF),
            pltpu.VMEM(cotangent.shape, BF),
            pltpu.VMEM(dec_row.shape, jnp.int32),
            pltpu.VMEM((LANES, points), BF),
            pltpu.VMEM((3 * NODE_DEV, points), BF),
            pltpu.SemaphoreType.DMA((6,)),
        ],
        compiler_params=params(),
        cost_estimate=pl.CostEstimate(flops=500_000_000, bytes_accessed=2 * w_qkv.size, transcendentals=0),
        name="prepare",
    )(*pinned(w_qkv, w_out, dec_cols, cotangent, dec_row), after)


def project_kernel(own_ref, mid_ref, far_ref, gain_ref, w_ref, packed_hbm, enc_ref, packed, sem):
    model = gain_ref.shape[1]
    enc = own_ref[...] + mid_ref[:NODE_DEV].astype(F32) + far_ref[...].astype(F32)
    enc_ref[...] = enc
    centred = enc - jnp.mean(enc, axis=1, keepdims=True)
    spread_sq = jnp.mean(centred * centred, axis=1, keepdims=True)
    normed = (centred * lax.rsqrt(spread_sq + 1e-05) * gain_ref[...]).astype(BF)
    scale = HDIM ** (-0.5) * LOG2E
    copies = []
    for pair in range(model // (2 * LANES)):
        for part in range(3):
            at = part * model + pair * 2 * LANES
            cols = dot(normed, w_ref[:, at : at + 2 * LANES], 1, 0)
            if part == 0:
                cols = cols * scale
            cols = cols.astype(BF)
            for half in range(2):
                packed[2 * pair + half, :, part * LANES : (part + 1) * LANES] = cols[:, half * LANES : (half + 1) * LANES]
        rows = pl.ds(2 * pair, 2)
        copies += started([pltpu.make_async_copy(packed.at[rows], packed_hbm.at[rows], sem.at[pair])])
    for copy in copies:
        copy.wait()


def project(own, mid, far, gain_row, w_qkv):
    model = w_qkv.shape[0]
    groups = model // LANES
    return pl.pallas_call(
        project_kernel,
        in_specs=[VMEM] * 5,
        out_specs=(HBM, VMEM),
        out_shape=(
            in_hbm(shape((groups, NODE_DEV, 3 * LANES), BF)),
            shape((NODE_DEV, model), F32),
        ),
        scratch_shapes=[
            pltpu.VMEM((groups, NODE_DEV, 3 * LANES), BF),
            pltpu.SemaphoreType.DMA((groups // 2,)),
        ],
        compiler_params=params(),
        name="project",
    )(own, mid, far, gain_row, w_qkv)


def side_kernel(enc_ref, own_ref, mid_ref, far_ref, dec_ref, send_hbm, node_ref, send, sem):
    groups = send.shape[0]
    enc = enc_ref[...]
    summed = (own_ref[...] + mid_ref[...].astype(F32) + far_ref[...].astype(F32)).astype(BF)
    high = enc.astype(BF)
    low = (enc - high.astype(F32)).astype(BF)
    node_ref[...] = dot(high, dec_ref[...], 1, 1)
    grad = (dot(summed, high, 0, 0) + dot(summed, low, 0, 0)).astype(BF)
    for group in range(groups):
        send[group, :NODE_DEV, :] = summed
        send[group, NODE_DEV:, :] = grad[:ROWS, group * LANES : (group + 1) * LANES]
    copy = pltpu.make_async_copy(send, send_hbm, sem)
    copy.start()
    copy.wait()


def side(enc, own, mid, far, dec_pad):
    groups = enc.shape[1] // LANES
    send_shape = (groups, NODE_DEV + ROWS, LANES)
    return pl.pallas_call(
        side_kernel,
        in_specs=[VMEM] * 5,
        out_specs=(HBM, VMEM),
        out_shape=(in_hbm(shape(send_shape, BF)), shape((NODE_DEV, LANES), F32)),
        scratch_shapes=[pltpu.VMEM(send_shape, BF), pltpu.SemaphoreType.DMA],
        compiler_params=params(),
        name="side",
    )(enc, own, mid, far, dec_pad)


def limits(win, reach, start, first_node, node_total):
    column = lax.broadcasted_iota(jnp.int32, (1, QB), 1) + reach
    bottom = jnp.maximum(column - win[0:1], reach - start - first_node)
    top = jnp.minimum(column + win[1:2], reach - start - first_node + node_total - 1)
    return jnp.concatenate([bottom, bottom], axis=1), jnp.concatenate([top, top], axis=1)


def masked(scores, at, reach, bottom, top):
    key = lax.broadcasted_iota(jnp.int32, scores.shape, 0) + at
    if at + KC - 1 <= reach:
        keep = key >= bottom
    elif at >= reach + QB - 1:
        keep = key <= top
    else:
        keep = (key >= bottom) & (key <= top)
    return jnp.where(keep, scores, NEG)


def fold(scores):
    return jnp.max(scores.reshape(KC // 8, 8, 2 * QB), axis=0)


def near_kernel(reach, qkv_ref, win_hbm, acc_hbm, top_hbm, q_hbm,
                win_ref, acc_ref, top_ref, q_ref, k_ref, v_ref, vt_ref, score_ref, prob_ref, sem):
    groups = qkv_ref.shape[0]
    win_copy = pltpu.make_async_copy(win_hbm, win_ref, sem.at[0])
    win_copy.start()
    band_rows = groups * NODE_DEV
    first_node = lax.axis_index("band") * band_rows
    node_total = lax.axis_size("band") * band_rows
    lane = lax.broadcasted_iota(jnp.int32, (NODE_DEV, LANES), 1)
    zero = jnp.zeros((NODE_DEV, LANES), BF)
    for group in range(groups):
        rows = pl.ds((group ^ 1) * NODE_DEV, NODE_DEV)
        queries = qkv_ref[group, :, :LANES]
        q_ref[0, rows, :] = jnp.where(lane < HDIM, queries, zero)
        q_ref[1, rows, :] = jnp.where(lane >= HDIM, queries, zero)
        k_ref[rows, :] = qkv_ref[group, :, LANES : 2 * LANES]
        v_ref[rows, :] = qkv_ref[group, :, 2 * LANES :].astype(F32)
    vt = v_ref[...].T.astype(BF)
    for head in range(2):
        vt_ref[head, :HDIM, :] = vt[head * HDIM : (head + 1) * HDIM]
        vt_ref[head, HDIM:, :] = jnp.ones((16, band_rows), BF)
    copies = started([pltpu.make_async_copy(q_ref, q_hbm, sem.at[1])])
    win_copy.wait()
    for block in range(band_rows // QB):
        start = block * QB
        both = jnp.concatenate([q_ref[0, start : start + QB, :], q_ref[1, start : start + QB, :]], axis=0)
        bottom, top = limits(win_ref[:, start : start + QB], reach, start, first_node, node_total)
        first = max(0, reach - start)
        last = min(QB + 2 * reach, band_rows + reach - start)
        largest = jnp.full((8, 2 * QB), NEG, F32)
        for at in range(first, last, KC):
            key = start + at - reach
            scores = masked(dot(k_ref[key : key + KC, :], both, 1, 1), at, reach, bottom, top)
            score_ref[at - first : at - first + KC, :] = scores
            largest = jnp.maximum(largest, fold(scores))
        largest = jnp.max(largest, axis=0, keepdims=True)
        top_ref[block] = largest
        for at in range(0, last - first, KC):
            prob_ref[at : at + KC, :] = jnp.exp2(score_ref[at : at + KC, :] - largest).astype(BF)
        key = start + first - reach
        for head in range(2):
            acc_ref[block, head] = dot(
                vt_ref[head, :, key : key + last - first],
                prob_ref[: last - first, head * QB : (head + 1) * QB],
                1,
                0,
            )
        copies += started([pltpu.make_async_copy(acc_ref.at[block], acc_hbm.at[block], sem.at[3 + block])])
    copies += started([pltpu.make_async_copy(top_ref, top_hbm, sem.at[2])])
    for copy in copies:
        copy.wait()


def near(qkv, win, reach):
    groups = qkv.shape[0]
    band_rows = groups * NODE_DEV
    blocks = band_rows // QB
    keys = min(QB + 2 * reach, band_rows)
    outs = (
        shape((blocks, 2, HDIM + 16, QB), F32),
        shape((blocks, 1, 2 * QB), F32),
        shape((2, band_rows, LANES), BF),
    )
    return pl.pallas_call(
        functools.partial(near_kernel, reach),
        in_specs=[VMEM, HBM],
        out_specs=(HBM,) * 3,
        out_shape=tuple(in_hbm(a) for a in outs),
        scratch_shapes=[
            pltpu.VMEM(win.shape, win.dtype),
            *[pltpu.VMEM(a.shape, a.dtype) for a in outs],
            pltpu.VMEM((band_rows, LANES), BF),
            pltpu.VMEM((band_rows, LANES), F32),
            pltpu.VMEM((2, HDIM + 16, band_rows), BF),
            pltpu.VMEM((keys, 2 * QB), F32),
            pltpu.VMEM((keys, 2 * QB), BF),
            pltpu.SemaphoreType.DMA((3 + blocks,)),
        ],
        compiler_params=params(),
        cost_estimate=pl.CostEstimate(flops=6_000_000_000, bytes_accessed=4_000_000, transcendentals=3_000_000),
        name="near",
    )(qkv, *pinned(win))


def far_kernel(reach, q_hbm, acc_hbm, top_hbm, win_hbm, mix_hbm, chip_hbm, off_hbm, node_hbm, out_ref,
               q_ref, acc_ref, top_ref, win_ref, mix_ref, chip_ref, off_ref,
               k_ref, v_ref, vt_ref, score_ref, prob_ref, node_ref, sem):
    band_rows = q_ref.shape[1]
    groups = band_rows // NODE_DEV
    first_node = lax.axis_index("band") * band_rows
    node_total = lax.axis_size("band") * band_rows
    copies = started(
        [
            pltpu.make_async_copy(source, target, sem.at[at])
            for at, (source, target) in enumerate(
                [(chip_hbm, chip_ref), (off_hbm, off_ref), (q_hbm, q_ref), (acc_hbm, acc_ref), (top_hbm, top_ref), (win_hbm, win_ref), (mix_hbm, mix_ref)]
            )
        ]
    )
    core = lax.rem(lax.axis_index("band"), 2)
    copies[0].wait()
    copies[1].wait()
    for base, half in (((1 - core) * reach, chip_ref), (core * reach, off_ref)):
        for group in range(groups // 2):
            rows = pl.ds(pl.multiple_of(base + (group ^ 1) * NODE_DEV, NODE_DEV), NODE_DEV)
            k_ref[rows, :] = half[group, :, :LANES]
            v_ref[rows, :] = half[group, :, LANES:].astype(F32)
    vt = v_ref[...].T.astype(BF)
    for head in range(2):
        vt_ref[head, :HDIM, :] = vt[head * HDIM : (head + 1) * HDIM]
        vt_ref[head, HDIM:, :] = jnp.ones((16, 2 * reach), BF)
    for copy in copies[2:]:
        copy.wait()
    for block in range(band_rows // QB):
        start = block * QB
        both = jnp.concatenate([q_ref[0, start : start + QB, :], q_ref[1, start : start + QB, :]], axis=0)
        bottom, top = limits(win_ref[:, start : start + QB], reach, start, first_node, node_total)
        low_to = max(0, reach - start)
        high_from = min(QB + 2 * reach, band_rows + reach - start)
        pieces = [(at, start + at) for at in range(0, low_to, KC)]
        pieces += [(at, start + at - band_rows) for at in range(high_from, QB + 2 * reach, KC)]
        before = top_ref[block]
        largest = jnp.full((8, 2 * QB), NEG, F32)
        for row, (at, key) in enumerate(pieces):
            scores = masked(dot(k_ref[key : key + KC, :], both, 1, 1), at, reach, bottom, top)
            score_ref[row * KC : (row + 1) * KC, :] = scores
            largest = jnp.maximum(largest, fold(scores))
        largest = jnp.maximum(jnp.max(largest, axis=0, keepdims=True), before)
        decay = jnp.exp2(before - largest)
        for row in range(len(pieces)):
            prob_ref[row * KC : (row + 1) * KC, :] = jnp.exp2(score_ref[row * KC : (row + 1) * KC, :] - largest).astype(BF)
        low_rows, high_rows = low_to, QB + 2 * reach - high_from
        for head in range(2):
            cols = slice(head * QB, (head + 1) * QB)
            mixed = acc_ref[block, head] * decay[:, cols]
            if low_rows:
                mixed += dot(vt_ref[head, :, start:reach], prob_ref[:low_rows, cols], 1, 0)
            if high_rows:
                at = reach
                mixed += dot(vt_ref[head, :, at : at + high_rows], prob_ref[low_rows : low_rows + high_rows, cols], 1, 0)
            out_ref[head * HDIM : (head + 1) * HDIM, start : start + QB] = (
                mixed[:HDIM] / mixed[HDIM : HDIM + 1]
            ).astype(BF)
    node_ref[...] = dot(mix_ref[...], out_ref[...], 0, 0).T.astype(BF)
    rows = pl.ds(0, NODE_DEV)
    sends = started(
        [
            pltpu.make_async_copy(
                node_ref.at[pl.ds((group ^ 1) * NODE_DEV, NODE_DEV), :],
                node_hbm.at[group, rows, :],
                sem.at[len(copies) + group],
            )
            for group in range(groups)
        ]
    )
    for copy in sends:
        copy.wait()


def far(queries, acc, top, on_chip, off_chip, win, mix):
    band_rows = queries.shape[1]
    groups = band_rows // NODE_DEV
    reach = on_chip.shape[0] * NODE_DEV
    held = (queries, acc, top, win, mix, on_chip, off_chip)
    return pl.pallas_call(
        functools.partial(far_kernel, reach),
        in_specs=[HBM] * 7,
        out_specs=(HBM, VMEM),
        out_shape=(
            in_hbm(shape((groups, NODE_DEV + ROWS, LANES), BF)),
            shape((LANES, band_rows), BF),
        ),
        scratch_shapes=[pltpu.VMEM(a.shape, a.dtype) for a in held]
        + [
            pltpu.VMEM((2 * reach, LANES), BF),
            pltpu.VMEM((2 * reach, LANES), F32),
            pltpu.VMEM((2, HDIM + 16, 2 * reach), BF),
            pltpu.VMEM((reach, 2 * QB), F32),
            pltpu.VMEM((reach, 2 * QB), BF),
            pltpu.VMEM((band_rows, LANES), BF),
            pltpu.SemaphoreType.DMA((len(held) + groups,)),
        ],
        compiler_params=params(),
        cost_estimate=pl.CostEstimate(flops=6_000_000_000, bytes_accessed=2_000_000, transcendentals=1_000_000),
        name="far",
    )(*pinned(*held))


def grads_kernel(out_ref, extra_ref, keep_ref, give_ref):
    groups = extra_ref.shape[0]
    grad = jnp.zeros((LANES, LANES), F32)
    total = jnp.zeros((ROWS, LANES), F32)
    for group in range(groups):
        at = (group ^ 1) * NODE_DEV
        grad += dot(extra_ref[group, :NODE_DEV, :], out_ref[:, at : at + NODE_DEV], 0, 1)
        total += extra_ref[group, NODE_DEV:, :].astype(F32)
    first = lax.rem(lax.axis_index("band"), 2) == 0
    keep_ref[...] = jnp.where(first, grad[:ROWS], total)
    give_ref[...] = jnp.where(first, total, grad[:ROWS])


def grads(out, extra):
    half = shape((ROWS, LANES), F32)
    return pl.pallas_call(
        grads_kernel,
        in_specs=[VMEM] * 2,
        out_specs=(VMEM,) * 2,
        out_shape=(half, half),
        compiler_params=params(),
        name="grads",
    )(out, extra)


def table_kernel(parts_ref, node_ref, table_ref):
    total = node_ref[...]
    for group in range(parts_ref.shape[0]):
        total += parts_ref[group, :NODE_DEV, :].astype(F32)
    table_ref[...] = total.astype(BF)


def make_table(parts, node):
    return pl.pallas_call(
        table_kernel,
        in_specs=[VMEM] * 2,
        out_specs=VMEM,
        out_shape=shape(node.shape, BF),
        compiler_params=params(),
        name="make_table",
    )(parts, node)


def decode_kernel(mid_ref, far_ref, own_ref, dec_ref, grid_ref, pred_ref):
    channels, points = grid_ref.shape
    nodes = NODE_DEV
    rows = 4 * LANES
    table = jnp.concatenate(
        [
            far_ref[...].astype(F32),
            mid_ref[...].astype(F32),
            own_ref[...].astype(F32),
            jnp.zeros((rows - 3 * nodes, LANES), F32),
        ],
        axis=0,
    ).T.astype(BF)
    width = 512
    bases = chunk_bases()
    node_id = lax.broadcasted_iota(jnp.int32, (nodes, width), 0)
    for at in range(0, points, width):
        target = dec_ref[:, at : at + width]
        pick = [jnp.where(node_id == target - base, 1.0, 0.0) for base in bases]
        pick = jnp.concatenate(pick + [jnp.zeros((rows - 3 * nodes, width), F32)], axis=0).astype(BF)
        decoded = dot(table, pick, 1, 0)
        pred_ref[:, at : at + width] = (
            grid_ref[:, at : at + width].astype(F32) + decoded[:channels]
        ).astype(BF)


def decode(far_rows, mid_rows, own_rows, dec_row, grid_in):
    return pl.pallas_call(
        decode_kernel,
        in_specs=[VMEM] * 5,
        out_specs=VMEM,
        out_shape=shape(grid_in.shape, BF),
        compiler_params=params(),
        name="decode",
    )(mid_rows, far_rows, own_rows, dec_row, grid_in)


def spread_kernel(grad_ref, more_ref, parts_hbm, filled_hbm, sum_ref, sem):
    sum_ref[...] = (grad_ref[...].astype(F32) + more_ref[...].astype(F32)).astype(BF)
    rows = pl.ds(NODE_DEV, sum_ref.shape[0])
    copies = [
        pltpu.make_async_copy(sum_ref, filled_hbm.at[at, rows, :], sem.at[at]) for at in range(filled_hbm.shape[0])
    ]
    for copy in started(copies):
        copy.wait()


def spread(grad, more, parts):
    return pl.pallas_call(
        spread_kernel,
        in_specs=[VMEM, VMEM, HBM],
        out_specs=HBM,
        out_shape=in_hbm(parts),
        input_output_aliases={2: 0},
        scratch_shapes=[pltpu.VMEM(grad.shape, BF), pltpu.SemaphoreType.DMA((parts.shape[0],))],
        compiler_params=params(),
        name="spread",
    )(grad, more, *pinned(parts))


def half_kernel(parts_ref, w_out_ref, half_ref):
    first = lax.rem(lax.axis_index("band"), 2) == 0
    groups = parts_ref.shape[0]

    @pl.when(first)
    def _():
        mixed = jnp.zeros(half_ref.shape, F32)
        for group in range(groups):
            rows = w_out_ref[group * LANES : (group + 1) * LANES, :]
            mixed += dot(parts_ref[group, NODE_DEV:, :], rows, 1, 0)
        half_ref[...] = mixed

    @pl.when(jnp.logical_not(first))
    def _():
        for group in range(groups):
            half_ref[:, group * LANES : (group + 1) * LANES] = parts_ref[group, NODE_DEV:, :].astype(F32)


def gradient_half(parts, w_out):
    return pl.pallas_call(
        half_kernel,
        in_specs=[VMEM] * 2,
        out_specs=VMEM,
        out_shape=shape((ROWS, w_out.shape[1]), F32),
        compiler_params=params(),
        name="gradient_half",
    )(parts, w_out)


def add_kernel(mine_ref, other_ref, out_ref):
    channels = out_ref.shape[0]
    out_ref[...] = mine_ref[:channels] + other_ref[:channels]


def add(mine, other, channels):
    return pl.pallas_call(
        add_kernel,
        in_specs=[VMEM] * 2,
        out_specs=VMEM,
        out_shape=shape((channels, mine.shape[1]), F32),
        compiler_params=params(),
        name="add",
    )(mine, other)


def total_devices():
    return lax.axis_size("band") * lax.axis_size("head")


def to_partner(block):
    return lax.ppermute(block, BOTH, [(i, i ^ 1) for i in range(total_devices())])


def two_over(block, sign):
    count = total_devices()
    pairs = [(i, i + sign * (2 - 4 * (i % 2))) for i in range(count)]
    return lax.ppermute(block, BOTH, [(i, j) for i, j in pairs if 0 <= j < count])


def next_chip(block):
    count = lax.axis_size("band")
    pairs = [(i, i - 1 + 2 * (i % 2)) for i in range(count)]
    return lax.ppermute(block, "band", [(i, j) for i, j in pairs if 0 <= j < count])


def flipped(block, axis, bit):
    return lax.ppermute(block, axis, [(i, i ^ (1 << bit)) for i in range(lax.axis_size(axis))])


def across(block):
    planes = lax.axis_size("band") // 4
    other = [(z + 6) % planes if z % 4 < 2 else (z + 2) % planes for z in range(planes)]
    return lax.ppermute(block, "band", [(i, other[i // 4] * 4 + i % 4) for i in range(planes * 4)])


def swap(block):
    return lax.all_to_all(block, "head", split_axis=0, concat_axis=0, tiled=True)


def shards(
    grid_in, enc_node, dec_node, win_offsets, w_in, b_in, w_qkv, w_out, norm_gain, w_dec, cotangent
):
    channels = grid_in.shape[0]
    groups = lax.axis_size("head")
    dec_row = dec_node[None]
    far_part, mid_part, own = encode(grid_in, enc_node[None], w_in, b_in[None])
    weights, dec_pad, mix, far_sum, mid_sum, own_sum = prepare(
        w_qkv, w_out, w_dec.T, cotangent, dec_row, far_part
    )
    mid_in = to_partner(mid_part)
    far_in = two_over(far_part, -1)
    mid_sum = to_partner(mid_sum)
    far_sum = two_over(far_sum, -1)
    packed, enc = project(own, mid_in, far_in, norm_gain[None], weights)
    packed, mid_sum, far_sum = lax.optimization_barrier((packed, mid_sum, far_sum))
    qkv = swap(packed)
    send, node = side(enc, own_sum, mid_sum, far_sum, dec_pad)
    qkv, send, node = lax.optimization_barrier((qkv, send, node))
    half = groups // 2
    reach = half * NODE_DEV
    core = lax.rem(lax.axis_index("band"), 2)
    kv = qkv[:, :, LANES:]
    on_chip = flipped(lax.dynamic_slice_in_dim(kv, (1 - core) * half, half, 0), "band", 0)
    off_chip = next_chip(lax.dynamic_slice_in_dim(kv, core * half, half, 0))
    extra = swap(send)
    acc, top, queries = near(qkv, win_offsets, reach)
    parts, attended = far(queries, acc, top, on_chip, off_chip, win_offsets, mix)
    grad, give = grads(attended, extra)
    grad = (grad + flipped(give, "band", 0)).astype(BF)
    for bit in (1, 2, 3):
        grad = (grad.astype(F32) + flipped(grad, "band", bit).astype(F32)).astype(BF)
    parts = swap(spread(grad, across(grad), parts))
    table = make_table(parts, node)
    half_grad = gradient_half(parts, w_out)
    grad_dec = add(half_grad, flipped(half_grad, "band", 0), channels)
    grad_dec, mid_rows = lax.optimization_barrier((grad_dec, to_partner(table)))
    prediction = decode(two_over(table, 1), mid_rows, table, dec_row, grid_in)
    return (prediction, grad_dec.T)


def solution(mesh):
    placed = (
        P(None, BOTH),
        P(BOTH),
        P(BOTH),
        P(None, "band"),
        P(),
        P(),
        P(),
        P(),
        P(),
        P(),
        P(None, BOTH),
    )
    return jax.shard_map(
        shards,
        mesh=mesh,
        in_specs=placed,
        out_specs=(P(None, BOTH), P()),
        check_vma=False,
    )
```

```python
import functools

import jax
import jax.numpy as jnp
from jax import lax
from jax.experimental import pallas as pl
from jax.experimental.pallas import tpu as pltpu
from jax.sharding import PartitionSpec as P

HDIM = 64
NODE_DEV = 160
BOTH = ("band", "head")
LANES = 128
QB = 256
KC = 128
ROWS = 112
EXTRA = 16
BF = jnp.bfloat16
F32 = jnp.float32
LOG2E = 1.4426950408889634
NEG = -1e30
HBM = pl.BlockSpec(memory_space=pltpu.HBM)
VMEM = pl.BlockSpec(memory_space=pltpu.VMEM)


def params(mib=24):
    return pltpu.CompilerParams(vmem_limit_bytes=mib * 1024 * 1024)


def dot(a, b, ca, cb):
    return lax.dot_general(a, b, (((ca,), (cb,)), ((), ())), preferred_element_type=F32)


def shape(dims, dtype):
    return jax.ShapeDtypeStruct(dims, dtype)


def in_hbm(a):
    return pltpu.HBM(a.shape, a.dtype)


def pinned(*arrays):
    return tuple(pltpu.with_memory_space_constraint(a, pltpu.HBM) for a in arrays)


def started(copies):
    for copy in copies:
        copy.start()
    return copies


def chunk_bases():
    index = lax.axis_index("band") * lax.axis_size("head") + lax.axis_index("head")
    side = 1 - 2 * lax.rem(index, 2)
    return (index - side) * NODE_DEV, index * NODE_DEV, (index + side) * NODE_DEV


def fill_pick(pick_ref, target):
    nodes, points = NODE_DEV, pick_ref.shape[1]
    node_id = lax.broadcasted_iota(jnp.int32, (nodes, points), 0)
    for at, base in enumerate(chunk_bases()):
        pick_ref[at * nodes : (at + 1) * nodes, :] = jnp.where(node_id == target - base, 1.0, 0.0).astype(BF)


def encode_kernel(grid_hbm, enc_hbm, w_hbm, b_hbm, far_ref, mid_ref, own_ref,
                  grid_ref, enc_ref, w_ref, b_ref, w_half, pick_ref, sem):
    model = w_ref.shape[1]
    nodes = NODE_DEV
    copies = started(
        [
            pltpu.make_async_copy(source, target, sem.at[at])
            for at, (source, target) in enumerate(
                [(grid_hbm, grid_ref), (enc_hbm, enc_ref), (w_hbm, w_ref), (b_hbm, b_ref)]
            )
        ]
    )
    copies[1].wait()
    fill_pick(pick_ref, enc_ref[...])
    copies[2].wait()
    w_half[...] = (w_ref[...].astype(F32) * 0.5).astype(BF)
    copies[0].wait()
    copies[3].wait()
    width = 512
    mid_ref[nodes:, :] = jnp.zeros((EXTRA, model), BF)
    for at in range(0, model, width):
        half = dot(grid_ref[...], w_half[:, at : at + width], 0, 0) + b_ref[:, at : at + width] * 0.5
        message = (half + half * jnp.tanh(half)).astype(BF)
        spread = dot(pick_ref[...], message, 1, 0)
        far_ref[:, at : at + width] = spread[:nodes].astype(BF)
        mid_ref[:nodes, at : at + width] = spread[nodes : 2 * nodes].astype(BF)
        own_ref[:, at : at + width] = spread[2 * nodes :]


def encode(grid_in, enc_row, w_in, b_row):
    points = grid_in.shape[1]
    model = w_in.shape[1]
    operands = (grid_in, enc_row, w_in, b_row)
    return pl.pallas_call(
        encode_kernel,
        in_specs=[HBM] * 4,
        out_specs=(VMEM,) * 3,
        out_shape=(shape((NODE_DEV, model), BF), shape((NODE_DEV + EXTRA, model), BF), shape((NODE_DEV, model), F32)),
        scratch_shapes=[pltpu.VMEM(a.shape, a.dtype) for a in operands]
        + [
            pltpu.VMEM(w_in.shape, BF),
            pltpu.VMEM((3 * NODE_DEV, points), BF),
            pltpu.SemaphoreType.DMA((4,)),
        ],
        compiler_params=params(),
        name="encode",
    )(*pinned(*operands))


def prepare_kernel(w_hbm, out_hbm, dec_hbm, cot_hbm, target_hbm, after_ref,
                   w_ref, pad_ref, mix_hbm, far_ref, mid_ref, own_ref,
                   mix_ref, out_rows, dec_rows, cot_ref, target_ref, cot_pad, pick_ref, sem):
    channels = dec_rows.shape[0]
    nodes = NODE_DEV
    at = pl.multiple_of(lax.axis_index("head") * LANES, LANES)
    copies = started(
        [
            pltpu.make_async_copy(source, target, sem.at[number])
            for number, (source, target) in enumerate(
                [
                    (target_hbm, target_ref),
                    (cot_hbm, cot_ref),
                    (dec_hbm, dec_rows),
                    (out_hbm.at[pl.ds(at, LANES), :], out_rows),
                    (w_hbm, w_ref),
                ]
            )
        ]
    )
    copies[0].wait()
    fill_pick(pick_ref, target_ref[...])
    copies[1].wait()
    cot_pad[...] = jnp.zeros_like(cot_pad)
    cot_pad[:channels, :] = cot_ref[...]
    spread = dot(pick_ref[...], cot_pad[...], 1, 1)
    far_ref[...] = spread[:nodes].astype(BF)
    mid_ref[...] = spread[nodes : 2 * nodes].astype(BF)
    own_ref[...] = spread[2 * nodes :]
    copies[2].wait()
    pad_ref[...] = jnp.zeros_like(pad_ref)
    pad_ref[:channels, :] = dec_rows[...]
    copies[3].wait()
    mix_ref[...] = dot(out_rows[...], pad_ref[...], 1, 1).astype(BF)
    copy = pltpu.make_async_copy(mix_ref, mix_hbm, sem.at[len(copies)])
    copy.start()
    copy.wait()
    copies[4].wait()


def prepare(w_qkv, w_out, dec_cols, cotangent, dec_row, after):
    model = w_qkv.shape[0]
    points = cotangent.shape[1]
    part = (NODE_DEV, LANES)
    return pl.pallas_call(
        prepare_kernel,
        in_specs=[HBM] * 5 + [pl.BlockSpec(memory_space=pl.ANY)],
        out_specs=(VMEM, VMEM, HBM, VMEM, VMEM, VMEM),
        out_shape=(
            shape(w_qkv.shape, BF),
            shape((LANES, model), BF),
            in_hbm(shape((LANES, LANES), BF)),
            shape(part, BF),
            shape(part, BF),
            shape(part, F32),
        ),
        scratch_shapes=[
            pltpu.VMEM((LANES, LANES), BF),
            pltpu.VMEM((LANES, model), BF),
            pltpu.VMEM(dec_cols.shape, BF),
            pltpu.VMEM(cotangent.shape, BF),
            pltpu.VMEM(dec_row.shape, jnp.int32),
            pltpu.VMEM((LANES, points), BF),
            pltpu.VMEM((3 * NODE_DEV, points), BF),
            pltpu.SemaphoreType.DMA((6,)),
        ],
        compiler_params=params(),
        cost_estimate=pl.CostEstimate(flops=500_000_000, bytes_accessed=2 * w_qkv.size, transcendentals=0),
        name="prepare",
    )(*pinned(w_qkv, w_out, dec_cols, cotangent, dec_row), after)


def project_kernel(own_ref, mid_ref, far_ref, gain_ref, w_ref, packed_hbm, enc_ref, packed, sem):
    model = gain_ref.shape[1]
    enc = own_ref[...] + mid_ref[:NODE_DEV].astype(F32) + far_ref[...].astype(F32)
    enc_ref[...] = enc
    centred = enc - jnp.mean(enc, axis=1, keepdims=True)
    spread_sq = jnp.mean(centred * centred, axis=1, keepdims=True)
    normed = (centred * lax.rsqrt(spread_sq + 1e-05) * gain_ref[...]).astype(BF)
    scale = HDIM ** (-0.5) * LOG2E
    copies = []
    for pair in range(model // (2 * LANES)):
        for part in range(3):
            at = part * model + pair * 2 * LANES
            cols = dot(normed, w_ref[:, at : at + 2 * LANES], 1, 0)
            if part == 0:
                cols = cols * scale
            cols = cols.astype(BF)
            for half in range(2):
                packed[2 * pair + half, :, part * LANES : (part + 1) * LANES] = cols[:, half * LANES : (half + 1) * LANES]
        rows = pl.ds(2 * pair, 2)
        copies += started([pltpu.make_async_copy(packed.at[rows], packed_hbm.at[rows], sem.at[pair])])
    for copy in copies:
        copy.wait()


def project(own, mid, far, gain_row, w_qkv):
    model = w_qkv.shape[0]
    groups = model // LANES
    return pl.pallas_call(
        project_kernel,
        in_specs=[VMEM] * 5,
        out_specs=(HBM, VMEM),
        out_shape=(
            in_hbm(shape((groups, NODE_DEV, 3 * LANES), BF)),
            shape((NODE_DEV, model), F32),
        ),
        scratch_shapes=[
            pltpu.VMEM((groups, NODE_DEV, 3 * LANES), BF),
            pltpu.SemaphoreType.DMA((groups // 2,)),
        ],
        compiler_params=params(),
        name="project",
    )(own, mid, far, gain_row, w_qkv)


def side_kernel(enc_ref, own_ref, mid_ref, far_ref, dec_ref, send_hbm, node_ref, send, sem):
    groups = send.shape[0]
    enc = enc_ref[...]
    summed = (own_ref[...] + mid_ref[...].astype(F32) + far_ref[...].astype(F32)).astype(BF)
    high = enc.astype(BF)
    low = (enc - high.astype(F32)).astype(BF)
    node_ref[...] = dot(high, dec_ref[...], 1, 1)
    grad = (dot(summed, high, 0, 0) + dot(summed, low, 0, 0)).astype(BF)
    for group in range(groups):
        send[group, :NODE_DEV, :] = summed
        send[group, NODE_DEV:, :] = grad[:ROWS, group * LANES : (group + 1) * LANES]
    copy = pltpu.make_async_copy(send, send_hbm, sem)
    copy.start()
    copy.wait()


def side(enc, own, mid, far, dec_pad):
    groups = enc.shape[1] // LANES
    send_shape = (groups, NODE_DEV + ROWS, LANES)
    return pl.pallas_call(
        side_kernel,
        in_specs=[VMEM] * 5,
        out_specs=(HBM, VMEM),
        out_shape=(in_hbm(shape(send_shape, BF)), shape((NODE_DEV, LANES), F32)),
        scratch_shapes=[pltpu.VMEM(send_shape, BF), pltpu.SemaphoreType.DMA],
        compiler_params=params(),
        name="side",
    )(enc, own, mid, far, dec_pad)


def limits(win, reach, start, first_node, node_total):
    column = lax.broadcasted_iota(jnp.int32, (1, QB), 1) + reach
    bottom = jnp.maximum(column - win[0:1], reach - start - first_node)
    top = jnp.minimum(column + win[1:2], reach - start - first_node + node_total - 1)
    return jnp.concatenate([bottom, bottom], axis=1), jnp.concatenate([top, top], axis=1)


def masked(scores, at, reach, bottom, top):
    key = lax.broadcasted_iota(jnp.int32, scores.shape, 0) + at
    if at + KC - 1 <= reach:
        keep = key >= bottom
    elif at >= reach + QB - 1:
        keep = key <= top
    else:
        keep = (key >= bottom) & (key <= top)
    return jnp.where(keep, scores, NEG)


def fold(scores):
    return jnp.max(scores.reshape(KC // 8, 8, 2 * QB), axis=0)


def near_kernel(reach, qkv_ref, win_hbm, acc_hbm, top_hbm, q_hbm,
                win_ref, acc_ref, top_ref, q_ref, k_ref, v_ref, vt_ref, score_ref, prob_ref, sem):
    groups = qkv_ref.shape[0]
    win_copy = pltpu.make_async_copy(win_hbm, win_ref, sem.at[0])
    win_copy.start()
    band_rows = groups * NODE_DEV
    first_node = lax.axis_index("band") * band_rows
    node_total = lax.axis_size("band") * band_rows
    lane = lax.broadcasted_iota(jnp.int32, (NODE_DEV, LANES), 1)
    zero = jnp.zeros((NODE_DEV, LANES), BF)
    for group in range(groups):
        rows = pl.ds((group ^ 1) * NODE_DEV, NODE_DEV)
        queries = qkv_ref[group, :, :LANES]
        q_ref[0, rows, :] = jnp.where(lane < HDIM, queries, zero)
        q_ref[1, rows, :] = jnp.where(lane >= HDIM, queries, zero)
        k_ref[rows, :] = qkv_ref[group, :, LANES : 2 * LANES]
        v_ref[rows, :] = qkv_ref[group, :, 2 * LANES :].astype(F32)
    vt = v_ref[...].T.astype(BF)
    for head in range(2):
        vt_ref[head, :HDIM, :] = vt[head * HDIM : (head + 1) * HDIM]
        vt_ref[head, HDIM:, :] = jnp.ones((16, band_rows), BF)
    copies = started([pltpu.make_async_copy(q_ref, q_hbm, sem.at[1])])
    win_copy.wait()
    for block in range(band_rows // QB):
        start = block * QB
        both = jnp.concatenate([q_ref[0, start : start + QB, :], q_ref[1, start : start + QB, :]], axis=0)
        bottom, top = limits(win_ref[:, start : start + QB], reach, start, first_node, node_total)
        first = max(0, reach - start)
        last = min(QB + 2 * reach, band_rows + reach - start)
        largest = jnp.full((8, 2 * QB), NEG, F32)
        for at in range(first, last, KC):
            key = start + at - reach
            scores = masked(dot(k_ref[key : key + KC, :], both, 1, 1), at, reach, bottom, top)
            score_ref[at - first : at - first + KC, :] = scores
            largest = jnp.maximum(largest, fold(scores))
        largest = jnp.max(largest, axis=0, keepdims=True)
        top_ref[block] = largest
        for at in range(0, last - first, KC):
            prob_ref[at : at + KC, :] = jnp.exp2(score_ref[at : at + KC, :] - largest).astype(BF)
        key = start + first - reach
        for head in range(2):
            acc_ref[block, head] = dot(
                vt_ref[head, :, key : key + last - first],
                prob_ref[: last - first, head * QB : (head + 1) * QB],
                1,
                0,
            )
        copies += started([pltpu.make_async_copy(acc_ref.at[block], acc_hbm.at[block], sem.at[3 + block])])
    copies += started([pltpu.make_async_copy(top_ref, top_hbm, sem.at[2])])
    for copy in copies:
        copy.wait()


def near(qkv, win, reach):
    groups = qkv.shape[0]
    band_rows = groups * NODE_DEV
    blocks = band_rows // QB
    keys = min(QB + 2 * reach, band_rows)
    outs = (
        shape((blocks, 2, HDIM + 16, QB), F32),
        shape((blocks, 1, 2 * QB), F32),
        shape((2, band_rows, LANES), BF),
    )
    return pl.pallas_call(
        functools.partial(near_kernel, reach),
        in_specs=[VMEM, HBM],
        out_specs=(HBM,) * 3,
        out_shape=tuple(in_hbm(a) for a in outs),
        scratch_shapes=[
            pltpu.VMEM(win.shape, win.dtype),
            *[pltpu.VMEM(a.shape, a.dtype) for a in outs],
            pltpu.VMEM((band_rows, LANES), BF),
            pltpu.VMEM((band_rows, LANES), F32),
            pltpu.VMEM((2, HDIM + 16, band_rows), BF),
            pltpu.VMEM((keys, 2 * QB), F32),
            pltpu.VMEM((keys, 2 * QB), BF),
            pltpu.SemaphoreType.DMA((3 + blocks,)),
        ],
        compiler_params=params(),
        cost_estimate=pl.CostEstimate(flops=6_000_000_000, bytes_accessed=4_000_000, transcendentals=3_000_000),
        name="near",
    )(qkv, *pinned(win))


def far_kernel(reach, q_hbm, acc_hbm, top_hbm, win_hbm, mix_hbm, off_hbm, chip_ref, node_hbm, out_ref,
               q_ref, acc_ref, top_ref, win_ref, mix_ref, off_ref,
               k_ref, v_ref, vt_ref, score_ref, prob_ref, node_ref, sem):
    band_rows = q_ref.shape[1]
    groups = band_rows // NODE_DEV
    first_node = lax.axis_index("band") * band_rows
    node_total = lax.axis_size("band") * band_rows
    copies = started(
        [
            pltpu.make_async_copy(source, target, sem.at[at])
            for at, (source, target) in enumerate(
                [(off_hbm, off_ref), (q_hbm, q_ref), (acc_hbm, acc_ref), (top_hbm, top_ref), (win_hbm, win_ref), (mix_hbm, mix_ref)]
            )
        ]
    )
    core = lax.rem(lax.axis_index("band"), 2)
    for base, half in (((1 - core) * reach, chip_ref), (core * reach, off_ref)):
        if half is off_ref:
            copies[0].wait()
        for group in range(groups // 2):
            rows = pl.ds(pl.multiple_of(base + (group ^ 1) * NODE_DEV, NODE_DEV), NODE_DEV)
            k_ref[rows, :] = half[group, :, :LANES]
            v_ref[rows, :] = half[group, :, LANES:].astype(F32)
    vt = v_ref[...].T.astype(BF)
    for head in range(2):
        vt_ref[head, :HDIM, :] = vt[head * HDIM : (head + 1) * HDIM]
        vt_ref[head, HDIM:, :] = jnp.ones((16, 2 * reach), BF)
    for copy in copies[1:]:
        copy.wait()
    for block in range(band_rows // QB):
        start = block * QB
        both = jnp.concatenate([q_ref[0, start : start + QB, :], q_ref[1, start : start + QB, :]], axis=0)
        bottom, top = limits(win_ref[:, start : start + QB], reach, start, first_node, node_total)
        low_to = max(0, reach - start)
        high_from = min(QB + 2 * reach, band_rows + reach - start)
        pieces = [(at, start + at) for at in range(0, low_to, KC)]
        pieces += [(at, start + at - band_rows) for at in range(high_from, QB + 2 * reach, KC)]
        before = top_ref[block]
        largest = jnp.full((8, 2 * QB), NEG, F32)
        for row, (at, key) in enumerate(pieces):
            scores = masked(dot(k_ref[key : key + KC, :], both, 1, 1), at, reach, bottom, top)
            score_ref[row * KC : (row + 1) * KC, :] = scores
            largest = jnp.maximum(largest, fold(scores))
        largest = jnp.maximum(jnp.max(largest, axis=0, keepdims=True), before)
        decay = jnp.exp2(before - largest)
        for row in range(len(pieces)):
            prob_ref[row * KC : (row + 1) * KC, :] = jnp.exp2(score_ref[row * KC : (row + 1) * KC, :] - largest).astype(BF)
        low_rows, high_rows = low_to, QB + 2 * reach - high_from
        for head in range(2):
            cols = slice(head * QB, (head + 1) * QB)
            mixed = acc_ref[block, head] * decay[:, cols]
            if low_rows:
                mixed += dot(vt_ref[head, :, start:reach], prob_ref[:low_rows, cols], 1, 0)
            if high_rows:
                at = reach
                mixed += dot(vt_ref[head, :, at : at + high_rows], prob_ref[low_rows : low_rows + high_rows, cols], 1, 0)
            out_ref[head * HDIM : (head + 1) * HDIM, start : start + QB] = (
                mixed[:HDIM] / mixed[HDIM : HDIM + 1]
            ).astype(BF)
    node_ref[...] = dot(mix_ref[...], out_ref[...], 0, 0).T.astype(BF)
    rows = pl.ds(0, NODE_DEV)
    sends = started(
        [
            pltpu.make_async_copy(
                node_ref.at[pl.ds((group ^ 1) * NODE_DEV, NODE_DEV), :],
                node_hbm.at[group, rows, :],
                sem.at[len(copies) + group],
            )
            for group in range(groups)
        ]
    )
    for copy in sends:
        copy.wait()


def far(queries, acc, top, on_chip, off_chip, win, mix):
    band_rows = queries.shape[1]
    groups = band_rows // NODE_DEV
    reach = on_chip.shape[0] * NODE_DEV
    held = (queries, acc, top, win, mix, off_chip)
    return pl.pallas_call(
        functools.partial(far_kernel, reach),
        in_specs=[HBM] * 6 + [VMEM],
        out_specs=(HBM, VMEM),
        out_shape=(
            in_hbm(shape((groups, NODE_DEV + ROWS, LANES), BF)),
            shape((LANES, band_rows), BF),
        ),
        scratch_shapes=[pltpu.VMEM(a.shape, a.dtype) for a in held]
        + [
            pltpu.VMEM((2 * reach, LANES), BF),
            pltpu.VMEM((2 * reach, LANES), F32),
            pltpu.VMEM((2, HDIM + 16, 2 * reach), BF),
            pltpu.VMEM((reach, 2 * QB), F32),
            pltpu.VMEM((reach, 2 * QB), BF),
            pltpu.VMEM((band_rows, LANES), BF),
            pltpu.SemaphoreType.DMA((len(held) + groups,)),
        ],
        compiler_params=params(),
        cost_estimate=pl.CostEstimate(flops=6_000_000_000, bytes_accessed=2_000_000, transcendentals=1_000_000),
        name="far",
    )(*pinned(*held), on_chip)


def grads_kernel(out_ref, extra_ref, keep_ref, give_ref):
    groups = extra_ref.shape[0]
    grad = jnp.zeros((LANES, LANES), F32)
    total = jnp.zeros((ROWS, LANES), F32)
    for group in range(groups):
        at = (group ^ 1) * NODE_DEV
        grad += dot(extra_ref[group, :NODE_DEV, :], out_ref[:, at : at + NODE_DEV], 0, 1)
        total += extra_ref[group, NODE_DEV:, :].astype(F32)
    first = lax.rem(lax.axis_index("band"), 2) == 0
    keep_ref[...] = jnp.where(first, grad[:ROWS], total)
    give_ref[...] = jnp.where(first, total, grad[:ROWS])


def grads(out, extra):
    half = shape((ROWS, LANES), F32)
    return pl.pallas_call(
        grads_kernel,
        in_specs=[VMEM] * 2,
        out_specs=(VMEM,) * 2,
        out_shape=(half, half),
        compiler_params=params(),
        name="grads",
    )(out, extra)


def table_kernel(parts_ref, node_ref, table_ref, padded_ref):
    total = node_ref[...]
    for group in range(parts_ref.shape[0]):
        total += parts_ref[group, :NODE_DEV, :].astype(F32)
    table_ref[...] = total.astype(BF)
    padded_ref[:NODE_DEV, :] = total.astype(BF)
    padded_ref[NODE_DEV:, :] = jnp.zeros((EXTRA, LANES), BF)


def make_table(parts, node):
    return pl.pallas_call(
        table_kernel,
        in_specs=[VMEM] * 2,
        out_specs=(VMEM,) * 2,
        out_shape=(shape(node.shape, BF), shape((NODE_DEV + EXTRA, LANES), BF)),
        compiler_params=params(),
        name="make_table",
    )(parts, node)


def decode_kernel(mid_ref, far_ref, own_ref, dec_ref, grid_ref, pred_ref):
    channels, points = grid_ref.shape
    nodes = NODE_DEV
    rows = 4 * LANES
    table = jnp.concatenate(
        [
            far_ref[:NODE_DEV].astype(F32),
            mid_ref[...].astype(F32),
            own_ref[...].astype(F32),
            jnp.zeros((rows - 3 * nodes, LANES), F32),
        ],
        axis=0,
    ).T.astype(BF)
    width = 512
    bases = chunk_bases()
    node_id = lax.broadcasted_iota(jnp.int32, (nodes, width), 0)
    for at in range(0, points, width):
        target = dec_ref[:, at : at + width]
        pick = [jnp.where(node_id == target - base, 1.0, 0.0) for base in bases]
        pick = jnp.concatenate(pick + [jnp.zeros((rows - 3 * nodes, width), F32)], axis=0).astype(BF)
        decoded = dot(table, pick, 1, 0)
        pred_ref[:, at : at + width] = (
            grid_ref[:, at : at + width].astype(F32) + decoded[:channels]
        ).astype(BF)


def decode(far_rows, mid_rows, own_rows, dec_row, grid_in):
    return pl.pallas_call(
        decode_kernel,
        in_specs=[VMEM] * 5,
        out_specs=VMEM,
        out_shape=shape(grid_in.shape, BF),
        compiler_params=params(),
        name="decode",
    )(mid_rows, far_rows, own_rows, dec_row, grid_in)


def spread_kernel(grad_ref, more_ref, parts_hbm, filled_hbm, sum_ref, sem):
    sum_ref[...] = (grad_ref[...].astype(F32) + more_ref[...].astype(F32)).astype(BF)
    rows = pl.ds(NODE_DEV, sum_ref.shape[0])
    copies = [
        pltpu.make_async_copy(sum_ref, filled_hbm.at[at, rows, :], sem.at[at]) for at in range(filled_hbm.shape[0])
    ]
    for copy in started(copies):
        copy.wait()


def spread(grad, more, parts):
    return pl.pallas_call(
        spread_kernel,
        in_specs=[VMEM, VMEM, HBM],
        out_specs=HBM,
        out_shape=in_hbm(parts),
        input_output_aliases={2: 0},
        scratch_shapes=[pltpu.VMEM(grad.shape, BF), pltpu.SemaphoreType.DMA((parts.shape[0],))],
        compiler_params=params(),
        name="spread",
    )(grad, more, *pinned(parts))


def half_kernel(parts_ref, w_out_ref, half_ref):
    first = lax.rem(lax.axis_index("band"), 2) == 0
    groups = parts_ref.shape[0]

    @pl.when(first)
    def _():
        mixed = jnp.zeros(half_ref.shape, F32)
        for group in range(groups):
            rows = w_out_ref[group * LANES : (group + 1) * LANES, :]
            mixed += dot(parts_ref[group, NODE_DEV:, :], rows, 1, 0)
        half_ref[...] = mixed

    @pl.when(jnp.logical_not(first))
    def _():
        for group in range(groups):
            half_ref[:, group * LANES : (group + 1) * LANES] = parts_ref[group, NODE_DEV:, :].astype(F32)


def gradient_half(parts, w_out):
    return pl.pallas_call(
        half_kernel,
        in_specs=[VMEM] * 2,
        out_specs=VMEM,
        out_shape=shape((ROWS, w_out.shape[1]), F32),
        compiler_params=params(),
        name="gradient_half",
    )(parts, w_out)


def add_kernel(mine_ref, other_ref, out_ref):
    channels = out_ref.shape[0]
    out_ref[...] = mine_ref[:channels] + other_ref[:channels]


def add(mine, other, channels):
    return pl.pallas_call(
        add_kernel,
        in_specs=[VMEM] * 2,
        out_specs=VMEM,
        out_shape=shape((channels, mine.shape[1]), F32),
        compiler_params=params(),
        name="add",
    )(mine, other)


def total_devices():
    return lax.axis_size("band") * lax.axis_size("head")


def to_partner(block):
    return lax.ppermute(block, BOTH, [(i, i ^ 1) for i in range(total_devices())])


def two_over(block, sign):
    count = total_devices()
    pairs = [(i, i + sign * (2 - 4 * (i % 2))) for i in range(count)]
    return lax.ppermute(block, BOTH, [(i, j) for i, j in pairs if 0 <= j < count])


def next_chip(block):
    count = lax.axis_size("band")
    pairs = [(i, i - 1 + 2 * (i % 2)) for i in range(count)]
    return lax.ppermute(block, "band", [(i, j) for i, j in pairs if 0 <= j < count])


def flipped(block, axis, bit):
    return lax.ppermute(block, axis, [(i, i ^ (1 << bit)) for i in range(lax.axis_size(axis))])


def across(block):
    planes = lax.axis_size("band") // 4
    other = [(z + 6) % planes if z % 4 < 2 else (z + 2) % planes for z in range(planes)]
    return lax.ppermute(block, "band", [(i, other[i // 4] * 4 + i % 4) for i in range(planes * 4)])


def swap(block):
    return lax.all_to_all(block, "head", split_axis=0, concat_axis=0, tiled=True)


def shards(
    grid_in, enc_node, dec_node, win_offsets, w_in, b_in, w_qkv, w_out, norm_gain, w_dec, cotangent
):
    channels = grid_in.shape[0]
    groups = lax.axis_size("head")
    dec_row = dec_node[None]
    far_part, mid_part, own = encode(grid_in, enc_node[None], w_in, b_in[None])
    weights, dec_pad, mix, far_sum, mid_sum, own_sum = prepare(
        w_qkv, w_out, w_dec.T, cotangent, dec_row, far_part
    )
    mid_in = to_partner(mid_part)
    far_in = two_over(far_part, -1)
    mid_sum = to_partner(mid_sum)
    far_sum = two_over(far_sum, -1)
    packed, enc = project(own, mid_in, far_in, norm_gain[None], weights)
    packed, mid_sum, far_sum = lax.optimization_barrier((packed, mid_sum, far_sum))
    qkv = swap(packed)
    send, node = side(enc, own_sum, mid_sum, far_sum, dec_pad)
    qkv, send, node = lax.optimization_barrier((qkv, send, node))
    half = groups // 2
    reach = half * NODE_DEV
    core = lax.rem(lax.axis_index("band"), 2)
    kv = qkv[:, :, LANES:]
    on_chip = flipped(lax.dynamic_slice_in_dim(kv, (1 - core) * half, half, 0), "band", 0)
    off_chip = next_chip(lax.dynamic_slice_in_dim(kv, core * half, half, 0))
    extra = swap(send)
    acc, top, queries = near(qkv, win_offsets, reach)
    parts, attended = far(queries, acc, top, on_chip, off_chip, win_offsets, mix)
    grad, give = grads(attended, extra)
    grad = (grad + flipped(give, "band", 0)).astype(BF)
    for bit in (1, 2, 3):
        grad = (grad.astype(F32) + flipped(grad, "band", bit).astype(F32)).astype(BF)
    parts = swap(spread(grad, across(grad), parts))
    table, padded = make_table(parts, node)
    half_grad = gradient_half(parts, w_out)
    grad_dec = add(half_grad, flipped(half_grad, "band", 0), channels)
    grad_dec, mid_rows = lax.optimization_barrier((grad_dec, to_partner(table)))
    prediction = decode(two_over(padded, 1), mid_rows, table, dec_row, grid_in)
    return (prediction, grad_dec.T)


def solution(mesh):
    placed = (
        P(None, BOTH),
        P(BOTH),
        P(BOTH),
        P(None, "band"),
        P(),
        P(),
        P(),
        P(),
        P(),
        P(),
        P(None, BOTH),
    )
    return jax.shard_map(
        shards,
        mesh=mesh,
        in_specs=placed,
        out_specs=(P(None, BOTH), P()),
        check_vma=False,
    )
```

```python
import functools

import jax
import jax.numpy as jnp
from jax import lax
from jax.experimental import pallas as pl
from jax.experimental.pallas import tpu as pltpu
from jax.sharding import PartitionSpec as P

HDIM = 64
NODE_DEV = 160
BOTH = ("band", "head")
LANES = 128
QB = 256
KC = 128
ROWS = 112
EXTRA = 16
BF = jnp.bfloat16
F32 = jnp.float32
LOG2E = 1.4426950408889634
NEG = -1e30
HBM = pl.BlockSpec(memory_space=pltpu.HBM)
VMEM = pl.BlockSpec(memory_space=pltpu.VMEM)


def params(mib=24):
    return pltpu.CompilerParams(vmem_limit_bytes=mib * 1024 * 1024)


def dot(a, b, ca, cb):
    return lax.dot_general(a, b, (((ca,), (cb,)), ((), ())), preferred_element_type=F32)


def shape(dims, dtype):
    return jax.ShapeDtypeStruct(dims, dtype)


def in_hbm(a):
    return pltpu.HBM(a.shape, a.dtype)


def pinned(*arrays):
    return tuple(pltpu.with_memory_space_constraint(a, pltpu.HBM) for a in arrays)


def started(copies):
    for copy in copies:
        copy.start()
    return copies


def chunk_bases():
    index = lax.axis_index("band") * lax.axis_size("head") + lax.axis_index("head")
    side = 1 - 2 * lax.rem(index, 2)
    return (index - side) * NODE_DEV, index * NODE_DEV, (index + side) * NODE_DEV


def fill_pick(pick_ref, target):
    nodes, points = NODE_DEV, pick_ref.shape[1]
    node_id = lax.broadcasted_iota(jnp.int32, (nodes, points), 0)
    for at, base in enumerate(chunk_bases()):
        pick_ref[at * nodes : (at + 1) * nodes, :] = jnp.where(node_id == target - base, 1.0, 0.0).astype(BF)


def encode_kernel(grid_hbm, enc_hbm, w_hbm, b_hbm, far_ref, mid_ref, own_ref,
                  grid_ref, enc_ref, w_ref, b_ref, w_half, pick_ref, sem):
    model = w_ref.shape[1]
    nodes = NODE_DEV
    copies = started(
        [
            pltpu.make_async_copy(source, target, sem.at[at])
            for at, (source, target) in enumerate(
                [(grid_hbm, grid_ref), (enc_hbm, enc_ref), (w_hbm, w_ref), (b_hbm, b_ref)]
            )
        ]
    )
    copies[1].wait()
    fill_pick(pick_ref, enc_ref[...])
    copies[2].wait()
    w_half[...] = (w_ref[...].astype(F32) * 0.5).astype(BF)
    copies[0].wait()
    copies[3].wait()
    width = 512
    mid_ref[nodes:, :] = jnp.zeros((EXTRA, model), BF)
    for at in range(0, model, width):
        half = dot(grid_ref[...], w_half[:, at : at + width], 0, 0) + b_ref[:, at : at + width] * 0.5
        message = (half + half * jnp.tanh(half)).astype(BF)
        spread = dot(pick_ref[...], message, 1, 0)
        far_ref[:, at : at + width] = spread[:nodes].astype(BF)
        mid_ref[:nodes, at : at + width] = spread[nodes : 2 * nodes].astype(BF)
        own_ref[:, at : at + width] = spread[2 * nodes :]


def encode(grid_in, enc_row, w_in, b_row):
    points = grid_in.shape[1]
    model = w_in.shape[1]
    operands = (grid_in, enc_row, w_in, b_row)
    return pl.pallas_call(
        encode_kernel,
        in_specs=[HBM] * 4,
        out_specs=(VMEM,) * 3,
        out_shape=(shape((NODE_DEV, model), BF), shape((NODE_DEV + EXTRA, model), BF), shape((NODE_DEV, model), F32)),
        scratch_shapes=[pltpu.VMEM(a.shape, a.dtype) for a in operands]
        + [
            pltpu.VMEM(w_in.shape, BF),
            pltpu.VMEM((3 * NODE_DEV, points), BF),
            pltpu.SemaphoreType.DMA((4,)),
        ],
        compiler_params=params(),
        name="encode",
    )(*pinned(*operands))


def prepare_kernel(w_hbm, out_hbm, dec_hbm, cot_hbm, target_hbm, after_ref,
                   w_ref, pad_ref, mix_hbm, far_ref, mid_ref, own_ref,
                   mix_ref, out_rows, dec_rows, cot_ref, target_ref, cot_pad, pick_ref, sem):
    channels = dec_rows.shape[0]
    nodes = NODE_DEV
    at = pl.multiple_of(lax.axis_index("head") * LANES, LANES)
    copies = started(
        [
            pltpu.make_async_copy(source, target, sem.at[number])
            for number, (source, target) in enumerate(
                [
                    (target_hbm, target_ref),
                    (cot_hbm, cot_ref),
                    (dec_hbm, dec_rows),
                    (out_hbm.at[pl.ds(at, LANES), :], out_rows),
                    (w_hbm, w_ref),
                ]
            )
        ]
    )
    copies[0].wait()
    fill_pick(pick_ref, target_ref[...])
    copies[1].wait()
    cot_pad[...] = jnp.zeros_like(cot_pad)
    cot_pad[:channels, :] = cot_ref[...]
    spread = dot(pick_ref[...], cot_pad[...], 1, 1)
    far_ref[...] = spread[:nodes].astype(BF)
    mid_ref[...] = spread[nodes : 2 * nodes].astype(BF)
    own_ref[...] = spread[2 * nodes :]
    copies[2].wait()
    pad_ref[...] = jnp.zeros_like(pad_ref)
    pad_ref[:channels, :] = dec_rows[...]
    copies[3].wait()
    mix_ref[...] = dot(out_rows[...], pad_ref[...], 1, 1).astype(BF)
    copy = pltpu.make_async_copy(mix_ref, mix_hbm, sem.at[len(copies)])
    copy.start()
    copy.wait()
    copies[4].wait()


def prepare(w_qkv, w_out, dec_cols, cotangent, dec_row, after):
    model = w_qkv.shape[0]
    points = cotangent.shape[1]
    part = (NODE_DEV, LANES)
    return pl.pallas_call(
        prepare_kernel,
        in_specs=[HBM] * 5 + [pl.BlockSpec(memory_space=pl.ANY)],
        out_specs=(VMEM, VMEM, HBM, VMEM, VMEM, VMEM),
        out_shape=(
            shape(w_qkv.shape, BF),
            shape((LANES, model), BF),
            in_hbm(shape((LANES, LANES), BF)),
            shape(part, BF),
            shape(part, BF),
            shape(part, F32),
        ),
        scratch_shapes=[
            pltpu.VMEM((LANES, LANES), BF),
            pltpu.VMEM((LANES, model), BF),
            pltpu.VMEM(dec_cols.shape, BF),
            pltpu.VMEM(cotangent.shape, BF),
            pltpu.VMEM(dec_row.shape, jnp.int32),
            pltpu.VMEM((LANES, points), BF),
            pltpu.VMEM((3 * NODE_DEV, points), BF),
            pltpu.SemaphoreType.DMA((6,)),
        ],
        compiler_params=params(),
        cost_estimate=pl.CostEstimate(flops=500_000_000, bytes_accessed=2 * w_qkv.size, transcendentals=0),
        name="prepare",
    )(*pinned(w_qkv, w_out, dec_cols, cotangent, dec_row), after)


def project_kernel(own_ref, mid_ref, far_ref, gain_ref, w_ref, packed_hbm, enc_ref, packed, sem):
    model = gain_ref.shape[1]
    enc = own_ref[...] + mid_ref[:NODE_DEV].astype(F32) + far_ref[...].astype(F32)
    enc_ref[...] = enc
    centred = enc - jnp.mean(enc, axis=1, keepdims=True)
    spread_sq = jnp.mean(centred * centred, axis=1, keepdims=True)
    normed = (centred * lax.rsqrt(spread_sq + 1e-05) * gain_ref[...]).astype(BF)
    scale = HDIM ** (-0.5) * LOG2E
    copies = []
    for pair in range(model // (2 * LANES)):
        for part in range(3):
            at = part * model + pair * 2 * LANES
            cols = dot(normed, w_ref[:, at : at + 2 * LANES], 1, 0)
            if part == 0:
                cols = cols * scale
            cols = cols.astype(BF)
            for half in range(2):
                packed[2 * pair + half, :, part * LANES : (part + 1) * LANES] = cols[:, half * LANES : (half + 1) * LANES]
        rows = pl.ds(2 * pair, 2)
        copies += started([pltpu.make_async_copy(packed.at[rows], packed_hbm.at[rows], sem.at[pair])])
    for copy in copies:
        copy.wait()


def project(own, mid, far, gain_row, w_qkv):
    model = w_qkv.shape[0]
    groups = model // LANES
    return pl.pallas_call(
        project_kernel,
        in_specs=[VMEM] * 5,
        out_specs=(HBM, VMEM),
        out_shape=(
            in_hbm(shape((groups, NODE_DEV, 3 * LANES), BF)),
            shape((NODE_DEV, model), F32),
        ),
        scratch_shapes=[
            pltpu.VMEM((groups, NODE_DEV, 3 * LANES), BF),
            pltpu.SemaphoreType.DMA((groups // 2,)),
        ],
        compiler_params=params(),
        name="project",
    )(own, mid, far, gain_row, w_qkv)


def side_kernel(enc_ref, own_ref, mid_ref, far_ref, dec_ref, send_hbm, node_ref, send, sem):
    groups = send.shape[0]
    enc = enc_ref[...]
    summed = (own_ref[...] + mid_ref[...].astype(F32) + far_ref[...].astype(F32)).astype(BF)
    high = enc.astype(BF)
    low = (enc - high.astype(F32)).astype(BF)
    node_ref[...] = dot(high, dec_ref[...], 1, 1)
    grad = (dot(summed, high, 0, 0) + dot(summed, low, 0, 0)).astype(BF)
    for group in range(groups):
        send[group, :NODE_DEV, :] = summed
        send[group, NODE_DEV:, :] = grad[:ROWS, group * LANES : (group + 1) * LANES]
    copy = pltpu.make_async_copy(send, send_hbm, sem)
    copy.start()
    copy.wait()


def side(enc, own, mid, far, dec_pad):
    groups = enc.shape[1] // LANES
    send_shape = (groups, NODE_DEV + ROWS, LANES)
    return pl.pallas_call(
        side_kernel,
        in_specs=[VMEM] * 5,
        out_specs=(HBM, VMEM),
        out_shape=(in_hbm(shape(send_shape, BF)), shape((NODE_DEV, LANES), F32)),
        scratch_shapes=[pltpu.VMEM(send_shape, BF), pltpu.SemaphoreType.DMA],
        compiler_params=params(),
        name="side",
    )(enc, own, mid, far, dec_pad)


def limits(win, reach, start, first_node, node_total):
    column = lax.broadcasted_iota(jnp.int32, (1, QB), 1) + reach
    bottom = jnp.maximum(column - win[0:1], reach - start - first_node)
    top = jnp.minimum(column + win[1:2], reach - start - first_node + node_total - 1)
    return jnp.concatenate([bottom, bottom], axis=1), jnp.concatenate([top, top], axis=1)


def masked(scores, at, reach, bottom, top):
    key = lax.broadcasted_iota(jnp.int32, scores.shape, 0) + at
    if at + KC - 1 <= reach:
        keep = key >= bottom
    elif at >= reach + QB - 1:
        keep = key <= top
    else:
        keep = (key >= bottom) & (key <= top)
    return jnp.where(keep, scores, NEG)


def fold(scores):
    return jnp.max(scores.reshape(KC // 8, 8, 2 * QB), axis=0)


def near_kernel(reach, qkv_ref, win_hbm, acc_hbm, top_hbm, q_hbm,
                win_ref, acc_ref, top_ref, q_ref, k_ref, v_ref, vt_ref, score_ref, prob_ref, sem):
    groups = qkv_ref.shape[0]
    win_copy = pltpu.make_async_copy(win_hbm, win_ref, sem.at[0])
    win_copy.start()
    band_rows = groups * NODE_DEV
    first_node = lax.axis_index("band") * band_rows
    node_total = lax.axis_size("band") * band_rows
    lane = lax.broadcasted_iota(jnp.int32, (NODE_DEV, LANES), 1)
    zero = jnp.zeros((NODE_DEV, LANES), BF)
    for group in range(groups):
        rows = pl.ds((group ^ 1) * NODE_DEV, NODE_DEV)
        queries = qkv_ref[group, :, :LANES]
        q_ref[0, rows, :] = jnp.where(lane < HDIM, queries, zero)
        q_ref[1, rows, :] = jnp.where(lane >= HDIM, queries, zero)
        k_ref[rows, :] = qkv_ref[group, :, LANES : 2 * LANES]
        v_ref[rows, :] = qkv_ref[group, :, 2 * LANES :].astype(F32)
    vt = v_ref[...].T.astype(BF)
    for head in range(2):
        vt_ref[head, :HDIM, :] = vt[head * HDIM : (head + 1) * HDIM]
        vt_ref[head, HDIM:, :] = jnp.ones((16, band_rows), BF)
    copies = started([pltpu.make_async_copy(q_ref, q_hbm, sem.at[1])])
    win_copy.wait()
    for block in range(band_rows // QB):
        start = block * QB
        both = jnp.concatenate([q_ref[0, start : start + QB, :], q_ref[1, start : start + QB, :]], axis=0)
        bottom, top = limits(win_ref[:, start : start + QB], reach, start, first_node, node_total)
        first = max(0, reach - start)
        last = min(QB + 2 * reach, band_rows + reach - start)
        largest = jnp.full((8, 2 * QB), NEG, F32)
        for at in range(first, last, KC):
            key = start + at - reach
            scores = masked(dot(k_ref[key : key + KC, :], both, 1, 1), at, reach, bottom, top)
            score_ref[at - first : at - first + KC, :] = scores
            largest = jnp.maximum(largest, fold(scores))
        largest = jnp.max(largest, axis=0, keepdims=True)
        top_ref[block] = largest
        for at in range(0, last - first, KC):
            prob_ref[at : at + KC, :] = jnp.exp2(score_ref[at : at + KC, :] - largest).astype(BF)
        key = start + first - reach
        for head in range(2):
            acc_ref[block, head] = dot(
                vt_ref[head, :, key : key + last - first],
                prob_ref[: last - first, head * QB : (head + 1) * QB],
                1,
                0,
            )
        copies += started([pltpu.make_async_copy(acc_ref.at[block], acc_hbm.at[block], sem.at[3 + block])])
    copies += started([pltpu.make_async_copy(top_ref, top_hbm, sem.at[2])])
    for copy in copies:
        copy.wait()


def near(qkv, win, reach):
    groups = qkv.shape[0]
    band_rows = groups * NODE_DEV
    blocks = band_rows // QB
    keys = min(QB + 2 * reach, band_rows)
    outs = (
        shape((blocks, 2, HDIM + 16, QB), F32),
        shape((blocks, 1, 2 * QB), F32),
        shape((2, band_rows, LANES), BF),
    )
    return pl.pallas_call(
        functools.partial(near_kernel, reach),
        in_specs=[VMEM, HBM],
        out_specs=(HBM,) * 3,
        out_shape=tuple(in_hbm(a) for a in outs),
        scratch_shapes=[
            pltpu.VMEM(win.shape, win.dtype),
            *[pltpu.VMEM(a.shape, a.dtype) for a in outs],
            pltpu.VMEM((band_rows, LANES), BF),
            pltpu.VMEM((band_rows, LANES), F32),
            pltpu.VMEM((2, HDIM + 16, band_rows), BF),
            pltpu.VMEM((keys, 2 * QB), F32),
            pltpu.VMEM((keys, 2 * QB), BF),
            pltpu.SemaphoreType.DMA((3 + blocks,)),
        ],
        compiler_params=params(),
        cost_estimate=pl.CostEstimate(flops=6_000_000_000, bytes_accessed=4_000_000, transcendentals=3_000_000),
        name="near",
    )(qkv, *pinned(win))


def far_kernel(reach, q_hbm, acc_hbm, top_hbm, win_hbm, mix_hbm, off_hbm, chip_ref, node_hbm, out_ref,
               q_ref, acc_ref, top_ref, win_ref, mix_ref, off_ref,
               k_ref, v_ref, vt_ref, score_ref, prob_ref, node_ref, sem):
    band_rows = q_ref.shape[1]
    groups = band_rows // NODE_DEV
    first_node = lax.axis_index("band") * band_rows
    node_total = lax.axis_size("band") * band_rows
    copies = started(
        [
            pltpu.make_async_copy(source, target, sem.at[at])
            for at, (source, target) in enumerate(
                [(off_hbm, off_ref), (q_hbm, q_ref), (acc_hbm, acc_ref), (top_hbm, top_ref), (win_hbm, win_ref), (mix_hbm, mix_ref)]
            )
        ]
    )
    core = lax.rem(lax.axis_index("band"), 2)
    for base, half in (((1 - core) * reach, chip_ref), (core * reach, off_ref)):
        if half is off_ref:
            copies[0].wait()
        for group in range(groups // 2):
            rows = pl.ds(pl.multiple_of(base + (group ^ 1) * NODE_DEV, NODE_DEV), NODE_DEV)
            k_ref[rows, :] = half[group, :, :LANES]
            v_ref[rows, :] = half[group, :, LANES:].astype(F32)
    vt = v_ref[...].T.astype(BF)
    for head in range(2):
        vt_ref[head, :HDIM, :] = vt[head * HDIM : (head + 1) * HDIM]
        vt_ref[head, HDIM:, :] = jnp.ones((16, 2 * reach), BF)
    for copy in copies[1:]:
        copy.wait()
    for block in range(band_rows // QB):
        start = block * QB
        both = jnp.concatenate([q_ref[0, start : start + QB, :], q_ref[1, start : start + QB, :]], axis=0)
        bottom, top = limits(win_ref[:, start : start + QB], reach, start, first_node, node_total)
        low_to = max(0, reach - start)
        high_from = min(QB + 2 * reach, band_rows + reach - start)
        pieces = [(at, start + at) for at in range(0, low_to, KC)]
        pieces += [(at, start + at - band_rows) for at in range(high_from, QB + 2 * reach, KC)]
        before = top_ref[block]
        largest = jnp.full((8, 2 * QB), NEG, F32)
        for row, (at, key) in enumerate(pieces):
            scores = masked(dot(k_ref[key : key + KC, :], both, 1, 1), at, reach, bottom, top)
            score_ref[row * KC : (row + 1) * KC, :] = scores
            largest = jnp.maximum(largest, fold(scores))
        largest = jnp.maximum(jnp.max(largest, axis=0, keepdims=True), before)
        decay = jnp.exp2(before - largest)
        for row in range(len(pieces)):
            prob_ref[row * KC : (row + 1) * KC, :] = jnp.exp2(score_ref[row * KC : (row + 1) * KC, :] - largest).astype(BF)
        low_rows, high_rows = low_to, QB + 2 * reach - high_from
        for head in range(2):
            cols = slice(head * QB, (head + 1) * QB)
            mixed = acc_ref[block, head] * decay[:, cols]
            if low_rows:
                mixed += dot(vt_ref[head, :, start:reach], prob_ref[:low_rows, cols], 1, 0)
            if high_rows:
                at = reach
                mixed += dot(vt_ref[head, :, at : at + high_rows], prob_ref[low_rows : low_rows + high_rows, cols], 1, 0)
            out_ref[head * HDIM : (head + 1) * HDIM, start : start + QB] = (
                mixed[:HDIM] / mixed[HDIM : HDIM + 1]
            ).astype(BF)
    node_ref[...] = dot(mix_ref[...], out_ref[...], 0, 0).T.astype(BF)
    rows = pl.ds(0, NODE_DEV)
    sends = started(
        [
            pltpu.make_async_copy(
                node_ref.at[pl.ds((group ^ 1) * NODE_DEV, NODE_DEV), :],
                node_hbm.at[group, rows, :],
                sem.at[len(copies) + group],
            )
            for group in range(groups)
        ]
    )
    for copy in sends:
        copy.wait()


def far(queries, acc, top, on_chip, off_chip, win, mix):
    band_rows = queries.shape[1]
    groups = band_rows // NODE_DEV
    reach = on_chip.shape[0] * NODE_DEV
    held = (queries, acc, top, win, mix, off_chip)
    return pl.pallas_call(
        functools.partial(far_kernel, reach),
        in_specs=[HBM] * 6 + [VMEM],
        out_specs=(HBM, VMEM),
        out_shape=(
            in_hbm(shape((groups, NODE_DEV + ROWS, LANES), BF)),
            shape((LANES, band_rows), BF),
        ),
        scratch_shapes=[pltpu.VMEM(a.shape, a.dtype) for a in held]
        + [
            pltpu.VMEM((2 * reach, LANES), BF),
            pltpu.VMEM((2 * reach, LANES), F32),
            pltpu.VMEM((2, HDIM + 16, 2 * reach), BF),
            pltpu.VMEM((reach, 2 * QB), F32),
            pltpu.VMEM((reach, 2 * QB), BF),
            pltpu.VMEM((band_rows, LANES), BF),
            pltpu.SemaphoreType.DMA((len(held) + groups,)),
        ],
        compiler_params=params(),
        cost_estimate=pl.CostEstimate(flops=6_000_000_000, bytes_accessed=2_000_000, transcendentals=1_000_000),
        name="far",
    )(*pinned(*held), on_chip)


def grads_kernel(out_ref, extra_ref, keep_ref, give_ref):
    groups = extra_ref.shape[0]
    grad = jnp.zeros((LANES, LANES), F32)
    total = jnp.zeros((ROWS, LANES), F32)
    for group in range(groups):
        at = (group ^ 1) * NODE_DEV
        grad += dot(extra_ref[group, :NODE_DEV, :], out_ref[:, at : at + NODE_DEV], 0, 1)
        total += extra_ref[group, NODE_DEV:, :].astype(F32)
    first = lax.rem(lax.axis_index("band"), 2) == 0
    keep_ref[...] = jnp.where(first, grad[:ROWS], total)
    give_ref[...] = jnp.where(first, total, grad[:ROWS])


def grads(out, extra):
    half = shape((ROWS, LANES), F32)
    return pl.pallas_call(
        grads_kernel,
        in_specs=[VMEM] * 2,
        out_specs=(VMEM,) * 2,
        out_shape=(half, half),
        compiler_params=params(),
        name="grads",
    )(out, extra)


def table_kernel(parts_ref, node_ref, table_ref, padded_ref):
    total = node_ref[...]
    for group in range(parts_ref.shape[0]):
        total += parts_ref[group, :NODE_DEV, :].astype(F32)
    table_ref[...] = total.astype(BF)
    padded_ref[:NODE_DEV, :] = total.astype(BF)
    padded_ref[NODE_DEV:, :] = jnp.zeros((EXTRA, LANES), BF)


def make_table(parts, node):
    return pl.pallas_call(
        table_kernel,
        in_specs=[VMEM] * 2,
        out_specs=(VMEM,) * 2,
        out_shape=(shape(node.shape, BF), shape((NODE_DEV + EXTRA, LANES), BF)),
        compiler_params=params(),
        name="make_table",
    )(parts, node)


def decode_kernel(mid_ref, far_ref, own_ref, dec_ref, grid_ref, pred_ref):
    channels, points = grid_ref.shape
    nodes = NODE_DEV
    rows = 4 * LANES
    table = jnp.concatenate(
        [
            far_ref[:NODE_DEV].astype(F32),
            mid_ref[...].astype(F32),
            own_ref[...].astype(F32),
            jnp.zeros((rows - 3 * nodes, LANES), F32),
        ],
        axis=0,
    ).T.astype(BF)
    width = 512
    bases = chunk_bases()
    node_id = lax.broadcasted_iota(jnp.int32, (nodes, width), 0)
    for at in range(0, points, width):
        target = dec_ref[:, at : at + width]
        pick = [jnp.where(node_id == target - base, 1.0, 0.0) for base in bases]
        pick = jnp.concatenate(pick + [jnp.zeros((rows - 3 * nodes, width), F32)], axis=0).astype(BF)
        decoded = dot(table, pick, 1, 0)
        pred_ref[:, at : at + width] = (
            grid_ref[:, at : at + width].astype(F32) + decoded[:channels]
        ).astype(BF)


def decode(far_rows, mid_rows, own_rows, dec_row, grid_in):
    return pl.pallas_call(
        decode_kernel,
        in_specs=[VMEM] * 5,
        out_specs=VMEM,
        out_shape=shape(grid_in.shape, BF),
        compiler_params=params(),
        name="decode",
    )(mid_rows, far_rows, own_rows, dec_row, grid_in)


def spread_kernel(grad_ref, more_ref, parts_hbm, filled_hbm, sum_ref, sem):
    sum_ref[...] = (grad_ref[...].astype(F32) + more_ref[...].astype(F32)).astype(BF)
    rows = pl.ds(NODE_DEV, sum_ref.shape[0])
    copies = [
        pltpu.make_async_copy(sum_ref, filled_hbm.at[at, rows, :], sem.at[at]) for at in range(filled_hbm.shape[0])
    ]
    for copy in started(copies):
        copy.wait()


def spread(grad, more, parts):
    return pl.pallas_call(
        spread_kernel,
        in_specs=[VMEM, VMEM, HBM],
        out_specs=HBM,
        out_shape=in_hbm(parts),
        input_output_aliases={2: 0},
        scratch_shapes=[pltpu.VMEM(grad.shape, BF), pltpu.SemaphoreType.DMA((parts.shape[0],))],
        compiler_params=params(),
        name="spread",
    )(grad, more, *pinned(parts))


def half_kernel(parts_ref, w_out_ref, half_ref):
    first = lax.rem(lax.axis_index("band"), 2) == 0
    groups = parts_ref.shape[0]

    @pl.when(first)
    def _():
        mixed = jnp.zeros(half_ref.shape, F32)
        for group in range(groups):
            rows = w_out_ref[group * LANES : (group + 1) * LANES, :]
            mixed += dot(parts_ref[group, NODE_DEV:, :], rows, 1, 0)
        half_ref[...] = mixed

    @pl.when(jnp.logical_not(first))
    def _():
        for group in range(groups):
            half_ref[:, group * LANES : (group + 1) * LANES] = parts_ref[group, NODE_DEV:, :].astype(F32)


def gradient_half(parts, w_out):
    return pl.pallas_call(
        half_kernel,
        in_specs=[VMEM] * 2,
        out_specs=VMEM,
        out_shape=shape((ROWS, w_out.shape[1]), F32),
        compiler_params=params(),
        name="gradient_half",
    )(parts, w_out)


def add_kernel(mine_ref, other_ref, out_ref):
    channels = out_ref.shape[0]
    out_ref[...] = mine_ref[:channels] + other_ref[:channels]


def add(mine, other, channels):
    return pl.pallas_call(
        add_kernel,
        in_specs=[VMEM] * 2,
        out_specs=VMEM,
        out_shape=shape((channels, mine.shape[1]), F32),
        compiler_params=params(),
        name="add",
    )(mine, other)


def total_devices():
    return lax.axis_size("band") * lax.axis_size("head")


def to_partner(block):
    return lax.ppermute(block, BOTH, [(i, i ^ 1) for i in range(total_devices())])


def two_over(block, sign):
    count = total_devices()
    pairs = [(i, i + sign * (2 - 4 * (i % 2))) for i in range(count)]
    return lax.ppermute(block, BOTH, [(i, j) for i, j in pairs if 0 <= j < count])


def next_chip(block):
    count = lax.axis_size("band")
    pairs = [(i, i - 1 + 2 * (i % 2)) for i in range(count)]
    return lax.ppermute(block, "band", [(i, j) for i, j in pairs if 0 <= j < count])


def flipped(block, axis, bit):
    return lax.ppermute(block, axis, [(i, i ^ (1 << bit)) for i in range(lax.axis_size(axis))])


def across(block):
    planes = lax.axis_size("band") // 4
    other = [(z + 6) % planes if z % 4 < 2 else (z + 2) % planes for z in range(planes)]
    return lax.ppermute(block, "band", [(i, other[i // 4] * 4 + i % 4) for i in range(planes * 4)])


def swap(block):
    return lax.all_to_all(block, "head", split_axis=0, concat_axis=0, tiled=True)


def shards(
    grid_in, enc_node, dec_node, win_offsets, w_in, b_in, w_qkv, w_out, norm_gain, w_dec, cotangent
):
    channels = grid_in.shape[0]
    groups = lax.axis_size("head")
    dec_row = dec_node[None]
    far_part, mid_part, own = encode(grid_in, enc_node[None], w_in, b_in[None])
    weights, dec_pad, mix, far_sum, mid_sum, own_sum = prepare(
        w_qkv, w_out, w_dec.T, cotangent, dec_row, far_part
    )
    mid_in = to_partner(mid_part)
    far_in = two_over(far_part, -1)
    mid_sum = to_partner(mid_sum)
    far_sum = two_over(far_sum, -1)
    packed, enc = project(own, mid_in, far_in, norm_gain[None], weights)
    packed, mid_sum = lax.optimization_barrier((packed, mid_sum))
    qkv = swap(packed)
    send, node = side(enc, own_sum, mid_sum, far_sum, dec_pad)
    qkv, send, node = lax.optimization_barrier((qkv, send, node))
    half = groups // 2
    reach = half * NODE_DEV
    core = lax.rem(lax.axis_index("band"), 2)
    kv = qkv[:, :, LANES:]
    on_chip = flipped(lax.dynamic_slice_in_dim(kv, (1 - core) * half, half, 0), "band", 0)
    off_chip = next_chip(lax.dynamic_slice_in_dim(kv, core * half, half, 0))
    extra = swap(send)
    acc, top, queries = near(qkv, win_offsets, reach)
    parts, attended = far(queries, acc, top, on_chip, off_chip, win_offsets, mix)
    grad, give = grads(attended, extra)
    grad = (grad + flipped(give, "band", 0)).astype(BF)
    for bit in (1, 2, 3):
        grad = (grad.astype(F32) + flipped(grad, "band", bit).astype(F32)).astype(BF)
    parts = swap(spread(grad, across(grad), parts))
    table, padded = make_table(parts, node)
    half_grad = gradient_half(parts, w_out)
    grad_dec = add(half_grad, flipped(half_grad, "band", 0), channels)
    grad_dec, mid_rows = lax.optimization_barrier((grad_dec, to_partner(table)))
    prediction = decode(two_over(padded, 1), mid_rows, table, dec_row, grid_in)
    return (prediction, grad_dec.T)


def solution(mesh):
    placed = (
        P(None, BOTH),
        P(BOTH),
        P(BOTH),
        P(None, "band"),
        P(),
        P(),
        P(),
        P(),
        P(),
        P(),
        P(None, BOTH),
    )
    return jax.shard_map(
        shards,
        mesh=mesh,
        in_specs=placed,
        out_specs=(P(None, BOTH), P()),
        check_vma=False,
    )
```

```python
import functools

import jax
import jax.numpy as jnp
from jax import lax
from jax.experimental import pallas as pl
from jax.experimental.pallas import tpu as pltpu
from jax.sharding import PartitionSpec as P

HDIM = 64
NODE_DEV = 160
BOTH = ("band", "head")
LANES = 128
QB = 256
KC = 128
ROWS = 112
EXTRA = 16
BF = jnp.bfloat16
F32 = jnp.float32
LOG2E = 1.4426950408889634
NEG = -1e30
HBM = pl.BlockSpec(memory_space=pltpu.HBM)
VMEM = pl.BlockSpec(memory_space=pltpu.VMEM)


def params(mib=24):
    return pltpu.CompilerParams(vmem_limit_bytes=mib * 1024 * 1024)


def dot(a, b, ca, cb):
    return lax.dot_general(a, b, (((ca,), (cb,)), ((), ())), preferred_element_type=F32)


def shape(dims, dtype):
    return jax.ShapeDtypeStruct(dims, dtype)


def in_hbm(a):
    return pltpu.HBM(a.shape, a.dtype)


def pinned(*arrays):
    return tuple(pltpu.with_memory_space_constraint(a, pltpu.HBM) for a in arrays)


def started(copies):
    for copy in copies:
        copy.start()
    return copies


def chunk_bases():
    index = lax.axis_index("band") * lax.axis_size("head") + lax.axis_index("head")
    side = 1 - 2 * lax.rem(index, 2)
    return (index - side) * NODE_DEV, index * NODE_DEV, (index + side) * NODE_DEV


def fill_pick(pick_ref, target):
    nodes, points = NODE_DEV, pick_ref.shape[1]
    node_id = lax.broadcasted_iota(jnp.int32, (nodes, points), 0)
    for at, base in enumerate(chunk_bases()):
        pick_ref[at * nodes : (at + 1) * nodes, :] = jnp.where(node_id == target - base, 1.0, 0.0).astype(BF)


def encode_kernel(grid_hbm, enc_hbm, w_hbm, b_hbm, far_ref, mid_ref, own_ref,
                  grid_ref, enc_ref, w_ref, b_ref, w_half, pick_ref, sem):
    model = w_ref.shape[1]
    nodes = NODE_DEV
    copies = started(
        [
            pltpu.make_async_copy(source, target, sem.at[at])
            for at, (source, target) in enumerate(
                [(grid_hbm, grid_ref), (enc_hbm, enc_ref), (w_hbm, w_ref), (b_hbm, b_ref)]
            )
        ]
    )
    copies[1].wait()
    fill_pick(pick_ref, enc_ref[...])
    copies[2].wait()
    w_half[...] = (w_ref[...].astype(F32) * 0.5).astype(BF)
    copies[0].wait()
    copies[3].wait()
    width = 512
    mid_ref[nodes:, :] = jnp.zeros((EXTRA, model), BF)
    for at in range(0, model, width):
        half = dot(grid_ref[...], w_half[:, at : at + width], 0, 0) + b_ref[:, at : at + width] * 0.5
        message = (half + half * jnp.tanh(half)).astype(BF)
        spread = dot(pick_ref[...], message, 1, 0)
        far_ref[:, at : at + width] = spread[:nodes].astype(BF)
        mid_ref[:nodes, at : at + width] = spread[nodes : 2 * nodes].astype(BF)
        own_ref[:, at : at + width] = spread[2 * nodes :]


def encode(grid_in, enc_row, w_in, b_row):
    points = grid_in.shape[1]
    model = w_in.shape[1]
    operands = (grid_in, enc_row, w_in, b_row)
    return pl.pallas_call(
        encode_kernel,
        in_specs=[HBM] * 4,
        out_specs=(VMEM,) * 3,
        out_shape=(shape((NODE_DEV, model), BF), shape((NODE_DEV + EXTRA, model), BF), shape((NODE_DEV, model), F32)),
        scratch_shapes=[pltpu.VMEM(a.shape, a.dtype) for a in operands]
        + [
            pltpu.VMEM(w_in.shape, BF),
            pltpu.VMEM((3 * NODE_DEV, points), BF),
            pltpu.SemaphoreType.DMA((4,)),
        ],
        compiler_params=params(),
        name="encode",
    )(*pinned(*operands))


def prepare_kernel(w_hbm, out_hbm, dec_hbm, cot_hbm, target_hbm, after_ref,
                   w_ref, pad_ref, mix_hbm, far_ref, mid_ref, own_ref,
                   mix_ref, out_rows, dec_rows, cot_ref, target_ref, cot_pad, pick_ref, sem):
    channels = dec_rows.shape[0]
    nodes = NODE_DEV
    at = pl.multiple_of(lax.axis_index("head") * LANES, LANES)
    copies = started(
        [
            pltpu.make_async_copy(source, target, sem.at[number])
            for number, (source, target) in enumerate(
                [
                    (target_hbm, target_ref),
                    (cot_hbm, cot_ref),
                    (dec_hbm, dec_rows),
                    (out_hbm.at[pl.ds(at, LANES), :], out_rows),
                    (w_hbm, w_ref),
                ]
            )
        ]
    )
    copies[0].wait()
    fill_pick(pick_ref, target_ref[...])
    copies[1].wait()
    cot_pad[...] = jnp.zeros_like(cot_pad)
    cot_pad[:channels, :] = cot_ref[...]
    spread = dot(pick_ref[...], cot_pad[...], 1, 1)
    far_ref[...] = spread[:nodes].astype(BF)
    mid_ref[...] = spread[nodes : 2 * nodes].astype(BF)
    own_ref[...] = spread[2 * nodes :]
    copies[2].wait()
    pad_ref[...] = jnp.zeros_like(pad_ref)
    pad_ref[:channels, :] = dec_rows[...]
    copies[3].wait()
    mix_ref[...] = dot(out_rows[...], pad_ref[...], 1, 1).astype(BF)
    copy = pltpu.make_async_copy(mix_ref, mix_hbm, sem.at[len(copies)])
    copy.start()
    copy.wait()
    copies[4].wait()


def prepare(w_qkv, w_out, dec_cols, cotangent, dec_row, after):
    model = w_qkv.shape[0]
    points = cotangent.shape[1]
    part = (NODE_DEV, LANES)
    return pl.pallas_call(
        prepare_kernel,
        in_specs=[HBM] * 5 + [pl.BlockSpec(memory_space=pl.ANY)],
        out_specs=(VMEM, VMEM, HBM, VMEM, VMEM, VMEM),
        out_shape=(
            shape(w_qkv.shape, BF),
            shape((LANES, model), BF),
            in_hbm(shape((LANES, LANES), BF)),
            shape(part, BF),
            shape(part, BF),
            shape(part, F32),
        ),
        scratch_shapes=[
            pltpu.VMEM((LANES, LANES), BF),
            pltpu.VMEM((LANES, model), BF),
            pltpu.VMEM(dec_cols.shape, BF),
            pltpu.VMEM(cotangent.shape, BF),
            pltpu.VMEM(dec_row.shape, jnp.int32),
            pltpu.VMEM((LANES, points), BF),
            pltpu.VMEM((3 * NODE_DEV, points), BF),
            pltpu.SemaphoreType.DMA((6,)),
        ],
        compiler_params=params(),
        cost_estimate=pl.CostEstimate(flops=500_000_000, bytes_accessed=2 * w_qkv.size, transcendentals=0),
        name="prepare",
    )(*pinned(w_qkv, w_out, dec_cols, cotangent, dec_row), after)


def project_kernel(own_ref, mid_ref, far_ref, gain_ref, w_ref, packed_hbm, enc_ref, packed, sem):
    model = gain_ref.shape[1]
    enc = own_ref[...] + mid_ref[:NODE_DEV].astype(F32) + far_ref[...].astype(F32)
    enc_ref[...] = enc
    centred = enc - jnp.mean(enc, axis=1, keepdims=True)
    spread_sq = jnp.mean(centred * centred, axis=1, keepdims=True)
    normed = (centred * lax.rsqrt(spread_sq + 1e-05) * gain_ref[...]).astype(BF)
    scale = HDIM ** (-0.5) * LOG2E
    copies = []
    for pair in range(model // (2 * LANES)):
        for part in range(3):
            at = part * model + pair * 2 * LANES
            cols = dot(normed, w_ref[:, at : at + 2 * LANES], 1, 0)
            if part == 0:
                cols = cols * scale
            cols = cols.astype(BF)
            for half in range(2):
                packed[2 * pair + half, :, part * LANES : (part + 1) * LANES] = cols[:, half * LANES : (half + 1) * LANES]
        rows = pl.ds(2 * pair, 2)
        copies += started([pltpu.make_async_copy(packed.at[rows], packed_hbm.at[rows], sem.at[pair])])
    for copy in copies:
        copy.wait()


def project(own, mid, far, gain_row, w_qkv):
    model = w_qkv.shape[0]
    groups = model // LANES
    return pl.pallas_call(
        project_kernel,
        in_specs=[VMEM] * 5,
        out_specs=(HBM, VMEM),
        out_shape=(
            in_hbm(shape((groups, NODE_DEV, 3 * LANES), BF)),
            shape((NODE_DEV, model), F32),
        ),
        scratch_shapes=[
            pltpu.VMEM((groups, NODE_DEV, 3 * LANES), BF),
            pltpu.SemaphoreType.DMA((groups // 2,)),
        ],
        compiler_params=params(),
        name="project",
    )(own, mid, far, gain_row, w_qkv)


def side_kernel(enc_ref, own_ref, mid_ref, far_ref, dec_ref, send_hbm, node_ref, send, sem):
    groups = send.shape[0]
    enc = enc_ref[...]
    summed = (own_ref[...] + mid_ref[...].astype(F32) + far_ref[...].astype(F32)).astype(BF)
    high = enc.astype(BF)
    low = (enc - high.astype(F32)).astype(BF)
    node_ref[...] = dot(high, dec_ref[...], 1, 1)
    grad = (dot(summed, high, 0, 0) + dot(summed, low, 0, 0)).astype(BF)
    for group in range(groups):
        send[group, :NODE_DEV, :] = summed
        send[group, NODE_DEV:, :] = grad[:ROWS, group * LANES : (group + 1) * LANES]
    copy = pltpu.make_async_copy(send, send_hbm, sem)
    copy.start()
    copy.wait()


def side(enc, own, mid, far, dec_pad):
    groups = enc.shape[1] // LANES
    send_shape = (groups, NODE_DEV + ROWS, LANES)
    return pl.pallas_call(
        side_kernel,
        in_specs=[VMEM] * 5,
        out_specs=(HBM, VMEM),
        out_shape=(in_hbm(shape(send_shape, BF)), shape((NODE_DEV, LANES), F32)),
        scratch_shapes=[pltpu.VMEM(send_shape, BF), pltpu.SemaphoreType.DMA],
        compiler_params=params(),
        name="side",
    )(enc, own, mid, far, dec_pad)


def limits(win, reach, start, first_node, node_total):
    column = lax.broadcasted_iota(jnp.int32, (1, QB), 1) + reach
    bottom = jnp.maximum(column - win[0:1], reach - start - first_node)
    top = jnp.minimum(column + win[1:2], reach - start - first_node + node_total - 1)
    return jnp.concatenate([bottom, bottom], axis=1), jnp.concatenate([top, top], axis=1)


def masked(scores, at, reach, bottom, top):
    key = lax.broadcasted_iota(jnp.int32, scores.shape, 0) + at
    if at + KC - 1 <= reach:
        keep = key >= bottom
    elif at >= reach + QB - 1:
        keep = key <= top
    else:
        keep = (key >= bottom) & (key <= top)
    return jnp.where(keep, scores, NEG)


def fold(scores):
    return jnp.max(scores.reshape(KC // 8, 8, 2 * QB), axis=0)


def near_kernel(reach, qkv_ref, win_hbm, acc_hbm, top_hbm, q_hbm,
                win_ref, acc_ref, top_ref, q_ref, k_ref, v_ref, vt_ref, score_ref, prob_ref, sem):
    groups = qkv_ref.shape[0]
    win_copy = pltpu.make_async_copy(win_hbm, win_ref, sem.at[0])
    win_copy.start()
    band_rows = groups * NODE_DEV
    first_node = lax.axis_index("band") * band_rows
    node_total = lax.axis_size("band") * band_rows
    lane = lax.broadcasted_iota(jnp.int32, (NODE_DEV, LANES), 1)
    zero = jnp.zeros((NODE_DEV, LANES), BF)
    for group in range(groups):
        rows = pl.ds((group ^ 1) * NODE_DEV, NODE_DEV)
        queries = qkv_ref[group, :, :LANES]
        q_ref[0, rows, :] = jnp.where(lane < HDIM, queries, zero)
        q_ref[1, rows, :] = jnp.where(lane >= HDIM, queries, zero)
        k_ref[rows, :] = qkv_ref[group, :, LANES : 2 * LANES]
        v_ref[rows, :] = qkv_ref[group, :, 2 * LANES :].astype(F32)
    vt = v_ref[...].T.astype(BF)
    for head in range(2):
        vt_ref[head, :HDIM, :] = vt[head * HDIM : (head + 1) * HDIM]
        vt_ref[head, HDIM:, :] = jnp.ones((16, band_rows), BF)
    copies = started([pltpu.make_async_copy(q_ref, q_hbm, sem.at[1])])
    win_copy.wait()
    for block in range(band_rows // QB):
        start = block * QB
        both = jnp.concatenate([q_ref[0, start : start + QB, :], q_ref[1, start : start + QB, :]], axis=0)
        bottom, top = limits(win_ref[:, start : start + QB], reach, start, first_node, node_total)
        first = max(0, reach - start)
        last = min(QB + 2 * reach, band_rows + reach - start)
        largest = jnp.full((8, 2 * QB), NEG, F32)
        for at in range(first, last, KC):
            key = start + at - reach
            scores = masked(dot(k_ref[key : key + KC, :], both, 1, 1), at, reach, bottom, top)
            score_ref[at - first : at - first + KC, :] = scores
            largest = jnp.maximum(largest, fold(scores))
        largest = jnp.max(largest, axis=0, keepdims=True)
        top_ref[block] = largest
        for at in range(0, last - first, KC):
            prob_ref[at : at + KC, :] = jnp.exp2(score_ref[at : at + KC, :] - largest).astype(BF)
        key = start + first - reach
        for head in range(2):
            acc_ref[block, head] = dot(
                vt_ref[head, :, key : key + last - first],
                prob_ref[: last - first, head * QB : (head + 1) * QB],
                1,
                0,
            )
        copies += started([pltpu.make_async_copy(acc_ref.at[block], acc_hbm.at[block], sem.at[3 + block])])
    copies += started([pltpu.make_async_copy(top_ref, top_hbm, sem.at[2])])
    for copy in copies:
        copy.wait()


def near(qkv, win, reach):
    groups = qkv.shape[0]
    band_rows = groups * NODE_DEV
    blocks = band_rows // QB
    keys = min(QB + 2 * reach, band_rows)
    outs = (
        shape((blocks, 2, HDIM + 16, QB), F32),
        shape((blocks, 1, 2 * QB), F32),
        shape((2, band_rows, LANES), BF),
    )
    return pl.pallas_call(
        functools.partial(near_kernel, reach),
        in_specs=[VMEM, HBM],
        out_specs=(HBM,) * 3,
        out_shape=tuple(in_hbm(a) for a in outs),
        scratch_shapes=[
            pltpu.VMEM(win.shape, win.dtype),
            *[pltpu.VMEM(a.shape, a.dtype) for a in outs],
            pltpu.VMEM((band_rows, LANES), BF),
            pltpu.VMEM((band_rows, LANES), F32),
            pltpu.VMEM((2, HDIM + 16, band_rows), BF),
            pltpu.VMEM((keys, 2 * QB), F32),
            pltpu.VMEM((keys, 2 * QB), BF),
            pltpu.SemaphoreType.DMA((3 + blocks,)),
        ],
        compiler_params=params(),
        cost_estimate=pl.CostEstimate(flops=6_000_000_000, bytes_accessed=4_000_000, transcendentals=3_000_000),
        name="near",
    )(qkv, *pinned(win))


def far_kernel(reach, q_hbm, acc_hbm, top_hbm, win_hbm, mix_hbm, off_hbm, chip_ref, node_hbm, out_ref,
               q_ref, acc_ref, top_ref, win_ref, mix_ref, off_ref,
               k_ref, v_ref, vt_ref, score_ref, prob_ref, node_ref, sem):
    band_rows = q_ref.shape[1]
    groups = band_rows // NODE_DEV
    first_node = lax.axis_index("band") * band_rows
    node_total = lax.axis_size("band") * band_rows
    copies = started(
        [
            pltpu.make_async_copy(source, target, sem.at[at])
            for at, (source, target) in enumerate(
                [(off_hbm, off_ref), (q_hbm, q_ref), (acc_hbm, acc_ref), (top_hbm, top_ref), (win_hbm, win_ref), (mix_hbm, mix_ref)]
            )
        ]
    )
    core = lax.rem(lax.axis_index("band"), 2)
    for base, half in (((1 - core) * reach, chip_ref), (core * reach, off_ref)):
        if half is off_ref:
            copies[0].wait()
        for group in range(groups // 2):
            rows = pl.ds(pl.multiple_of(base + (group ^ 1) * NODE_DEV, NODE_DEV), NODE_DEV)
            k_ref[rows, :] = half[group, :, :LANES]
            v_ref[rows, :] = half[group, :, LANES:].astype(F32)
    vt = v_ref[...].T.astype(BF)
    for head in range(2):
        vt_ref[head, :HDIM, :] = vt[head * HDIM : (head + 1) * HDIM]
        vt_ref[head, HDIM:, :] = jnp.ones((16, 2 * reach), BF)
    for copy in copies[1:]:
        copy.wait()
    for block in range(band_rows // QB):
        start = block * QB
        both = jnp.concatenate([q_ref[0, start : start + QB, :], q_ref[1, start : start + QB, :]], axis=0)
        bottom, top = limits(win_ref[:, start : start + QB], reach, start, first_node, node_total)
        low_to = max(0, reach - start)
        high_from = min(QB + 2 * reach, band_rows + reach - start)
        pieces = [(at, start + at) for at in range(0, low_to, KC)]
        pieces += [(at, start + at - band_rows) for at in range(high_from, QB + 2 * reach, KC)]
        before = top_ref[block]
        largest = jnp.full((8, 2 * QB), NEG, F32)
        for row, (at, key) in enumerate(pieces):
            scores = masked(dot(k_ref[key : key + KC, :], both, 1, 1), at, reach, bottom, top)
            score_ref[row * KC : (row + 1) * KC, :] = scores
            largest = jnp.maximum(largest, fold(scores))
        largest = jnp.maximum(jnp.max(largest, axis=0, keepdims=True), before)
        decay = jnp.exp2(before - largest)
        for row in range(len(pieces)):
            prob_ref[row * KC : (row + 1) * KC, :] = jnp.exp2(score_ref[row * KC : (row + 1) * KC, :] - largest).astype(BF)
        low_rows, high_rows = low_to, QB + 2 * reach - high_from
        for head in range(2):
            cols = slice(head * QB, (head + 1) * QB)
            mixed = acc_ref[block, head] * decay[:, cols]
            if low_rows:
                mixed += dot(vt_ref[head, :, start:reach], prob_ref[:low_rows, cols], 1, 0)
            if high_rows:
                at = reach
                mixed += dot(vt_ref[head, :, at : at + high_rows], prob_ref[low_rows : low_rows + high_rows, cols], 1, 0)
            out_ref[head * HDIM : (head + 1) * HDIM, start : start + QB] = (
                mixed[:HDIM] / mixed[HDIM : HDIM + 1]
            ).astype(BF)
    node_ref[...] = dot(mix_ref[...], out_ref[...], 0, 0).T.astype(BF)
    rows = pl.ds(0, NODE_DEV)
    sends = started(
        [
            pltpu.make_async_copy(
                node_ref.at[pl.ds((group ^ 1) * NODE_DEV, NODE_DEV), :],
                node_hbm.at[group, rows, :],
                sem.at[len(copies) + group],
            )
            for group in range(groups)
        ]
    )
    for copy in sends:
        copy.wait()


def far(queries, acc, top, on_chip, off_chip, win, mix):
    band_rows = queries.shape[1]
    groups = band_rows // NODE_DEV
    reach = on_chip.shape[0] * NODE_DEV
    held = (queries, acc, top, win, mix, off_chip)
    return pl.pallas_call(
        functools.partial(far_kernel, reach),
        in_specs=[HBM] * 6 + [VMEM],
        out_specs=(HBM, VMEM),
        out_shape=(
            in_hbm(shape((groups, NODE_DEV + ROWS, LANES), BF)),
            shape((LANES, band_rows), BF),
        ),
        scratch_shapes=[pltpu.VMEM(a.shape, a.dtype) for a in held]
        + [
            pltpu.VMEM((2 * reach, LANES), BF),
            pltpu.VMEM((2 * reach, LANES), F32),
            pltpu.VMEM((2, HDIM + 16, 2 * reach), BF),
            pltpu.VMEM((reach, 2 * QB), F32),
            pltpu.VMEM((reach, 2 * QB), BF),
            pltpu.VMEM((band_rows, LANES), BF),
            pltpu.SemaphoreType.DMA((len(held) + groups,)),
        ],
        compiler_params=params(),
        cost_estimate=pl.CostEstimate(flops=6_000_000_000, bytes_accessed=2_000_000, transcendentals=1_000_000),
        name="far",
    )(*pinned(*held), on_chip)


def grads_kernel(out_ref, extra_ref, keep_ref, give_ref):
    groups = extra_ref.shape[0]
    grad = jnp.zeros((LANES, LANES), F32)
    total = jnp.zeros((ROWS, LANES), F32)
    for group in range(groups):
        at = (group ^ 1) * NODE_DEV
        grad += dot(extra_ref[group, :NODE_DEV, :], out_ref[:, at : at + NODE_DEV], 0, 1)
        total += extra_ref[group, NODE_DEV:, :].astype(F32)
    first = lax.rem(lax.axis_index("band"), 2) == 0
    keep_ref[...] = jnp.where(first, grad[:ROWS], total)
    give_ref[...] = jnp.where(first, total, grad[:ROWS])


def grads(out, extra):
    half = shape((ROWS, LANES), F32)
    return pl.pallas_call(
        grads_kernel,
        in_specs=[VMEM] * 2,
        out_specs=(VMEM,) * 2,
        out_shape=(half, half),
        compiler_params=params(),
        name="grads",
    )(out, extra)


def decode_kernel(mid_ref, far_ref, own_ref, dec_ref, grid_ref, pred_ref):
    channels, points = grid_ref.shape
    nodes = NODE_DEV
    rows = 4 * LANES
    table = jnp.concatenate(
        [
            far_ref[:NODE_DEV].astype(F32),
            mid_ref[...].astype(F32),
            own_ref[...].astype(F32),
            jnp.zeros((rows - 3 * nodes, LANES), F32),
        ],
        axis=0,
    ).T.astype(BF)
    width = 512
    bases = chunk_bases()
    node_id = lax.broadcasted_iota(jnp.int32, (nodes, width), 0)
    for at in range(0, points, width):
        target = dec_ref[:, at : at + width]
        pick = [jnp.where(node_id == target - base, 1.0, 0.0) for base in bases]
        pick = jnp.concatenate(pick + [jnp.zeros((rows - 3 * nodes, width), F32)], axis=0).astype(BF)
        decoded = dot(table, pick, 1, 0)
        pred_ref[:, at : at + width] = (
            grid_ref[:, at : at + width].astype(F32) + decoded[:channels]
        ).astype(BF)


def decode(far_rows, mid_rows, own_rows, dec_row, grid_in):
    return pl.pallas_call(
        decode_kernel,
        in_specs=[VMEM] * 5,
        out_specs=VMEM,
        out_shape=shape(grid_in.shape, BF),
        compiler_params=params(),
        name="decode",
    )(mid_rows, far_rows, own_rows, dec_row, grid_in)


def spread_kernel(grad_ref, more_ref, parts_hbm, filled_hbm, sum_ref, sem):
    sum_ref[...] = (grad_ref[...].astype(F32) + more_ref[...].astype(F32)).astype(BF)
    rows = pl.ds(NODE_DEV, sum_ref.shape[0])
    copies = [
        pltpu.make_async_copy(sum_ref, filled_hbm.at[at, rows, :], sem.at[at]) for at in range(filled_hbm.shape[0])
    ]
    for copy in started(copies):
        copy.wait()


def spread(grad, more, parts):
    return pl.pallas_call(
        spread_kernel,
        in_specs=[VMEM, VMEM, HBM],
        out_specs=HBM,
        out_shape=in_hbm(parts),
        input_output_aliases={2: 0},
        scratch_shapes=[pltpu.VMEM(grad.shape, BF), pltpu.SemaphoreType.DMA((parts.shape[0],))],
        compiler_params=params(),
        name="spread",
    )(grad, more, *pinned(parts))


def finish_kernel(parts_ref, node_ref, w_out_ref, table_ref, padded_ref, half_ref):
    groups = parts_ref.shape[0]
    total = node_ref[...]
    for group in range(groups):
        total += parts_ref[group, :NODE_DEV, :].astype(F32)
    table_ref[...] = total.astype(BF)
    padded_ref[:NODE_DEV, :] = total.astype(BF)
    padded_ref[NODE_DEV:, :] = jnp.zeros((EXTRA, LANES), BF)
    first = lax.rem(lax.axis_index("band"), 2) == 0

    @pl.when(first)
    def _():
        mixed = jnp.zeros(half_ref.shape, F32)
        for group in range(groups):
            rows = w_out_ref[group * LANES : (group + 1) * LANES, :]
            mixed += dot(parts_ref[group, NODE_DEV:, :], rows, 1, 0)
        half_ref[...] = mixed

    @pl.when(jnp.logical_not(first))
    def _():
        for group in range(groups):
            half_ref[:, group * LANES : (group + 1) * LANES] = parts_ref[group, NODE_DEV:, :].astype(F32)


def finish(parts, node, w_out):
    return pl.pallas_call(
        finish_kernel,
        in_specs=[VMEM] * 3,
        out_specs=(VMEM,) * 3,
        out_shape=(
            shape(node.shape, BF),
            shape((NODE_DEV + EXTRA, LANES), BF),
            shape((ROWS, w_out.shape[1]), F32),
        ),
        compiler_params=params(),
        name="finish",
    )(parts, node, w_out)


def add_kernel(mine_ref, other_ref, out_ref):
    channels = out_ref.shape[0]
    out_ref[...] = mine_ref[:channels] + other_ref[:channels]


def add(mine, other, channels):
    return pl.pallas_call(
        add_kernel,
        in_specs=[VMEM] * 2,
        out_specs=VMEM,
        out_shape=shape((channels, mine.shape[1]), F32),
        compiler_params=params(),
        name="add",
    )(mine, other)


def total_devices():
    return lax.axis_size("band") * lax.axis_size("head")


def to_partner(block):
    return lax.ppermute(block, BOTH, [(i, i ^ 1) for i in range(total_devices())])


def two_over(block, sign):
    count = total_devices()
    pairs = [(i, i + sign * (2 - 4 * (i % 2))) for i in range(count)]
    return lax.ppermute(block, BOTH, [(i, j) for i, j in pairs if 0 <= j < count])


def next_chip(block):
    count = lax.axis_size("band")
    pairs = [(i, i - 1 + 2 * (i % 2)) for i in range(count)]
    return lax.ppermute(block, "band", [(i, j) for i, j in pairs if 0 <= j < count])


def flipped(block, axis, bit):
    return lax.ppermute(block, axis, [(i, i ^ (1 << bit)) for i in range(lax.axis_size(axis))])


def across(block):
    planes = lax.axis_size("band") // 4
    other = [(z + 6) % planes if z % 4 < 2 else (z + 2) % planes for z in range(planes)]
    return lax.ppermute(block, "band", [(i, other[i // 4] * 4 + i % 4) for i in range(planes * 4)])


def swap(block):
    return lax.all_to_all(block, "head", split_axis=0, concat_axis=0, tiled=True)


def shards(
    grid_in, enc_node, dec_node, win_offsets, w_in, b_in, w_qkv, w_out, norm_gain, w_dec, cotangent
):
    channels = grid_in.shape[0]
    groups = lax.axis_size("head")
    dec_row = dec_node[None]
    far_part, mid_part, own = encode(grid_in, enc_node[None], w_in, b_in[None])
    weights, dec_pad, mix, far_sum, mid_sum, own_sum = prepare(
        w_qkv, w_out, w_dec.T, cotangent, dec_row, far_part
    )
    mid_in = to_partner(mid_part)
    far_in = two_over(far_part, -1)
    mid_sum = to_partner(mid_sum)
    far_sum = two_over(far_sum, -1)
    packed, enc = project(own, mid_in, far_in, norm_gain[None], weights)
    packed, mid_sum = lax.optimization_barrier((packed, mid_sum))
    qkv = swap(packed)
    send, node = side(enc, own_sum, mid_sum, far_sum, dec_pad)
    qkv, send, node = lax.optimization_barrier((qkv, send, node))
    half = groups // 2
    reach = half * NODE_DEV
    core = lax.rem(lax.axis_index("band"), 2)
    kv = qkv[:, :, LANES:]
    on_chip = flipped(lax.dynamic_slice_in_dim(kv, (1 - core) * half, half, 0), "band", 0)
    off_chip = next_chip(lax.dynamic_slice_in_dim(kv, core * half, half, 0))
    extra = swap(send)
    acc, top, queries = near(qkv, win_offsets, reach)
    parts, attended = far(queries, acc, top, on_chip, off_chip, win_offsets, mix)
    grad, give = grads(attended, extra)
    grad = (grad + flipped(give, "band", 0)).astype(BF)
    for bit in (1, 2, 3):
        grad = (grad.astype(F32) + flipped(grad, "band", bit).astype(F32)).astype(BF)
    parts = swap(spread(grad, across(grad), parts))
    table, padded, half_grad = finish(parts, node, w_out)
    grad_dec = add(half_grad, flipped(half_grad, "band", 0), channels)
    grad_dec, mid_rows = lax.optimization_barrier((grad_dec, to_partner(table)))
    prediction = decode(two_over(padded, 1), mid_rows, table, dec_row, grid_in)
    return (prediction, grad_dec.T)


def solution(mesh):
    placed = (
        P(None, BOTH),
        P(BOTH),
        P(BOTH),
        P(None, "band"),
        P(),
        P(),
        P(),
        P(),
        P(),
        P(),
        P(None, BOTH),
    )
    return jax.shard_map(
        shards,
        mesh=mesh,
        in_specs=placed,
        out_specs=(P(None, BOTH), P()),
        check_vma=False,
    )
```
